32 devices in a mesh: groups: 2 (over y), filt: 4 (over z), sp: 2 (over x), in: 2 (over core).
Axes of the slice: x: 2, y: 2, z: 4, core: 2. Of those that a mesh axis runs over, the one named last changes fastest.
Arguments:
- image: bfloat16 [16, 256, 1024], P(('groups', 'sp', 'filt'), None, 'in'), parts along dimension 0, may hold values from -6 to 6
- weight: bfloat16 [3, 3, 1024, 1024], P(None, None, 'filt'), may hold values from -0.0625 to 0.0625
- bias: float32 [1024], P('filt'), may hold values from -3 to 3
- cotangent: bfloat16 [16, 1024, 256], P(('groups', 'sp'), 'filt'), parts along dimension 0, may hold values from -0.029907227 to 0.029907227
Outputs:
- output: bfloat16 [16, 1024, 256], P(('groups', 'sp', 'filt'), None, 'in'), parts along dimension 0
- grad_weight: float32 [6, 3, 1024, 1024], P('groups', None, 'filt', 'in'), parts along dimension 0
- grad_bias: float32 [2048], P(('groups', 'filt')), parts along dimension 0
The draws below stay inside these ranges and needn't reach their ends.
There are 2 independent parts, one for each index of `groups`. The reference program is written for one: setup_inputs(seed, part) draws one part's arguments, and reference() takes and returns one part's arrays. A program takes and returns all parts, laid end to end along the dimension named above; an argument that names none is the same for every part. Nothing has to cross between parts.
All inputs are finite; a program needn't handle non-finite values.
Results may differ from the reference program's by a relative error of at most 0.0055.
Values may be sent and summed in bfloat16 or wider, within the bound.
No kernel may reach another device: no remote copies, remote signals or barrier semaphores. Data moves between devices by JAX's collectives and lax.ppermute only.
A program may use at most 64 MiB of HBM per device.

```python
import jax
import jax.numpy as jnp

CH = 1024
ROWS_DEV = 1
COLS = 256
ROWS = 8
N_FILT = 4
N_SP = 2


def shard_levels(own_key, dims, cuts, least, largest):
    def one(axis_at, shards_of):
        draws = jax.random.uniform(jax.random.fold_in(jax.random.fold_in(own_key, 6), axis_at), (shards_of,), jnp.float32, least / len(cuts), largest / len(cuts))
        return jnp.repeat(jnp.exp(draws), dims[axis_at] // shards_of).reshape((-1,) + (1,) * (len(dims) - axis_at - 1))

    level = one(*cuts[0])
    for cut in cuts[1:]:
        level = level * one(*cut)
    return level


def noise(key, dims, deviation, most, cuts=(), dtype=jnp.bfloat16):
    array = deviation * jax.random.normal(key, dims, jnp.float32)
    if cuts:
        array = array * shard_levels(key, dims, cuts, -0.22, 0.18)
    return jnp.clip(array, -most, most).astype(dtype)


def setup_inputs(seed: int = 0, part: int = 0) -> dict:
    key_of = jax.random.split(jax.random.key(seed), 5)
    part_keys = jax.random.split(jax.random.fold_in(key_of[4], part), 5)
    image = noise(part_keys[0], (ROWS, COLS, CH), 1.0, 6.0, ((0, 8), (2, 2)))
    weight = noise(key_of[1], (3, 3, CH, CH), (9 * CH) ** -0.5, 0.0625, ((2, 4),))
    bias = noise(key_of[2], (CH,), 0.5, 3.0, ((0, 4),), jnp.float32)
    cotangent = noise(part_keys[3], (ROWS, CH, COLS), 0.005, 0.029907227, ((0, 2), (1, 4)))
    return {"image": image, "weight": weight, "bias": bias, "cotangent": cotangent}


def reference(image, weight, bias, cotangent):
    row_count = ROWS_DEV * N_FILT * N_SP
    col_count = COLS
    padded = jnp.pad(image, ((1, 1), (1, 1), (0, 0)))
    running = jnp.zeros((row_count * col_count, CH), jnp.float32)
    for row_tap in range(3):
        for col_tap in range(3):
            window = padded[row_tap:row_tap + row_count, col_tap:col_tap + col_count].reshape(-1, CH)
            running = running + jnp.dot(window, weight[row_tap, col_tap].T, preferred_element_type=jnp.float32)
    shifted = running + bias[None, :]
    sigmoid_v = jax.nn.sigmoid(shifted)
    output = (shifted * sigmoid_v).astype(jnp.bfloat16).reshape(row_count, col_count, CH).transpose(0, 2, 1)
    slope = sigmoid_v * (1.0 + shifted * (1.0 - sigmoid_v))
    cot_rows = cotangent.transpose(0, 2, 1).reshape(-1, CH)
    grad_out = (cot_rows.astype(jnp.float32) * slope).astype(jnp.bfloat16)
    pieces = []
    for row_tap in range(3):
        for col_tap in range(3):
            window = padded[row_tap:row_tap + row_count, col_tap:col_tap + col_count].reshape(-1, CH)
            pieces.append(jnp.dot(grad_out.T, window, preferred_element_type=jnp.float32))
    grad_weight = jnp.stack(pieces).reshape(3, 3, CH, CH)
    grad_bias = jnp.sum(grad_out.astype(jnp.float32), axis=0)
    return (output, grad_weight, grad_bias)
```

```python
import functools

import jax
import jax.numpy as jnp
from jax import lax
from jax.experimental import pallas as pl
from jax.experimental.pallas import tpu as pltpu
from jax.sharding import PartitionSpec as P

VMEM_LIMIT = 56 * 1024 * 1024


def shifted_ring(axis, shift):
    size = lax.axis_size(axis)
    return [(i, (i + shift) % size) for i in range(size)]


def gather_blocks(image):
    n_filt, n_sp = lax.axis_size("filt"), lax.axis_size("sp")
    blocks = [[None] * n_filt for _ in range(n_sp)]
    blocks[0][0] = image
    for k in range(n_filt):
        if k:
            blocks[0][k] = lax.ppermute(blocks[0][k - 1], "filt", shifted_ring("filt", 1))
        for j in range(1, n_sp):
            if k and k == n_filt - 1:
                blocks[j][k] = lax.ppermute(blocks[j][0], "filt", shifted_ring("filt", -1))
            else:
                blocks[j][k] = lax.ppermute(blocks[j - 1][k], "sp", shifted_ring("sp", 1))
    return blocks


def move_columns(values, by):
    size = values.shape[1]
    column = lax.broadcasted_iota(jnp.int32, values.shape, 1)
    edge = 0 if by == 1 else size - 1
    return jnp.where(column == edge, 0.0, pltpu.roll(values, by % size, 1))


def forward_kernel(n_blocks, place, weight, *refs):
    blocks, (out, taps, panel, weight_sem, block_sem) = refs[:n_blocks], refs[n_blocks:]
    side_rows = pl.num_programs(0)
    step = pl.program_id(0)
    side, half = place[0], place[1]
    depth, rows_dev = blocks[0].shape[2], blocks[0].shape[0]
    own = weight.shape[2]

    def weight_copies():
        for a in range(3):
            for b in range(3):
                yield pltpu.make_async_copy(
                    weight.at[a, b, :, pl.ds(pl.multiple_of(half * depth, depth), depth)],
                    taps.at[pl.ds(b * own, own), pl.ds(a * depth, depth)],
                    weight_sem.at[a * 3 + b],
                )

    def block_copies():
        for index, block in enumerate(blocks):
            for i in range(rows_dev):
                slot = place[2 + index] * rows_dev + i - side * side_rows + 1
                copy = pltpu.make_async_copy(
                    block.at[i],
                    panel.at[:, pl.ds(pl.multiple_of(slot * depth, depth), depth)],
                    block_sem.at[index * rows_dev + i],
                )
                yield (slot >= 0) & (slot < side_rows + 2), copy

    @pl.when(step == 0)
    def _():
        for copy in weight_copies():
            copy.start()
        for held, copy in block_copies():
            pl.when(held)(copy.start)
        last = (n_blocks * rows_dev) // side_rows - 1
        zeros = jnp.zeros((panel.shape[0], depth), panel.dtype)

        @pl.when(side == 0)
        def _():
            panel[:, pl.ds(0, depth)] = zeros

        @pl.when(side == last)
        def _():
            panel[:, pl.ds((side_rows + 1) * depth, depth)] = zeros

        for copy in weight_copies():
            copy.wait()
        for held, copy in block_copies():
            pl.when(held)(copy.wait)

    window = panel[:, pl.ds(pl.multiple_of(step * depth, depth), 3 * depth)]
    product = lax.dot_general(
        taps[...], window, (((1,), (1,)), ((), ())), preferred_element_type=jnp.float32
    )
    out[0] = (
        product[own : 2 * own]
        + move_columns(product[:own], 1)
        + move_columns(product[2 * own :], -1)
    )


def forward(place, weight, blocks, side_rows):
    rows_dev, width, depth = blocks[0].shape
    own = weight.shape[2]
    n_blocks = len(blocks)
    anywhere = pl.BlockSpec(memory_space=pl.ANY)
    return pl.pallas_call(
        functools.partial(forward_kernel, n_blocks),
        grid=(side_rows,),
        out_shape=jax.ShapeDtypeStruct((side_rows, own, width), jnp.float32),
        in_specs=[pl.BlockSpec(memory_space=pltpu.SMEM), anywhere] + [anywhere] * n_blocks,
        out_specs=pl.BlockSpec((1, own, width), lambda r: (r, 0, 0)),
        scratch_shapes=[
            pltpu.VMEM((3 * own, 3 * depth), weight.dtype),
            pltpu.VMEM((width, (side_rows + 2) * depth), blocks[0].dtype),
            pltpu.SemaphoreType.DMA((9,)),
            pltpu.SemaphoreType.DMA((n_blocks * rows_dev,)),
        ],
        compiler_params=pltpu.CompilerParams(vmem_limit_bytes=VMEM_LIMIT),
        cost_estimate=pl.CostEstimate(
            flops=18 * side_rows * own * width * depth,
            bytes_accessed=18 * own * depth + 6 * side_rows * width * depth,
            transcendentals=0,
        ),
    )(place, weight, *blocks)


def silu_parts(shifted, cotangent):
    sigmoid_v = jax.nn.sigmoid(shifted)
    slope = sigmoid_v * (1.0 + shifted * (1.0 - sigmoid_v))
    grad_out = (cotangent.astype(jnp.float32) * slope).astype(jnp.bfloat16)
    return sigmoid_v, grad_out


def silu_kernel(place, mine, theirs, bias, cotangent, grad_out, activated):
    shifted = (mine[0] + theirs[0]) + bias[...]
    sigmoid_v, grad_out[0] = silu_parts(shifted, cotangent[0])
    value = (shifted * sigmoid_v).astype(activated.dtype)
    half = activated.shape[2]
    first, second = value[:, :half], value[:, half:]
    activated[0] = jnp.where(place[1] == 0, first, second)


def silu(place, mine, theirs, bias, cotangent):
    rows, own, width = mine.shape
    row = pl.BlockSpec((1, own, width), lambda r: (r, 0, 0))
    return pl.pallas_call(
        silu_kernel,
        grid=(rows,),
        out_shape=(
            jax.ShapeDtypeStruct((rows, own, width), jnp.bfloat16),
            jax.ShapeDtypeStruct((rows, own, width // 2), jnp.bfloat16),
        ),
        in_specs=[
            pl.BlockSpec(memory_space=pltpu.SMEM),
            row,
            row,
            pl.BlockSpec((own, 1), lambda r: (0, 0)),
            row,
        ],
        out_specs=(row, pl.BlockSpec((1, own, width // 2), lambda r: (r, 0, 0))),
        compiler_params=pltpu.CompilerParams(vmem_limit_bytes=VMEM_LIMIT),
        cost_estimate=pl.CostEstimate(
            flops=10 * rows * own * width,
            bytes_accessed=14 * rows * own * width,
            transcendentals=2 * rows * own * width,
        ),
    )(place, mine, theirs, bias, cotangent)


def gradient_kernel(n_blocks, n_others, n_halves, place, bias, own_grad, *refs):
    blocks, refs = refs[:n_blocks], refs[n_blocks:]
    sides, refs = refs[:n_others], refs[n_others:]
    grad_weight, grad_bias, grads, panel, block_sem = refs
    rows_dev, width, depth = blocks[0].shape
    side_rows, own, _ = own_grad.shape
    all_rows = n_blocks * rows_dev
    step = pl.program_id(0)
    half_rows = side_rows // 2

    def block_copies():
        for index, block in enumerate(blocks):
            for i in range(rows_dev):
                slot = place[2 + index] * rows_dev + i + 1
                yield pltpu.make_async_copy(
                    block.at[i],
                    panel.at[pl.ds(pl.multiple_of(slot * width, width), width), :],
                    block_sem.at[index * rows_dev + i],
                )

    def keep(grad_out, row):
        wide = grad_out.astype(jnp.float32)
        at = pl.ds(pl.multiple_of(row * width, width), width)
        grads[pl.ds(0, own), at] = move_columns(wide, -1).astype(grads.dtype)
        grads[pl.ds(own, own), at] = grad_out
        grads[pl.ds(2 * own, own), at] = move_columns(wide, 1).astype(grads.dtype)

    @pl.when(step == 0)
    def _():
        for copy in block_copies():
            copy.start()
        zeros = jnp.zeros((width, depth), panel.dtype)
        panel[pl.ds(0, width), :] = zeros
        panel[pl.ds((all_rows + 1) * width, width), :] = zeros

        @pl.loop(0, side_rows)
        def _(r):
            keep(own_grad[r], place[0] * side_rows + r)

        for j in range(n_others // 4):
            mine, theirs, near, far = sides[4 * j : 4 * j + 4]
            side = lax.rem(place[0] + (n_others // 4 - j), n_others // 4 + 1)

            for h in range(2):
                cotangent = near if h == 0 else far
                start = (place[1] if h == 0 else 1 - place[1]) * half_rows

                @pl.loop(0, half_rows)
                def _(r):
                    shifted = (mine[start + r] + theirs[start + r]) + bias[...]
                    _, grad_out = silu_parts(shifted, cotangent[r])
                    keep(grad_out, side * side_rows + start + r)

        for copy in block_copies():
            copy.wait()
        ones = jnp.ones((16, grads.shape[1]), grads.dtype)
        sums = lax.dot_general(
            ones,
            grads[pl.ds(own, own), :],
            (((1,), (1,)), ((), ())),
            preferred_element_type=jnp.float32,
        )
        grad_bias[...] = sums[:1]

    window = panel[pl.ds(pl.multiple_of(step * width, width), all_rows * width), :]
    product = jnp.dot(grads[...], window, preferred_element_type=jnp.float32)
    grad_weight[0] = product.reshape(3, own, depth)


def gradient(place, bias, own_grad, blocks, sides):
    rows_dev, width, depth = blocks[0].shape
    _, own, _ = own_grad.shape
    n_blocks = len(blocks)
    all_rows = n_blocks * rows_dev
    anywhere = pl.BlockSpec(memory_space=pl.ANY)
    vmem = pl.BlockSpec(memory_space=pltpu.VMEM)
    return pl.pallas_call(
        functools.partial(gradient_kernel, n_blocks, len(sides), 2),
        grid=(3,),
        out_shape=(
            jax.ShapeDtypeStruct((3, 3, own, depth), jnp.float32),
            jax.ShapeDtypeStruct((1, own), jnp.float32),
        ),
        in_specs=[pl.BlockSpec(memory_space=pltpu.SMEM), vmem, vmem]
        + [anywhere] * n_blocks
        + [vmem] * len(sides),
        out_specs=(
            pl.BlockSpec((1, 3, own, depth), lambda a: (a, 0, 0, 0)),
            pl.BlockSpec((1, own), lambda a: (0, 0)),
        ),
        scratch_shapes=[
            pltpu.VMEM((3 * own, all_rows * width), jnp.bfloat16),
            pltpu.VMEM(((all_rows + 2) * width, depth), blocks[0].dtype),
            pltpu.SemaphoreType.DMA((n_blocks * rows_dev,)),
        ],
        compiler_params=pltpu.CompilerParams(vmem_limit_bytes=VMEM_LIMIT),
        cost_estimate=pl.CostEstimate(
            flops=18 * all_rows * own * width * depth,
            bytes_accessed=36 * own * depth + 2 * all_rows * width * depth,
            transcendentals=2 * all_rows * own * width,
        ),
    )(place, bias, own_grad, *blocks, *sides)


def on_device(image, weight, bias, cotangent):
    n_filt, n_sp = lax.axis_size("filt"), lax.axis_size("sp")
    filt, sp, half = lax.axis_index("filt"), lax.axis_index("sp"), lax.axis_index("in")
    side_rows = cotangent.shape[0]
    swap = shifted_ring("in", 1)

    blocks = gather_blocks(image)
    near = lax.dynamic_slice_in_dim(cotangent, half * (side_rows // 2), side_rows // 2, 0)
    halves = []
    for j in range(1, n_sp):
        near = lax.ppermute(near, "sp", shifted_ring("sp", 1))
        halves.append((near, lax.ppermute(near, "in", swap)))

    sides = [lax.rem(sp + (n_sp - j), n_sp) for j in range(n_sp)]
    flat = [block for side in blocks for block in side]
    at = [
        sides[j] * n_filt + lax.rem(filt + (n_filt - k), n_filt)
        for j in range(n_sp)
        for k in range(n_filt)
    ]
    bias_col = bias.reshape(-1, 1)

    place = [jnp.stack([side, half] + at).astype(jnp.int32) for side in sides]
    partial = [forward(place[j], weight, flat, side_rows) for j in range(n_sp)]
    other = [lax.ppermute(value, "in", swap) for value in partial]

    own_grad, activated = silu(place[0], partial[0], other[0], bias_col, cotangent)
    output = lax.all_to_all(activated, "filt", split_axis=0, concat_axis=1, tiled=True)
    rest = []
    for j in range(1, n_sp):
        rest += [partial[j], other[j], *halves[j - 1]]
    grad_weight, grad_bias = gradient(place[0], bias_col, own_grad, flat, rest)
    return (output, grad_weight, grad_bias.reshape(-1))


def solution(mesh):
    placed = (
        P(("groups", "sp", "filt"), None, "in"),
        P(None, None, "filt", None),
        P("filt"),
        P(("groups", "sp"), "filt", None),
    )
    return jax.shard_map(
        on_device,
        mesh=mesh,
        in_specs=placed,
        out_specs=(
            P(("groups", "sp", "filt"), None, "in"),
            P("groups", None, "filt", "in"),
            P(("groups", "filt")),
        ),
        check_vma=False,
    )
```

```python
import functools
import math

import jax
import jax.numpy as jnp
from jax import lax
from jax.experimental import pallas as pl
from jax.experimental.pallas import tpu as pltpu
from jax.sharding import PartitionSpec as P

MIB = 1024 * 1024


def params(*arrays):
    held = sum(math.prod(shape) * size for shape, size in arrays)
    return pltpu.CompilerParams(vmem_limit_bytes=max(20 * MIB, held * 5 // 4 + 8 * MIB))


def shifted_ring(axis, shift):
    size = lax.axis_size(axis)
    return [(i, (i + shift) % size) for i in range(size)]


def gather_blocks(image):
    n_filt, n_sp = lax.axis_size("filt"), lax.axis_size("sp")
    blocks = [[None] * n_filt for _ in range(n_sp)]
    blocks[0][0] = image
    for k in range(n_filt):
        if k:
            blocks[0][k] = lax.ppermute(blocks[0][k - 1], "filt", shifted_ring("filt", 1))
        for j in range(1, n_sp):
            if k and k == n_filt - 1:
                blocks[j][k] = lax.ppermute(blocks[j][0], "filt", shifted_ring("filt", -1))
            else:
                blocks[j][k] = lax.ppermute(blocks[j - 1][k], "sp", shifted_ring("sp", 1))
    return blocks


def move_columns(values, by):
    size = values.shape[1]
    column = lax.broadcasted_iota(jnp.int32, values.shape, 1)
    edge = 0 if by == 1 else size - 1
    return jnp.where(column == edge, 0.0, pltpu.roll(values, by % size, 1))


VMEM = pl.BlockSpec(memory_space=pltpu.VMEM)
SMEM = pl.BlockSpec(memory_space=pltpu.SMEM)
ANY = pl.BlockSpec(memory_space=pl.ANY)


def arrange_kernel(place, weight, out, sems):
    depth = out.shape[1] // 3
    own = weight.shape[2]
    copies = [
        pltpu.make_async_copy(
            weight.at[a, b, :, pl.ds(pl.multiple_of(place[1] * depth, depth), depth)],
            out.at[pl.ds(b * own, own), pl.ds(a * depth, depth)],
            sems.at[a * 3 + b],
        )
        for a in range(3)
        for b in range(3)
    ]
    for copy in copies:
        copy.start()
    for copy in copies:
        copy.wait()


def arrange(place, weight, depth):
    own = weight.shape[2]
    shape = (3 * own, 3 * depth)
    return pl.pallas_call(
        arrange_kernel,
        out_shape=jax.ShapeDtypeStruct(shape, weight.dtype),
        in_specs=[SMEM, ANY],
        out_specs=VMEM,
        scratch_shapes=[pltpu.SemaphoreType.DMA((9,))],
        compiler_params=params((shape, 2)),
        cost_estimate=pl.CostEstimate(
            flops=0, bytes_accessed=36 * own * depth, transcendentals=0
        ),
    )(place, weight)


def forward_kernel(n_blocks, n_sp, j, place, taps, *refs):
    blocks, (out, panel) = refs[:n_blocks], refs[n_blocks:]
    side_rows, own, width = out.shape
    rows_dev, _, depth = blocks[0].shape
    side = lax.rem(place[0] + (n_sp - j), n_sp)
    zeros = jnp.zeros((depth, width), panel.dtype)

    @pl.when(side == 0)
    def _():
        panel[pl.ds(0, depth), :] = zeros

    @pl.when(side == n_sp - 1)
    def _():
        panel[pl.ds((side_rows + 1) * depth, depth), :] = zeros

    for index, block in enumerate(blocks):
        for i in range(rows_dev):
            slot = place[2 + index] * rows_dev + i - side * side_rows + 1

            @pl.when((slot >= 0) & (slot < side_rows + 2))
            def _():
                panel[pl.ds(pl.multiple_of(slot * depth, depth), depth), :] = block[i].T

    @pl.loop(0, side_rows)
    def _(r):
        window = panel[pl.ds(pl.multiple_of(r * depth, depth), 3 * depth), :]
        product = jnp.dot(taps[...], window, preferred_element_type=jnp.float32)
        out[r] = (
            product[own : 2 * own]
            + move_columns(product[:own], 1)
            + move_columns(product[2 * own :], -1)
        )


def forward(place, taps, blocks, side_rows, n_sp, j):
    rows_dev, width, depth = blocks[0].shape
    own = taps.shape[0] // 3
    n_blocks = len(blocks)
    panel = ((side_rows + 2) * depth, width)
    out = (side_rows, own, width)
    return pl.pallas_call(
        functools.partial(forward_kernel, n_blocks, n_sp, j),
        out_shape=jax.ShapeDtypeStruct(out, jnp.float32),
        in_specs=[SMEM, VMEM] + [VMEM] * n_blocks,
        out_specs=VMEM,
        scratch_shapes=[pltpu.VMEM(panel, blocks[0].dtype)],
        compiler_params=params(
            (panel, 2), (out, 4), (taps.shape, 2), ((n_blocks * rows_dev, width, depth), 2)
        ),
        cost_estimate=pl.CostEstimate(
            flops=18 * side_rows * own * width * depth,
            bytes_accessed=18 * own * depth + 6 * side_rows * width * depth,
            transcendentals=0,
        ),
    )(place, taps, *blocks)


def silu_parts(shifted, cotangent):
    sigmoid_v = 0.5 * jnp.tanh(0.5 * shifted) + 0.5
    slope = sigmoid_v * (1.0 + shifted * (1.0 - sigmoid_v))
    grad_out = (cotangent.astype(jnp.float32) * slope).astype(jnp.bfloat16)
    return sigmoid_v, grad_out


def silu_kernel(place, mine, theirs, bias, cotangent, grad_out, activated):
    half = activated.shape[2]

    @pl.loop(0, mine.shape[0])
    def _(r):
        shifted = (mine[r] + theirs[r]) + bias[...]
        sigmoid_v, grad_out[r] = silu_parts(shifted, cotangent[r])
        value = (shifted * sigmoid_v).astype(activated.dtype)
        activated[r] = jnp.where(place[1] == 0, value[:, :half], value[:, half:])


def silu(place, mine, theirs, bias, cotangent):
    rows, own, width = mine.shape
    return pl.pallas_call(
        silu_kernel,
        out_shape=(
            jax.ShapeDtypeStruct((rows, own, width), jnp.bfloat16),
            jax.ShapeDtypeStruct((rows, own, width // 2), jnp.bfloat16),
        ),
        in_specs=[SMEM, VMEM, VMEM, VMEM, VMEM],
        out_specs=(VMEM, VMEM),
        compiler_params=params((mine.shape, 13)),
        cost_estimate=pl.CostEstimate(
            flops=10 * rows * own * width,
            bytes_accessed=13 * rows * own * width,
            transcendentals=rows * own * width,
        ),
    )(place, mine, theirs, bias, cotangent)


def gradient_kernel(n_blocks, n_sp, place, bias, own_grad, *refs):
    blocks, refs = refs[:n_blocks], refs[n_blocks:]
    others, refs = refs[: 4 * (n_sp - 1)], refs[4 * (n_sp - 1) :]
    grad_weight, grad_bias, grads, panel, stage, sems = refs
    rows_dev, width, depth = blocks[0].shape
    side_rows, own, _ = own_grad.shape
    all_rows = n_blocks * rows_dev
    half_rows = side_rows // 2

    def keep(grad_out, row):
        wide = grad_out.astype(jnp.float32)
        at = pl.ds(pl.multiple_of(row * width, width), width)
        grads[pl.ds(0, own), at] = move_columns(wide, -1).astype(grads.dtype)
        grads[pl.ds(own, own), at] = grad_out
        grads[pl.ds(2 * own, own), at] = move_columns(wide, 1).astype(grads.dtype)

    zeros = jnp.zeros((width, depth), panel.dtype)
    panel[pl.ds(0, width), :] = zeros
    panel[pl.ds((all_rows + 1) * width, width), :] = zeros
    for index, block in enumerate(blocks):
        for i in range(rows_dev):
            slot = place[2 + index] * rows_dev + i + 1
            panel[pl.ds(pl.multiple_of(slot * width, width), width), :] = block[i]

    @pl.loop(0, side_rows)
    def _(r):
        keep(own_grad[r], place[0] * side_rows + r)

    for j in range(1, n_sp):
        mine, theirs, near, far = others[4 * (j - 1) : 4 * j]
        side = lax.rem(place[0] + (n_sp - j), n_sp)
        for h, cotangent in enumerate((near, far)):
            start = (place[1] if h == 0 else 1 - place[1]) * half_rows

            @pl.loop(0, half_rows)
            def _(r):
                shifted = (mine[start + r] + theirs[start + r]) + bias[...]
                _, grad_out = silu_parts(shifted, cotangent[r])
                keep(grad_out, side * side_rows + start + r)

    ones = jnp.ones((16, grads.shape[1]), grads.dtype)
    sums = lax.dot_general(
        ones,
        grads[pl.ds(own, own), :],
        (((1,), (1,)), ((), ())),
        preferred_element_type=jnp.float32,
    )
    grad_bias[...] = sums[:1]

    def copy_out(a):
        return pltpu.make_async_copy(stage.at[a], grad_weight.at[a], sems.at[a])

    @pl.loop(0, 3)
    def _(a):
        window = panel[pl.ds(pl.multiple_of(a * width, width), all_rows * width), :]
        product = jnp.dot(grads[...], window, preferred_element_type=jnp.float32)
        stage[a] = product.reshape(3, own, depth)
        copy_out(a).start()

    @pl.loop(0, 3)
    def _(a):
        copy_out(a).wait()


def gradient(place, bias, own_grad, blocks, others, n_sp):
    rows_dev, width, depth = blocks[0].shape
    side_rows, own, _ = own_grad.shape
    n_blocks = len(blocks)
    all_rows = n_blocks * rows_dev
    grads = (3 * own, all_rows * width)
    panel = ((all_rows + 2) * width, depth)
    stage = (3, 3, own, depth)
    return pl.pallas_call(
        functools.partial(gradient_kernel, n_blocks, n_sp),
        out_shape=(
            jax.ShapeDtypeStruct(stage, jnp.float32),
            jax.ShapeDtypeStruct((1, own), jnp.float32),
        ),
        in_specs=[SMEM, VMEM, VMEM] + [VMEM] * (n_blocks + len(others)),
        out_specs=(ANY, VMEM),
        scratch_shapes=[
            pltpu.VMEM(grads, jnp.bfloat16),
            pltpu.VMEM(panel, blocks[0].dtype),
            pltpu.VMEM(stage, jnp.float32),
            pltpu.SemaphoreType.DMA((3,)),
        ],
        compiler_params=params(
            (grads, 2), (panel, 2), (stage, 4), (panel, 2), ((all_rows, own, width), 10)
        ),
        cost_estimate=pl.CostEstimate(
            flops=18 * all_rows * own * width * depth,
            bytes_accessed=36 * own * depth + 2 * all_rows * width * depth,
            transcendentals=all_rows * own * width,
        ),
    )(place, bias, own_grad, *blocks, *others)


def on_device(image, weight, bias, cotangent):
    n_filt, n_sp = lax.axis_size("filt"), lax.axis_size("sp")
    filt, sp, half = lax.axis_index("filt"), lax.axis_index("sp"), lax.axis_index("in")
    side_rows = cotangent.shape[0]
    swap = shifted_ring("in", 1)

    near = lax.dynamic_slice_in_dim(cotangent, half * (side_rows // 2), side_rows // 2, 0)
    halves = []
    for j in range(1, n_sp):
        near = lax.ppermute(near, "sp", shifted_ring("sp", 1))
        halves += [near, lax.ppermute(near, "in", swap)]
    blocks = [block for side in gather_blocks(image) for block in side]

    at = [
        lax.rem(sp + (n_sp - j), n_sp) * n_filt + lax.rem(filt + (n_filt - k), n_filt)
        for j in range(n_sp)
        for k in range(n_filt)
    ]
    place = jnp.stack([sp, half] + at).astype(jnp.int32)
    bias_col = bias.reshape(-1, 1)
    taps = arrange(place, weight, image.shape[2])
    place, taps, bias_col, *halves = lax.optimization_barrier(
        (place, taps, bias_col, *halves)
    )

    partial = [forward(place, taps, blocks, side_rows, n_sp, j) for j in range(n_sp)]
    other = [lax.ppermute(value, "in", swap) for value in partial]

    own_grad, activated = silu(place, partial[0], other[0], bias_col, cotangent)
    output = lax.all_to_all(activated, "filt", split_axis=0, concat_axis=1, tiled=True)
    others = []
    for j in range(1, n_sp):
        others += [partial[j], other[j], *halves[2 * j - 2 : 2 * j]]
    grad_weight, grad_bias = gradient(place, bias_col, own_grad, blocks, others, n_sp)
    return (output, grad_weight, grad_bias.reshape(-1))


def solution(mesh):
    placed = (
        P(("groups", "sp", "filt"), None, "in"),
        P(None, None, "filt", None),
        P("filt"),
        P(("groups", "sp"), "filt", None),
    )
    return jax.shard_map(
        on_device,
        mesh=mesh,
        in_specs=placed,
        out_specs=(
            P(("groups", "sp", "filt"), None, "in"),
            P("groups", None, "filt", "in"),
            P(("groups", "filt")),
        ),
        check_vma=False,
    )
```

```python
import functools
import math

import jax
import jax.numpy as jnp
from jax import lax
from jax.experimental import pallas as pl
from jax.experimental.pallas import tpu as pltpu
from jax.sharding import PartitionSpec as P

MIB = 1024 * 1024


def params(*arrays):
    held = sum(math.prod(shape) * size for shape, size in arrays)
    return pltpu.CompilerParams(vmem_limit_bytes=max(20 * MIB, held * 5 // 4 + 8 * MIB))


def shifted_ring(axis, shift):
    size = lax.axis_size(axis)
    return [(i, (i + shift) % size) for i in range(size)]


def gather_blocks(image):
    n_filt, n_sp = lax.axis_size("filt"), lax.axis_size("sp")
    blocks = [[None] * n_filt for _ in range(n_sp)]
    blocks[0][0] = image
    for k in range(n_filt):
        if k:
            blocks[0][k] = lax.ppermute(blocks[0][k - 1], "filt", shifted_ring("filt", 1))
        for j in range(1, n_sp):
            if k and k == n_filt - 1:
                blocks[j][k] = lax.ppermute(blocks[j][0], "filt", shifted_ring("filt", -1))
            else:
                blocks[j][k] = lax.ppermute(blocks[j - 1][k], "sp", shifted_ring("sp", 1))
    return blocks


def move_columns(values, by):
    size = values.shape[1]
    column = lax.broadcasted_iota(jnp.int32, values.shape, 1)
    edge = 0 if by == 1 else size - 1
    return jnp.where(column == edge, 0.0, pltpu.roll(values, by % size, 1))


VMEM = pl.BlockSpec(memory_space=pltpu.VMEM)
ANY = pl.BlockSpec(memory_space=pl.ANY)
HBM = pl.BlockSpec(memory_space=pltpu.HBM)


def behind(axis, size, by):
    return lax.rem(lax.axis_index(axis) + (size - by), size)


def half_kernel(cotangent, out, sem):
    rows = out.shape[0]
    copy = pltpu.make_async_copy(
        cotangent.at[pl.ds(lax.axis_index("in") * rows, rows)], out, sem
    )
    copy.start()
    copy.wait()


def own_half(cotangent):
    shape = (cotangent.shape[0] // 2,) + cotangent.shape[1:]
    return pl.pallas_call(
        half_kernel,
        out_shape=jax.ShapeDtypeStruct(shape, cotangent.dtype),
        in_specs=[HBM],
        out_specs=VMEM,
        scratch_shapes=[pltpu.SemaphoreType.DMA],
        compiler_params=params((shape, 2)),
        cost_estimate=pl.CostEstimate(
            flops=0, bytes_accessed=4 * math.prod(shape), transcendentals=0
        ),
    )(cotangent)


def arrange_kernel(weight, bias, taps, bias_col, sems):
    depth = taps.shape[1] // 3
    own = weight.shape[2]
    half = lax.axis_index("in")
    copies = [
        pltpu.make_async_copy(
            weight.at[a, b, :, pl.ds(pl.multiple_of(half * depth, depth), depth)],
            taps.at[pl.ds(b * own, own), pl.ds(a * depth, depth)],
            sems.at[a * 3 + b],
        )
        for a in range(3)
        for b in range(3)
    ]
    for copy in copies:
        copy.start()
    bias_col[...] = jnp.broadcast_to(bias[...], (128, own)).T[:, :1]
    for copy in copies:
        copy.wait()


def arrange(weight, bias, depth):
    own = weight.shape[2]
    shape = (3 * own, 3 * depth)
    return pl.pallas_call(
        arrange_kernel,
        out_shape=(
            jax.ShapeDtypeStruct(shape, weight.dtype),
            jax.ShapeDtypeStruct((own, 1), bias.dtype),
        ),
        in_specs=[HBM, VMEM],
        out_specs=(VMEM, VMEM),
        scratch_shapes=[pltpu.SemaphoreType.DMA((9,))],
        compiler_params=params((shape, 2)),
        cost_estimate=pl.CostEstimate(
            flops=0, bytes_accessed=36 * own * depth, transcendentals=0
        ),
    )(weight, bias.reshape(1, own))


def block_place(index, n_filt, n_sp):
    j, k = divmod(index, n_filt)
    return behind("sp", n_sp, j) * n_filt + behind("filt", n_filt, k)


def forward_kernel(n_blocks, n_sp, j, taps, *refs):
    blocks, (out, panel) = refs[:n_blocks], refs[n_blocks:]
    side_rows, own, width = out.shape
    rows_dev, _, depth = blocks[0].shape
    side = behind("sp", n_sp, j)
    zeros = jnp.zeros((depth, width), panel.dtype)

    @pl.when(side == 0)
    def _():
        panel[pl.ds(0, depth), :] = zeros

    @pl.when(side == n_sp - 1)
    def _():
        panel[pl.ds((side_rows + 1) * depth, depth), :] = zeros

    for index, block in enumerate(blocks):
        for i in range(rows_dev):
            place = block_place(index, n_blocks // n_sp, n_sp)
            slot = place * rows_dev + i - side * side_rows + 1

            @pl.when((slot >= 0) & (slot < side_rows + 2))
            def _():
                panel[pl.ds(pl.multiple_of(slot * depth, depth), depth), :] = block[i].T

    @pl.loop(0, side_rows)
    def _(r):
        window = panel[pl.ds(pl.multiple_of(r * depth, depth), 3 * depth), :]
        product = jnp.dot(taps[...], window, preferred_element_type=jnp.float32)
        out[r] = (
            product[own : 2 * own]
            + move_columns(product[:own], 1)
            + move_columns(product[2 * own :], -1)
        )


def forward(taps, blocks, side_rows, n_sp, j):
    rows_dev, width, depth = blocks[0].shape
    own = taps.shape[0] // 3
    n_blocks = len(blocks)
    panel = ((side_rows + 2) * depth, width)
    out = (side_rows, own, width)
    return pl.pallas_call(
        functools.partial(forward_kernel, n_blocks, n_sp, j),
        out_shape=jax.ShapeDtypeStruct(out, jnp.float32),
        in_specs=[VMEM] * (1 + n_blocks),
        out_specs=VMEM,
        scratch_shapes=[pltpu.VMEM(panel, blocks[0].dtype)],
        compiler_params=params(
            (panel, 2), (out, 4), (taps.shape, 2), ((n_blocks * rows_dev, width, depth), 2)
        ),
        cost_estimate=pl.CostEstimate(
            flops=18 * side_rows * own * width * depth,
            bytes_accessed=18 * own * depth + 6 * side_rows * width * depth,
            transcendentals=0,
        ),
    )(taps, *blocks)


def silu_parts(shifted, cotangent):
    sigmoid_v = 0.5 * jnp.tanh(0.5 * shifted) + 0.5
    slope = sigmoid_v * (1.0 + shifted * (1.0 - sigmoid_v))
    grad_out = (cotangent.astype(jnp.float32) * slope).astype(jnp.bfloat16)
    return sigmoid_v, grad_out


def silu_kernel(n_filt, mine, theirs, bias, cotangent, grad_out, *activated):
    rows, _, half = activated[0].shape

    for k in range(n_filt):
        first = behind("filt", n_filt, n_filt - k if k else 0) * rows

        @pl.loop(0, rows)
        def _(i):
            r = first + i
            shifted = (mine[r] + theirs[r]) + bias[...]
            sigmoid_v, grad_out[r] = silu_parts(shifted, cotangent[r])
            value = (shifted * sigmoid_v).astype(activated[k].dtype)
            activated[k][i] = jnp.where(
                lax.axis_index("in") == 0, value[:, :half], value[:, half:]
            )


def silu(mine, theirs, bias, cotangent, n_filt):
    rows, own, width = mine.shape
    return pl.pallas_call(
        functools.partial(silu_kernel, n_filt),
        out_shape=[jax.ShapeDtypeStruct((rows, own, width), jnp.bfloat16)]
        + [jax.ShapeDtypeStruct((rows // n_filt, own, width // 2), jnp.bfloat16)] * n_filt,
        in_specs=[VMEM] * 4,
        out_specs=[VMEM] * (1 + n_filt),
        compiler_params=params((mine.shape, 13)),
        cost_estimate=pl.CostEstimate(
            flops=10 * rows * own * width,
            bytes_accessed=13 * rows * own * width,
            transcendentals=rows * own * width,
        ),
    )(mine, theirs, bias, cotangent)


def gradient_kernel(n_filt, n_sp, bias, own_grad, *refs):
    n_blocks = n_filt * n_sp
    blocks, refs = refs[:n_blocks], refs[n_blocks:]
    others, refs = refs[: 4 * (n_sp - 1)], refs[4 * (n_sp - 1) :]
    pieces, refs = refs[:n_filt], refs[n_filt:]
    output, grad_weight, grad_bias, grads, panel, stage, sems, piece_sems = refs
    rows_dev, width, depth = blocks[0].shape
    side_rows, own, _ = own_grad.shape
    all_rows = n_blocks * rows_dev
    half_rows = side_rows // 2

    piece_copies = [
        pltpu.make_async_copy(
            piece,
            output.at[:, pl.ds(pl.multiple_of(behind("filt", n_filt, k) * own, own), own), :],
            piece_sems.at[k],
        )
        for k, piece in enumerate(pieces)
    ]
    for copy in piece_copies:
        copy.start()

    def keep(grad_out, row):
        wide = grad_out.astype(jnp.float32)
        at = pl.ds(pl.multiple_of(row * width, width), width)
        grads[pl.ds(0, own), at] = move_columns(wide, -1).astype(grads.dtype)
        grads[pl.ds(own, own), at] = grad_out
        grads[pl.ds(2 * own, own), at] = move_columns(wide, 1).astype(grads.dtype)

    zeros = jnp.zeros((width, depth), panel.dtype)
    panel[pl.ds(0, width), :] = zeros
    panel[pl.ds((all_rows + 1) * width, width), :] = zeros
    for index, block in enumerate(blocks):
        for i in range(rows_dev):
            slot = block_place(index, n_filt, n_sp) * rows_dev + i + 1
            panel[pl.ds(pl.multiple_of(slot * width, width), width), :] = block[i]

    @pl.loop(0, side_rows)
    def _(r):
        keep(own_grad[r], lax.axis_index("sp") * side_rows + r)

    for j in range(1, n_sp):
        mine, theirs, near, far = others[4 * (j - 1) : 4 * j]
        side = behind("sp", n_sp, j)
        half = lax.axis_index("in")
        for h, cotangent in enumerate((near, far)):
            start = (half if h == 0 else 1 - half) * half_rows

            @pl.loop(0, half_rows)
            def _(r):
                shifted = (mine[start + r] + theirs[start + r]) + bias[...]
                _, grad_out = silu_parts(shifted, cotangent[r])
                keep(grad_out, side * side_rows + start + r)

    ones = jnp.ones((16, grads.shape[1]), grads.dtype)
    sums = lax.dot_general(
        ones,
        grads[pl.ds(own, own), :],
        (((1,), (1,)), ((), ())),
        preferred_element_type=jnp.float32,
    )
    grad_bias[...] = sums[:1]

    def copy_out(a):
        return pltpu.make_async_copy(stage.at[a], grad_weight.at[a], sems.at[a])

    @pl.loop(0, 3)
    def _(a):
        window = panel[pl.ds(pl.multiple_of(a * width, width), all_rows * width), :]
        product = jnp.dot(grads[...], window, preferred_element_type=jnp.float32)
        stage[a] = product.reshape(3, own, depth)
        copy_out(a).start()

    @pl.loop(0, 3)
    def _(a):
        copy_out(a).wait()

    for copy in piece_copies:
        copy.wait()


def gradient(bias, own_grad, blocks, others, pieces, n_sp):
    rows_dev, width, depth = blocks[0].shape
    side_rows, own, _ = own_grad.shape
    n_blocks = len(blocks)
    all_rows = n_blocks * rows_dev
    grads = (3 * own, all_rows * width)
    panel = ((all_rows + 2) * width, depth)
    stage = (3, 3, own, depth)
    return pl.pallas_call(
        functools.partial(gradient_kernel, len(pieces), n_sp),
        out_shape=(
            jax.ShapeDtypeStruct((rows_dev, len(pieces) * own, width // 2), jnp.bfloat16),
            jax.ShapeDtypeStruct(stage, jnp.float32),
            jax.ShapeDtypeStruct((1, own), jnp.float32),
        ),
        in_specs=[VMEM] * (2 + n_blocks + len(others) + len(pieces)),
        out_specs=(ANY, ANY, VMEM),
        scratch_shapes=[
            pltpu.VMEM(grads, jnp.bfloat16),
            pltpu.VMEM(panel, blocks[0].dtype),
            pltpu.VMEM(stage, jnp.float32),
            pltpu.SemaphoreType.DMA((3,)),
            pltpu.SemaphoreType.DMA((len(pieces),)),
        ],
        compiler_params=params(
            (grads, 2), (panel, 2), (stage, 4), (panel, 2), ((all_rows, own, width), 10)
        ),
        cost_estimate=pl.CostEstimate(
            flops=18 * all_rows * own * width * depth,
            bytes_accessed=36 * own * depth + 2 * all_rows * width * depth,
            transcendentals=all_rows * own * width,
        ),
    )(bias, own_grad, *blocks, *others, *pieces)


def on_device(image, weight, bias, cotangent):
    n_filt, n_sp = lax.axis_size("filt"), lax.axis_size("sp")
    side_rows = cotangent.shape[0]
    swap = shifted_ring("in", 1)

    blocks = [block for side in gather_blocks(image) for block in side]
    near = own_half(cotangent)
    halves = []
    for j in range(1, n_sp):
        near = lax.ppermute(near, "sp", shifted_ring("sp", 1))
        halves += [near, lax.ppermute(near, "in", swap)]
    taps, bias_col = arrange(weight, bias, image.shape[2])
    taps, bias_col, *halves = lax.optimization_barrier((taps, bias_col, *halves))

    partial = [forward(taps, blocks, side_rows, n_sp, j) for j in range(n_sp)]
    other = [lax.ppermute(value, "in", swap) for value in partial]

    own_grad, *rows = silu(partial[0], other[0], bias_col, cotangent, n_filt)
    pieces = rows[:1]
    for k in range(1, n_filt):
        pieces.append(lax.ppermute(rows[k], "filt", shifted_ring("filt", k)))
    others = []
    for j in range(1, n_sp):
        others += [partial[j], other[j], *halves[2 * j - 2 : 2 * j]]
    output, grad_weight, grad_bias = gradient(
        bias_col, own_grad, blocks, others, pieces, n_sp
    )
    return (output, grad_weight, grad_bias.reshape(-1))


def solution(mesh):
    placed = (
        P(("groups", "sp", "filt"), None, "in"),
        P(None, None, "filt", None),
        P("filt"),
        P(("groups", "sp"), "filt", None),
    )
    return jax.shard_map(
        on_device,
        mesh=mesh,
        in_specs=placed,
        out_specs=(
            P(("groups", "sp", "filt"), None, "in"),
            P("groups", None, "filt", "in"),
            P(("groups", "filt")),
        ),
        check_vma=False,
    )
```

```python
import functools
import math

import jax
import jax.numpy as jnp
from jax import lax
from jax.experimental import pallas as pl
from jax.experimental.pallas import tpu as pltpu
from jax.sharding import PartitionSpec as P

MIB = 1024 * 1024


def params(*arrays):
    held = sum(math.prod(shape) * size for shape, size in arrays)
    return pltpu.CompilerParams(vmem_limit_bytes=max(20 * MIB, held * 5 // 4 + 8 * MIB))


def shifted_ring(axis, shift):
    size = lax.axis_size(axis)
    return [(i, (i + shift) % size) for i in range(size)]


def folded_ring(axis, shift):
    size = lax.axis_size(axis)
    order = [0, *range(1, size, 2), *reversed(range(2, size, 2))]
    return [(order[i], order[(i + shift) % size]) for i in range(size)]


def folded_behind(axis, size, by):
    index = lax.axis_index(axis)
    back = size - lax.div(index, 2)
    place = jnp.where(lax.rem(index, 2) == 1, lax.div(index + 1, 2), lax.rem(back, size))
    place = lax.rem(place + (size - by), size)
    out = 2 * place - 1
    return jnp.where(place == 0, 0, jnp.where(place <= size // 2, out, 2 * (size - place)))


def gather_blocks(image):
    n_filt, n_sp = lax.axis_size("filt"), lax.axis_size("sp")
    blocks = [[None] * n_filt for _ in range(n_sp)]
    blocks[0][0] = image
    for k in range(n_filt):
        if k:
            blocks[0][k] = lax.ppermute(blocks[0][k - 1], "filt", folded_ring("filt", 1))
        for j in range(1, n_sp):
            if k and k == n_filt - 1:
                blocks[j][k] = lax.ppermute(blocks[j][0], "filt", folded_ring("filt", -1))
            else:
                blocks[j][k] = lax.ppermute(blocks[j - 1][k], "sp", shifted_ring("sp", 1))
    return blocks


def move_columns(values, by):
    size = values.shape[1]
    column = lax.broadcasted_iota(jnp.int32, values.shape, 1)
    edge = 0 if by == 1 else size - 1
    return jnp.where(column == edge, 0.0, pltpu.roll(values, by % size, 1))


VMEM = pl.BlockSpec(memory_space=pltpu.VMEM)
ANY = pl.BlockSpec(memory_space=pl.ANY)


def behind(axis, size, by):
    return lax.rem(lax.axis_index(axis) + (size - by), size)


def half_kernel(cotangent, _, out, sem):
    rows = out.shape[0]
    copy = pltpu.make_async_copy(
        cotangent.at[pl.ds(lax.axis_index("in") * rows, rows)], out, sem
    )
    copy.start()
    copy.wait()


def own_half(cotangent, after):
    shape = (cotangent.shape[0] // 2,) + cotangent.shape[1:]
    return pl.pallas_call(
        half_kernel,
        out_shape=jax.ShapeDtypeStruct(shape, cotangent.dtype),
        in_specs=[ANY, ANY],
        out_specs=VMEM,
        scratch_shapes=[pltpu.SemaphoreType.DMA],
        compiler_params=params((shape, 2)),
        cost_estimate=pl.CostEstimate(
            flops=0, bytes_accessed=4 * math.prod(shape), transcendentals=0
        ),
    )(cotangent, after)


def arrange_kernel(weight, bias, taps, bias_col, sems):
    depth = taps.shape[1] // 3
    own = weight.shape[2]
    half = lax.axis_index("in")
    copies = [
        pltpu.make_async_copy(
            weight.at[a, b, :, pl.ds(pl.multiple_of(half * depth, depth), depth)],
            taps.at[pl.ds(b * own, own), pl.ds(a * depth, depth)],
            sems.at[a * 3 + b],
        )
        for a in range(3)
        for b in range(3)
    ]
    for copy in copies:
        copy.start()
    bias_col[...] = jnp.broadcast_to(bias[...], (128, own)).T[:, :1]
    for copy in copies:
        copy.wait()


def arrange(weight, bias, depth):
    own = weight.shape[2]
    shape = (3 * own, 3 * depth)
    return pl.pallas_call(
        arrange_kernel,
        out_shape=(
            jax.ShapeDtypeStruct(shape, weight.dtype),
            jax.ShapeDtypeStruct((own, 1), bias.dtype),
        ),
        in_specs=[ANY, VMEM],
        out_specs=(VMEM, VMEM),
        scratch_shapes=[pltpu.SemaphoreType.DMA((9,))],
        compiler_params=params((shape, 2)),
        cost_estimate=pl.CostEstimate(
            flops=0, bytes_accessed=36 * own * depth, transcendentals=0
        ),
    )(weight, bias.reshape(1, own))


def block_place(index, n_filt, n_sp):
    j, k = divmod(index, n_filt)
    return behind("sp", n_sp, j) * n_filt + folded_behind("filt", n_filt, k)


def forward_kernel(n_blocks, n_sp, j, taps, *refs):
    blocks, (out, panel) = refs[:n_blocks], refs[n_blocks:]
    side_rows, own, width = out.shape
    rows_dev, _, depth = blocks[0].shape
    side = behind("sp", n_sp, j)
    zeros = jnp.zeros((depth, width), panel.dtype)

    @pl.when(side == 0)
    def _():
        panel[pl.ds(0, depth), :] = zeros

    @pl.when(side == n_sp - 1)
    def _():
        panel[pl.ds((side_rows + 1) * depth, depth), :] = zeros

    for index, block in enumerate(blocks):
        for i in range(rows_dev):
            place = block_place(index, n_blocks // n_sp, n_sp)
            slot = place * rows_dev + i - side * side_rows + 1

            @pl.when((slot >= 0) & (slot < side_rows + 2))
            def _():
                panel[pl.ds(pl.multiple_of(slot * depth, depth), depth), :] = block[i].T

    @pl.loop(0, side_rows, unroll=4)
    def _(r):
        window = panel[pl.ds(pl.multiple_of(r * depth, depth), 3 * depth), :]
        product = jnp.dot(taps[...], window, preferred_element_type=jnp.float32)
        out[r] = (
            product[own : 2 * own]
            + move_columns(product[:own], 1)
            + move_columns(product[2 * own :], -1)
        )


def forward(taps, blocks, side_rows, n_sp, j):
    rows_dev, width, depth = blocks[0].shape
    own = taps.shape[0] // 3
    n_blocks = len(blocks)
    panel = ((side_rows + 2) * depth, width)
    out = (side_rows, own, width)
    return pl.pallas_call(
        functools.partial(forward_kernel, n_blocks, n_sp, j),
        out_shape=jax.ShapeDtypeStruct(out, jnp.float32),
        in_specs=[VMEM] * (1 + n_blocks),
        out_specs=VMEM,
        scratch_shapes=[pltpu.VMEM(panel, blocks[0].dtype)],
        compiler_params=params(
            (panel, 2), (out, 4), (taps.shape, 2), ((n_blocks * rows_dev, width, depth), 2)
        ),
        cost_estimate=pl.CostEstimate(
            flops=18 * side_rows * own * width * depth,
            bytes_accessed=18 * own * depth + 6 * side_rows * width * depth,
            transcendentals=0,
        ),
    )(taps, *blocks)


def silu_parts(shifted, cotangent):
    sigmoid_v = 0.5 * jnp.tanh(0.5 * shifted) + 0.5
    slope = sigmoid_v * (1.0 + shifted * (1.0 - sigmoid_v))
    grad_out = (cotangent.astype(jnp.float32) * slope).astype(jnp.bfloat16)
    return sigmoid_v, grad_out


def silu_kernel(n_filt, mine, theirs, bias, cotangent, grad_out, *activated):
    rows, _, half = activated[0].shape

    for k in range(n_filt):
        first = behind("filt", n_filt, n_filt - k if k else 0) * rows

        @pl.loop(0, rows)
        def _(i):
            r = first + i
            shifted = (mine[r] + theirs[r]) + bias[...]
            sigmoid_v, grad_out[r] = silu_parts(shifted, cotangent[r])
            value = (shifted * sigmoid_v).astype(activated[k].dtype)
            activated[k][i] = jnp.where(
                lax.axis_index("in") == 0, value[:, :half], value[:, half:]
            )


def silu(mine, theirs, bias, cotangent, n_filt):
    rows, own, width = mine.shape
    return pl.pallas_call(
        functools.partial(silu_kernel, n_filt),
        out_shape=[jax.ShapeDtypeStruct((rows, own, width), jnp.bfloat16)]
        + [jax.ShapeDtypeStruct((rows // n_filt, own, width // 2), jnp.bfloat16)] * n_filt,
        in_specs=[VMEM] * 4,
        out_specs=[VMEM] * (1 + n_filt),
        compiler_params=params((mine.shape, 13)),
        cost_estimate=pl.CostEstimate(
            flops=10 * rows * own * width,
            bytes_accessed=13 * rows * own * width,
            transcendentals=rows * own * width,
        ),
    )(mine, theirs, bias, cotangent)


def shift_grads(grads, grad_out, row):
    own, width = grad_out.shape
    wide = grad_out.astype(jnp.float32)
    at = pl.ds(pl.multiple_of(row * width, width), width)
    grads[pl.ds(0, own), at] = move_columns(wide, -1).astype(grads.dtype)
    grads[pl.ds(own, own), at] = grad_out
    grads[pl.ds(2 * own, own), at] = move_columns(wide, 1).astype(grads.dtype)


def place_blocks(panel, blocks, n_sp, j, side_rows):
    rows_dev, width, depth = blocks[0].shape
    side = behind("sp", n_sp, j)
    zeros = jnp.zeros((width, depth), panel.dtype)

    @pl.when(side == 0)
    def _():
        panel[pl.ds(0, width), :] = zeros

    @pl.when(side == n_sp - 1)
    def _():
        panel[pl.ds((side_rows + 1) * width, width), :] = zeros

    for index, block in enumerate(blocks):
        for i in range(rows_dev):
            place = block_place(index, len(blocks) // n_sp, n_sp)
            slot = place * rows_dev + i - side * side_rows + 1

            @pl.when((slot >= 0) & (slot < side_rows + 2))
            def _():
                panel[pl.ds(pl.multiple_of(slot * width, width), width), :] = block[i]


def row_sums(grads):
    own = grads.shape[0] // 3
    ones = jnp.ones((16, grads.shape[1]), grads.dtype)
    sums = lax.dot_general(
        ones,
        grads[pl.ds(own, own), :],
        (((1,), (1,)), ((), ())),
        preferred_element_type=jnp.float32,
    )
    return sums[:1]


def tap_gradient(grads, panel, a, width):
    window = panel[pl.ds(pl.multiple_of(a * width, width), grads.shape[1]), :]
    product = jnp.dot(grads[...], window, preferred_element_type=jnp.float32)
    return product.reshape(3, grads.shape[0] // 3, panel.shape[1])


def own_gradient_kernel(n_sp, own_grad, *refs):
    blocks, (weight_sum, bias_sum, grads, panel) = refs[:-4], refs[-4:]
    side_rows, _, width = own_grad.shape
    place_blocks(panel, blocks, n_sp, 0, side_rows)

    @pl.loop(0, side_rows)
    def _(r):
        shift_grads(grads, own_grad[r], r)

    bias_sum[...] = row_sums(grads)

    @pl.loop(0, 3)
    def _(a):
        weight_sum[a] = tap_gradient(grads, panel, a, width)


def add_gradient_kernel(n_sp, j, n_pieces, bias, mine, theirs, near, far, *refs):
    (weight_in, bias_in), refs = refs[:2], refs[2:]
    pieces, refs = refs[:n_pieces], refs[n_pieces:]
    if pieces:
        *refs, stage, sems, piece_sems = refs
    *blocks, weight_sum, bias_sum, grads, panel = refs
    if pieces:
        *blocks, output = blocks
    side_rows, own, width = mine.shape
    half_rows = side_rows // 2
    half = lax.axis_index("in")

    piece_copies = [
        pltpu.make_async_copy(
            piece,
            output.at[
                :, pl.ds(pl.multiple_of(behind("filt", n_pieces, k) * own, own), own), :
            ],
            piece_sems.at[k],
        )
        for k, piece in enumerate(pieces)
    ]
    for copy in piece_copies:
        copy.start()

    place_blocks(panel, blocks, n_sp, j, side_rows)
    for h, cotangent in enumerate((near, far)):
        start = (half if h == 0 else 1 - half) * half_rows

        @pl.loop(0, half_rows)
        def _(r):
            shifted = (mine[start + r] + theirs[start + r]) + bias[...]
            _, grad_out = silu_parts(shifted, cotangent[r])
            shift_grads(grads, grad_out, start + r)

    bias_sum[...] = bias_in[...] + row_sums(grads)

    def copy_out(a):
        return pltpu.make_async_copy(stage.at[a], weight_sum.at[a], sems.at[a])

    @pl.loop(0, 3)
    def _(a):
        total = weight_in[a] + tap_gradient(grads, panel, a, width)
        if pieces:
            stage[a] = total
            copy_out(a).start()
        else:
            weight_sum[a] = total

    if pieces:

        @pl.loop(0, 3)
        def _(a):
            copy_out(a).wait()

    for copy in piece_copies:
        copy.wait()


def gradient_call(kernel, operands, blocks, shape, first_out=(), specs=(VMEM, VMEM), scratch=()):
    side_rows, own, width = shape
    _, _, depth = blocks[0].shape
    grads = (3 * own, side_rows * width)
    panel = ((side_rows + 2) * width, depth)
    total = (3, 3, own, depth)
    held = math.prod((len(blocks),) + blocks[0].shape)
    return pl.pallas_call(
        kernel,
        out_shape=[
            *first_out,
            jax.ShapeDtypeStruct(total, jnp.float32),
            jax.ShapeDtypeStruct((1, own), jnp.float32),
        ],
        in_specs=[VMEM] * (len(operands) + len(blocks)),
        out_specs=list(specs),
        scratch_shapes=[
            pltpu.VMEM(grads, jnp.bfloat16),
            pltpu.VMEM(panel, blocks[0].dtype),
            *scratch,
        ],
        compiler_params=params((grads, 2), (panel, 2), (total, 8), (shape, 12), ((held,), 2)),
        cost_estimate=pl.CostEstimate(
            flops=18 * side_rows * own * width * depth,
            bytes_accessed=36 * own * depth + 2 * side_rows * width * depth,
            transcendentals=side_rows * own * width,
        ),
    )(*operands, *blocks)


def own_gradient(own_grad, blocks, n_sp):
    return gradient_call(
        functools.partial(own_gradient_kernel, n_sp), [own_grad], blocks, own_grad.shape
    )


def add_gradient(j, bias, side, sums, blocks, pieces, n_sp):
    shape = side[0].shape
    rows_dev, width, depth = blocks[0].shape
    own = shape[1]
    kernel = functools.partial(add_gradient_kernel, n_sp, j, len(pieces))
    operands = [bias, *side, *sums, *pieces]
    if not pieces:
        return gradient_call(kernel, operands, blocks, shape)
    rows = jax.ShapeDtypeStruct((rows_dev, len(pieces) * own, width // 2), pieces[0].dtype)
    scratch = [
        pltpu.VMEM((3, 3, own, depth), jnp.float32),
        pltpu.SemaphoreType.DMA((3,)),
        pltpu.SemaphoreType.DMA((len(pieces),)),
    ]
    return gradient_call(kernel, operands, blocks, shape, [rows], (ANY, ANY, VMEM), scratch)


def on_device(image, weight, bias, cotangent):
    n_filt, n_sp = lax.axis_size("filt"), lax.axis_size("sp")
    side_rows = cotangent.shape[0]
    swap = shifted_ring("in", 1)

    blocks = [block for side in gather_blocks(image) for block in side]
    near = own_half(cotangent, blocks[n_filt])
    halves = []
    for j in range(1, n_sp):
        near = lax.ppermute(near, "sp", shifted_ring("sp", 1))
        halves += [near, lax.ppermute(near, "in", swap)]
    taps, bias_col = arrange(weight, bias, image.shape[2])
    taps, bias_col, *halves = lax.optimization_barrier((taps, bias_col, *halves))

    partial = [forward(taps, blocks, side_rows, n_sp, j) for j in range(n_sp)]
    other = [lax.ppermute(value, "in", swap) for value in partial]

    own_grad, *rows = silu(partial[0], other[0], bias_col, cotangent, n_filt)
    pieces = rows[:1]
    for k in range(1, n_filt):
        pieces.append(lax.ppermute(rows[k], "filt", shifted_ring("filt", k)))
    sums = own_gradient(own_grad, blocks, n_sp)
    for j in range(1, n_sp):
        side = [partial[j], other[j], *halves[2 * j - 2 : 2 * j]]
        last = pieces if j == n_sp - 1 else []
        sums = add_gradient(j, bias_col, side, sums, blocks, last, n_sp)
    output, grad_weight, grad_bias = sums
    return (output, grad_weight, grad_bias.reshape(-1))


def solution(mesh):
    placed = (
        P(("groups", "sp", "filt"), None, "in"),
        P(None, None, "filt", None),
        P("filt"),
        P(("groups", "sp"), "filt", None),
    )
    return jax.shard_map(
        on_device,
        mesh=mesh,
        in_specs=placed,
        out_specs=(
            P(("groups", "sp", "filt"), None, "in"),
            P("groups", None, "filt", "in"),
            P(("groups", "filt")),
        ),
        check_vma=False,
    )
```

```python
import functools
import math

import jax
import jax.numpy as jnp
from jax import lax
from jax.experimental import pallas as pl
from jax.experimental.pallas import tpu as pltpu
from jax.sharding import PartitionSpec as P

MIB = 1024 * 1024


def params(*arrays):
    held = sum(math.prod(shape) * size for shape, size in arrays)
    return pltpu.CompilerParams(vmem_limit_bytes=max(20 * MIB, held * 5 // 4 + 8 * MIB))


def shifted_ring(axis, shift):
    size = lax.axis_size(axis)
    return [(i, (i + shift) % size) for i in range(size)]


def folded_ring(axis, shift):
    size = lax.axis_size(axis)
    order = [0, *range(1, size, 2), *reversed(range(2, size, 2))]
    return [(order[i], order[(i + shift) % size]) for i in range(size)]


def folded_behind(axis, size, by):
    index = lax.axis_index(axis)
    back = size - lax.div(index, 2)
    place = jnp.where(lax.rem(index, 2) == 1, lax.div(index + 1, 2), lax.rem(back, size))
    place = lax.rem(place + (size - by), size)
    out = 2 * place - 1
    return jnp.where(place == 0, 0, jnp.where(place <= size // 2, out, 2 * (size - place)))


def gather_blocks(image):
    n_filt, n_sp = lax.axis_size("filt"), lax.axis_size("sp")
    blocks = [[None] * n_filt for _ in range(n_sp)]
    blocks[0][0] = image
    for k in range(n_filt):
        if k:
            blocks[0][k] = lax.ppermute(blocks[0][k - 1], "filt", folded_ring("filt", 1))
        for j in range(1, n_sp):
            if k and k == n_filt - 1:
                blocks[j][k] = lax.ppermute(blocks[j][0], "filt", folded_ring("filt", -1))
            else:
                blocks[j][k] = lax.ppermute(blocks[j - 1][k], "sp", shifted_ring("sp", 1))
    return blocks


def move_columns(values, by):
    size = values.shape[1]
    column = lax.broadcasted_iota(jnp.int32, values.shape, 1)
    edge = 0 if by == 1 else size - 1
    return jnp.where(column == edge, 0.0, pltpu.roll(values, by % size, 1))


VMEM = pl.BlockSpec(memory_space=pltpu.VMEM)
ANY = pl.BlockSpec(memory_space=pl.ANY)


def behind(axis, size, by):
    return lax.rem(lax.axis_index(axis) + (size - by), size)


def half_kernel(cotangent, _, out, sem):
    rows = out.shape[0]
    copy = pltpu.make_async_copy(
        cotangent.at[pl.ds(lax.axis_index("in") * rows, rows)], out, sem
    )
    copy.start()
    copy.wait()


def own_half(cotangent, after):
    shape = (cotangent.shape[0] // 2,) + cotangent.shape[1:]
    return pl.pallas_call(
        half_kernel,
        out_shape=jax.ShapeDtypeStruct(shape, cotangent.dtype),
        in_specs=[ANY, ANY],
        out_specs=VMEM,
        scratch_shapes=[pltpu.SemaphoreType.DMA],
        compiler_params=params((shape, 2)),
        cost_estimate=pl.CostEstimate(
            flops=0, bytes_accessed=4 * math.prod(shape), transcendentals=0
        ),
    )(cotangent, after)


def arrange_kernel(weight, bias, taps, bias_col, sems):
    depth = taps.shape[1]
    own = weight.shape[2]
    half = lax.axis_index("in")
    copies = [
        pltpu.make_async_copy(
            weight.at[a, b, :, pl.ds(pl.multiple_of(half * depth, depth), depth)],
            taps.at[pl.ds((a * 3 + b) * own, own), :],
            sems.at[a * 3 + b],
        )
        for a in range(3)
        for b in range(3)
    ]
    for copy in copies:
        copy.start()
    bias_col[...] = jnp.broadcast_to(bias[...], (128, own)).T[:, :1]
    for copy in copies:
        copy.wait()


def arrange(weight, bias, depth):
    own = weight.shape[2]
    shape = (9 * own, depth)
    return pl.pallas_call(
        arrange_kernel,
        out_shape=(
            jax.ShapeDtypeStruct(shape, weight.dtype),
            jax.ShapeDtypeStruct((own, 1), bias.dtype),
        ),
        in_specs=[ANY, VMEM],
        out_specs=(VMEM, VMEM),
        scratch_shapes=[pltpu.SemaphoreType.DMA((9,))],
        compiler_params=params((shape, 2)),
        cost_estimate=pl.CostEstimate(
            flops=0, bytes_accessed=36 * own * depth, transcendentals=0
        ),
    )(weight, bias.reshape(1, own))


def block_place(index, n_filt, n_sp):
    j, k = divmod(index, n_filt)
    return behind("sp", n_sp, j) * n_filt + folded_behind("filt", n_filt, k)


def join_columns(product, own):
    return (
        product[own : 2 * own]
        + move_columns(product[:own], 1)
        + move_columns(product[2 * own :], -1)
    )


def add_row(total, slot, taps, row, turned):
    own = taps.shape[0] // 9
    turned[...] = row.T
    product = jnp.dot(taps[...], turned[...], preferred_element_type=jnp.float32)
    for a in range(3):
        total[slot + 1 - a] += join_columns(product[3 * a * own : 3 * (a + 1) * own], own)


def early_kernel(n_filt, n_sp, places, taps, *refs):
    *blocks, total, turned = refs
    rows_dev = blocks[0].shape[0]
    total[...] = jnp.zeros(total.shape, total.dtype)
    for index, block in enumerate(blocks):
        j, k = divmod(index, places)
        place = block_place(j * n_filt + k, n_filt, n_sp)
        for i in range(rows_dev):
            at = index * rows_dev + i
            add_row(total, place * rows_dev + i + 1, taps, block[i], turned.at[at])


def early(taps, sides, places, side_rows):
    n_sp, n_filt = len(sides), len(sides[0])
    blocks = [block for side in sides for block in side[:places]]
    rows_dev, width, depth = blocks[0].shape
    own = taps.shape[0] // 9
    shape = (n_sp * side_rows + 2, own, width)
    turned = (len(blocks) * rows_dev, depth, width)
    return pl.pallas_call(
        functools.partial(early_kernel, n_filt, n_sp, places),
        out_shape=jax.ShapeDtypeStruct(shape, jnp.float32),
        in_specs=[VMEM] * (1 + len(blocks)),
        out_specs=VMEM,
        scratch_shapes=[pltpu.VMEM(turned, blocks[0].dtype)],
        compiler_params=params((turned, 4), (shape, 4), (taps.shape, 6)),
        cost_estimate=pl.CostEstimate(
            flops=18 * len(blocks) * rows_dev * own * width * depth,
            bytes_accessed=18 * own * depth,
            transcendentals=0,
        ),
    )(taps, *blocks)


def late_kernel(n_filt, n_sp, j, places, n_riders, taps, begun, *refs):
    riders, refs = refs[:n_riders], refs[n_riders:]
    *blocks, out, total, turned = refs
    rows_dev = blocks[0].shape[0]
    side_rows, own = total.shape[0] - 2, total.shape[1]
    side = behind("sp", n_sp, j)
    total[...] = begun[pl.ds(side * side_rows, side_rows + 2)]
    count = n_filt - places

    def slot_of(index):
        place = block_place(index // count * n_filt + places + index % count, n_filt, n_sp)
        return place * rows_dev - side * side_rows + 1

    for index in range(j * count, (j + 1) * count):
        for i in range(rows_dev):
            at = index % count * rows_dev + i
            add_row(total, slot_of(index) + i, taps, blocks[index][i], turned.at[at])

    for index, block in enumerate(blocks):
        if index // count == j:
            continue
        for i, at, edge, a in ((rows_dev - 1, 0, 1, 0), (0, side_rows + 1, side_rows, 2)):

            @pl.when(slot_of(index) + i == at)
            def _():
                turned[0] = block[i].T
                rows = taps[pl.ds(3 * a * own, 3 * own), :]
                product = jnp.dot(rows, turned[0], preferred_element_type=jnp.float32)
                total[edge] += join_columns(product, own)

    out[pl.ds(0, side_rows)] = total[pl.ds(1, side_rows)]
    for index, rider in enumerate(riders):
        rows = rider.shape[0]
        out[pl.ds(side_rows + index * rows, rows)] = rider[...].astype(out.dtype)


def late(taps, begun, sides, j, places, side_rows, riders=()):
    n_sp, n_filt = len(sides), len(sides[0])
    blocks = [block for side in sides for block in side[places:]]
    rows_dev, width, depth = blocks[0].shape
    own = taps.shape[0] // 9
    out = (side_rows + sum(rider.shape[0] for rider in riders), own, width)
    total = (side_rows + 2, own, width)
    turned = ((n_filt - places) * rows_dev, depth, width)
    return pl.pallas_call(
        functools.partial(late_kernel, n_filt, n_sp, j, places, len(riders)),
        out_shape=jax.ShapeDtypeStruct(out, jnp.float32),
        in_specs=[VMEM] * (2 + len(riders) + len(blocks)),
        out_specs=VMEM,
        scratch_shapes=[
            pltpu.VMEM(total, jnp.float32),
            pltpu.VMEM(turned, blocks[0].dtype),
        ],
        compiler_params=params((turned, 2 + 2 * n_sp), (total, 12), (begun.shape, 4), (taps.shape, 6)),
        cost_estimate=pl.CostEstimate(
            flops=18 * (n_filt - places) * rows_dev * own * width * depth,
            bytes_accessed=18 * own * depth,
            transcendentals=0,
        ),
    )(taps, begun, *riders, *blocks)


def silu_parts(shifted, cotangent):
    sigmoid_v = 0.5 * jnp.tanh(0.5 * shifted) + 0.5
    slope = sigmoid_v * (1.0 + shifted * (1.0 - sigmoid_v))
    grad_out = (cotangent.astype(jnp.float32) * slope).astype(jnp.bfloat16)
    return sigmoid_v, grad_out


def silu_kernel(n_filt, mine, theirs, bias, cotangent, grad_out, *activated):
    rows, _, half = activated[0].shape

    for k in range(n_filt):
        first = behind("filt", n_filt, n_filt - k if k else 0) * rows

        @pl.loop(0, rows)
        def _(i):
            r = first + i
            shifted = (mine[r] + theirs[r]) + bias[...]
            sigmoid_v, grad_out[r] = silu_parts(shifted, cotangent[r])
            value = (shifted * sigmoid_v).astype(activated[k].dtype)
            activated[k][i] = jnp.where(
                lax.axis_index("in") == 0, value[:, :half], value[:, half:]
            )


def silu(mine, theirs, bias, cotangent, n_filt):
    rows, own, width = cotangent.shape
    return pl.pallas_call(
        functools.partial(silu_kernel, n_filt),
        out_shape=[jax.ShapeDtypeStruct((rows, own, width), jnp.bfloat16)]
        + [jax.ShapeDtypeStruct((rows // n_filt, own, width // 2), jnp.bfloat16)] * n_filt,
        in_specs=[VMEM] * 4,
        out_specs=[VMEM] * (1 + n_filt),
        compiler_params=params((cotangent.shape, 16)),
        cost_estimate=pl.CostEstimate(
            flops=10 * rows * own * width,
            bytes_accessed=13 * rows * own * width,
            transcendentals=rows * own * width,
        ),
    )(mine, theirs, bias, cotangent)


def shift_grads(grads, grad_out, row):
    own, width = grad_out.shape
    wide = grad_out.astype(jnp.float32)
    at = pl.ds(pl.multiple_of(row * width, width), width)
    grads[pl.ds(0, own), at] = move_columns(wide, -1).astype(grads.dtype)
    grads[pl.ds(own, own), at] = grad_out
    grads[pl.ds(2 * own, own), at] = move_columns(wide, 1).astype(grads.dtype)


def place_blocks(panel, blocks, n_sp, j, side_rows):
    rows_dev, width, depth = blocks[0].shape
    side = behind("sp", n_sp, j)
    zeros = jnp.zeros((width, depth), panel.dtype)

    @pl.when(side == 0)
    def _():
        panel[pl.ds(0, width), :] = zeros

    @pl.when(side == n_sp - 1)
    def _():
        panel[pl.ds((side_rows + 1) * width, width), :] = zeros

    for index, block in enumerate(blocks):
        for i in range(rows_dev):
            place = block_place(index, len(blocks) // n_sp, n_sp)
            slot = place * rows_dev + i - side * side_rows + 1

            @pl.when((slot >= 0) & (slot < side_rows + 2))
            def _():
                panel[pl.ds(pl.multiple_of(slot * width, width), width), :] = block[i]


def row_sums(grads):
    own = grads.shape[0] // 3
    ones = jnp.ones((16, grads.shape[1]), grads.dtype)
    sums = lax.dot_general(
        ones,
        grads[pl.ds(own, own), :],
        (((1,), (1,)), ((), ())),
        preferred_element_type=jnp.float32,
    )
    return sums[:1]


def tap_gradient(grads, panel, a, width):
    window = panel[pl.ds(pl.multiple_of(a * width, width), grads.shape[1]), :]
    product = jnp.dot(grads[...], window, preferred_element_type=jnp.float32)
    return product.reshape(3, grads.shape[0] // 3, panel.shape[1])


def own_gradient_kernel(n_sp, own_grad, *refs):
    blocks, (weight_sum, bias_sum, grads, panel) = refs[:-4], refs[-4:]
    side_rows, _, width = own_grad.shape
    place_blocks(panel, blocks, n_sp, 0, side_rows)

    for r in range(side_rows):
        shift_grads(grads, own_grad[r], r)

    bias_sum[...] = row_sums(grads)

    @pl.loop(0, 3)
    def _(a):
        weight_sum[a] = tap_gradient(grads, panel, a, width)


def add_gradient_kernel(n_sp, j, n_pieces, bias, mine, theirs, near, swapped, *refs):
    (weight_in, bias_in), refs = refs[:2], refs[2:]
    pieces, refs = refs[:n_pieces], refs[n_pieces:]
    if pieces:
        *refs, stage, sems, piece_sems = refs
    *blocks, weight_sum, bias_sum, grads, panel = refs
    if pieces:
        *blocks, output = blocks
    half_rows, own, width = near.shape
    side_rows = 2 * half_rows
    half = lax.axis_index("in")

    piece_copies = [
        pltpu.make_async_copy(
            piece,
            output.at[
                :, pl.ds(pl.multiple_of(behind("filt", n_pieces, k) * own, own), own), :
            ],
            piece_sems.at[k],
        )
        for k, piece in enumerate(pieces)
    ]
    for copy in piece_copies:
        copy.start()

    place_blocks(panel, blocks, n_sp, j, side_rows)
    far = swapped.at[pl.ds(side_rows + (j - 1) * half_rows, half_rows)]
    for h, cotangent in enumerate((near, far)):
        start = (half if h == 0 else 1 - half) * half_rows
        for r in range(half_rows):
            shifted = (mine[start + r] + theirs[start + r]) + bias[...]
            _, grad_out = silu_parts(shifted, cotangent[r])
            shift_grads(grads, grad_out, start + r)

    bias_sum[...] = bias_in[...] + row_sums(grads)

    def copy_out(a, b):
        return pltpu.make_async_copy(stage.at[a, b], weight_sum.at[a, b], sems.at[a, b])

    @pl.loop(0, 3)
    def _(a):
        product = tap_gradient(grads, panel, a, width)
        if pieces:
            for b in range(3):
                stage[a, b] = weight_in[a, b] + product[b]
                copy_out(a, b).start()
        else:
            weight_sum[a] = weight_in[a] + product

    if pieces:

        @pl.loop(0, 9)
        def _(i):
            copy_out(lax.div(i, 3), lax.rem(i, 3)).wait()

    for copy in piece_copies:
        copy.wait()


def gradient_call(kernel, operands, blocks, shape, first_out=(), specs=(VMEM, VMEM), scratch=()):
    side_rows, own, width = shape
    _, _, depth = blocks[0].shape
    grads = (3 * own, side_rows * width)
    panel = ((side_rows + 2) * width, depth)
    total = (3, 3, own, depth)
    held = math.prod((len(blocks),) + blocks[0].shape)
    return pl.pallas_call(
        kernel,
        out_shape=[
            *first_out,
            jax.ShapeDtypeStruct(total, jnp.float32),
            jax.ShapeDtypeStruct((1, own), jnp.float32),
        ],
        in_specs=[VMEM] * (len(operands) + len(blocks)),
        out_specs=list(specs),
        scratch_shapes=[
            pltpu.VMEM(grads, jnp.bfloat16),
            pltpu.VMEM(panel, blocks[0].dtype),
            *scratch,
        ],
        compiler_params=params((grads, 2), (panel, 2), (total, 8), (shape, 16), ((held,), 2)),
        cost_estimate=pl.CostEstimate(
            flops=18 * side_rows * own * width * depth,
            bytes_accessed=36 * own * depth + 2 * side_rows * width * depth,
            transcendentals=side_rows * own * width,
        ),
    )(*operands, *blocks)


def own_gradient(own_grad, blocks, n_sp):
    return gradient_call(
        functools.partial(own_gradient_kernel, n_sp), [own_grad], blocks, own_grad.shape
    )


def add_gradient(j, bias, side, sums, blocks, pieces, n_sp):
    half_rows, own, width = side[2].shape
    shape = (2 * half_rows, own, width)
    rows_dev, _, depth = blocks[0].shape
    kernel = functools.partial(add_gradient_kernel, n_sp, j, len(pieces))
    operands = [bias, *side, *sums, *pieces]
    if not pieces:
        return gradient_call(kernel, operands, blocks, shape)
    rows = jax.ShapeDtypeStruct((rows_dev, len(pieces) * own, width // 2), pieces[0].dtype)
    scratch = [
        pltpu.VMEM((3, 3, own, depth), jnp.float32),
        pltpu.SemaphoreType.DMA((3, 3)),
        pltpu.SemaphoreType.DMA((len(pieces),)),
    ]
    return gradient_call(kernel, operands, blocks, shape, [rows], (ANY, ANY, VMEM), scratch)


def on_device(image, weight, bias, cotangent):
    n_filt, n_sp = lax.axis_size("filt"), lax.axis_size("sp")
    side_rows = cotangent.shape[0]
    swap = shifted_ring("in", 1)

    gathered = gather_blocks(image)
    blocks = [block for side in gathered for block in side]
    near = [own_half(cotangent, blocks[n_filt])]
    for _ in range(1, n_sp):
        near.append(lax.ppermute(near[-1], "sp", shifted_ring("sp", 1)))
    taps, bias_col = arrange(weight, bias, image.shape[2])

    places = n_filt // 2
    begun = early(taps, gathered, places, side_rows)
    partial = [late(taps, begun, gathered, 0, places, side_rows, near[1:])]
    for j in range(1, n_sp):
        partial.append(late(taps, begun, gathered, j, places, side_rows))
    other = [lax.ppermute(value, "in", swap) for value in partial]

    own_grad, *rows = silu(partial[0], other[0], bias_col, cotangent, n_filt)
    pieces = rows[:1]
    for k in range(1, n_filt):
        pieces.append(lax.ppermute(rows[k], "filt", shifted_ring("filt", k)))
    sums = own_gradient(own_grad, blocks, n_sp)
    for j in range(1, n_sp):
        side = [partial[j], other[j], near[j], other[0]]
        last = pieces if j == n_sp - 1 else []
        sums = add_gradient(j, bias_col, side, sums, blocks, last, n_sp)
    output, grad_weight, grad_bias = sums
    return (output, grad_weight, grad_bias.reshape(-1))


def solution(mesh):
    placed = (
        P(("groups", "sp", "filt"), None, "in"),
        P(None, None, "filt", None),
        P("filt"),
        P(("groups", "sp"), "filt", None),
    )
    return jax.shard_map(
        on_device,
        mesh=mesh,
        in_specs=placed,
        out_specs=(
            P(("groups", "sp", "filt"), None, "in"),
            P("groups", None, "filt", "in"),
            P(("groups", "filt")),
        ),
        check_vma=False,
    )
```

```python
import functools
import math

import jax
import jax.numpy as jnp
from jax import lax
from jax.experimental import pallas as pl
from jax.experimental.pallas import tpu as pltpu
from jax.sharding import PartitionSpec as P

MIB = 1024 * 1024


def params(*arrays):
    held = sum(math.prod(shape) * size for shape, size in arrays)
    return pltpu.CompilerParams(vmem_limit_bytes=max(20 * MIB, held * 5 // 4 + 8 * MIB))


def shifted_ring(axis, shift):
    size = lax.axis_size(axis)
    return [(i, (i + shift) % size) for i in range(size)]


def folded_ring(axis, shift):
    size = lax.axis_size(axis)
    order = [0, *range(1, size, 2), *reversed(range(2, size, 2))]
    return [(order[i], order[(i + shift) % size]) for i in range(size)]


def folded_behind(axis, size, by):
    index = lax.axis_index(axis)
    back = size - lax.div(index, 2)
    place = jnp.where(lax.rem(index, 2) == 1, lax.div(index + 1, 2), lax.rem(back, size))
    place = lax.rem(place + (size - by), size)
    out = 2 * place - 1
    return jnp.where(place == 0, 0, jnp.where(place <= size // 2, out, 2 * (size - place)))


def gather_blocks(image):
    n_filt, n_sp = lax.axis_size("filt"), lax.axis_size("sp")
    onward, outward = shifted_ring("sp", 1), folded_ring("filt", 1)
    blocks = [[None] * n_filt for _ in range(n_sp)]
    blocks[0][0] = image
    last = n_filt - 1
    for k in range(n_filt):
        if k:
            blocks[0][k] = lax.ppermute(blocks[0][k - 1], "filt", outward)
        for j in range(1, n_sp):
            if k < max(last, 1):
                blocks[j][k] = lax.ppermute(blocks[j - 1][k], "sp", onward)
    return blocks


def send_held(blocks, cotangent, after):
    n_filt, n_sp = len(blocks[0]), len(blocks)
    first = [side[0] for side in blocks[1:]]
    half, *first = hold(cotangent, first, after)
    halves = [half]
    for j in range(1, n_sp):
        if n_filt > 1:
            blocks[j][-1] = lax.ppermute(first[j - 1], "filt", folded_ring("filt", -1))
        halves.append(lax.ppermute(halves[-1], "sp", shifted_ring("sp", 1)))
    return halves


def move_columns(values, by):
    size = values.shape[1]
    column = lax.broadcasted_iota(jnp.int32, values.shape, 1)
    edge = 0 if by == 1 else size - 1
    return jnp.where(column == edge, jnp.zeros_like(values), pltpu.roll(values, by % size, 1))


VMEM = pl.BlockSpec(memory_space=pltpu.VMEM)
ANY = pl.BlockSpec(memory_space=pl.ANY)


def behind(axis, size, by):
    return lax.rem(lax.axis_index(axis) + (size - by), size)


def hold_kernel(n_blocks, n_after, cotangent, *refs):
    blocks, (half, *copies, sems) = refs[:n_blocks], refs[n_blocks + n_after :]
    rows = half.shape[0]
    moves = [(cotangent.at[pl.ds(lax.axis_index("in") * rows, rows)], half)]
    moves += zip(blocks, copies)
    moves = [pltpu.make_async_copy(*move, sems.at[i]) for i, move in enumerate(moves)]
    for move in moves:
        move.start()
    for move in moves:
        move.wait()


def hold(cotangent, blocks, after):
    shape = (cotangent.shape[0] // 2,) + cotangent.shape[1:]
    held = [jax.ShapeDtypeStruct(block.shape, block.dtype) for block in blocks]
    return pl.pallas_call(
        functools.partial(hold_kernel, len(blocks), len(after)),
        out_shape=[jax.ShapeDtypeStruct(shape, cotangent.dtype), *held],
        in_specs=[ANY] * (1 + len(blocks) + len(after)),
        out_specs=[VMEM] * (1 + len(blocks)),
        scratch_shapes=[pltpu.SemaphoreType.DMA((1 + len(blocks),))],
        compiler_params=params((shape, 2), *((block.shape, 2) for block in blocks)),
        cost_estimate=pl.CostEstimate(
            flops=0, bytes_accessed=4 * math.prod(shape), transcendentals=0
        ),
    )(cotangent, *blocks, *after)


def arrange_kernel(weight, bias, *refs):
    taps, bias_col, sems = refs[-3:]
    depth = taps.shape[1] // 3
    own = weight.shape[2]
    half = lax.axis_index("in")
    copies = [
        pltpu.make_async_copy(
            weight.at[a, b, :, pl.ds(pl.multiple_of(half * depth, depth), depth)],
            taps.at[pl.ds(a * own, own), pl.ds(b * depth, depth)],
            sems.at[a * 3 + b],
        )
        for a in range(3)
        for b in range(3)
    ]
    for copy in copies:
        copy.start()
    bias_col[...] = jnp.broadcast_to(bias[...], (128, own)).T[:, :1]
    for copy in copies:
        copy.wait()


def arrange(weight, bias, depth, after):
    own = weight.shape[2]
    shape = (3 * own, 3 * depth)
    return pl.pallas_call(
        arrange_kernel,
        out_shape=(
            jax.ShapeDtypeStruct(shape, weight.dtype),
            jax.ShapeDtypeStruct((own, 1), bias.dtype),
        ),
        in_specs=[ANY, VMEM] + [ANY] * len(after),
        out_specs=(VMEM, VMEM),
        scratch_shapes=[pltpu.SemaphoreType.DMA((9,))],
        compiler_params=params((shape, 2)),
        cost_estimate=pl.CostEstimate(
            flops=0, bytes_accessed=36 * own * depth, transcendentals=0
        ),
    )(weight, bias.reshape(1, own), *after)


def block_place(index, n_filt, n_sp):
    j, k = divmod(index, n_filt)
    return behind("sp", n_sp, j) * n_filt + folded_behind("filt", n_filt, k)


def turn_row(turned, row):
    values = row.T
    depth = values.shape[0]
    turned[pl.ds(0, depth), :] = move_columns(values, 1)
    turned[pl.ds(depth, depth), :] = values
    turned[pl.ds(2 * depth, depth), :] = move_columns(values, -1)


def add_row(total, slot, taps, row, turned):
    own = taps.shape[0] // 3
    turn_row(turned, row)
    product = jnp.dot(taps[...], turned[...], preferred_element_type=jnp.float32)
    for a in range(3):
        total[slot + 1 - a] += product[a * own : (a + 1) * own]


def add_blocks_kernel(where, n_filt, n_sp, fresh, taps, *refs):
    *blocks, total, turned = refs if fresh else refs[1:]
    rows_dev = blocks[0].shape[0]
    total[...] = jnp.zeros(total.shape, total.dtype) if fresh else refs[0][...]
    for index, (block, (j, k)) in enumerate(zip(blocks, where)):
        place = block_place(j * n_filt + k, n_filt, n_sp)
        for i in range(rows_dev):
            at = index * rows_dev + i
            add_row(total, place * rows_dev + i + 1, taps, block[i], turned.at[at])


def add_blocks(taps, sides, where, side_rows, begun=()):
    n_sp, n_filt = len(sides), len(sides[0])
    blocks = [sides[j][k] for j, k in where]
    rows_dev, width, depth = blocks[0].shape
    own = taps.shape[0] // 3
    shape = (n_sp * side_rows + 2, own, width)
    turned = (len(blocks) * rows_dev, 3 * depth, width)
    return pl.pallas_call(
        functools.partial(add_blocks_kernel, where, n_filt, n_sp, not begun),
        out_shape=jax.ShapeDtypeStruct(shape, jnp.float32),
        in_specs=[VMEM] * (1 + len(begun) + len(blocks)),
        out_specs=VMEM,
        scratch_shapes=[pltpu.VMEM(turned, blocks[0].dtype)],
        compiler_params=params((turned, 2), (shape, 8), (taps.shape, 4)),
        cost_estimate=pl.CostEstimate(
            flops=18 * len(blocks) * rows_dev * own * width * depth,
            bytes_accessed=18 * own * depth,
            transcendentals=0,
        ),
    )(taps, *begun, *blocks)


def last_rows_kernel(n_filt, n_sp, j, n_riders, taps, begun, *refs):
    riders, refs = refs[:n_riders], refs[n_riders:]
    *blocks, out, total, turned = refs
    rows_dev = blocks[0].shape[0]
    side_rows, own = total.shape[0] - 2, total.shape[1]
    side = behind("sp", n_sp, j)
    total[...] = begun[pl.ds(side * side_rows, side_rows + 2)]

    def slot_of(other):
        place = block_place(other * n_filt + n_filt - 1, n_filt, n_sp)
        return place * rows_dev - side * side_rows + 1

    for other, block in enumerate(blocks, 1):
        for i in range(rows_dev):
            if other == j:
                add_row(total, slot_of(other) + i, taps, block[i], turned.at[i])
        if other != j:
            for i, at, edge, a in ((rows_dev - 1, 0, 1, 0), (0, side_rows + 1, side_rows, 2)):

                @pl.when(slot_of(other) + i == at)
                def _():
                    turn_row(turned.at[0], block[i])
                    rows = taps[pl.ds(a * own, own), :]
                    product = jnp.dot(rows, turned[0], preferred_element_type=jnp.float32)
                    total[edge] += product

    out[pl.ds(0, side_rows)] = total[pl.ds(1, side_rows)]
    for index, rider in enumerate(riders):
        rows = rider.shape[0]
        out[pl.ds(side_rows + index * rows, rows)] = rider[...].astype(out.dtype)


def last_rows(taps, begun, sides, j, side_rows, riders=()):
    n_sp, n_filt = len(sides), len(sides[0])
    blocks = [side[-1] for side in sides[1:]]
    rows_dev, width, depth = blocks[0].shape
    own = taps.shape[0] // 3
    out = (side_rows + sum(rider.shape[0] for rider in riders), own, width)
    total = (side_rows + 2, own, width)
    turned = (rows_dev, 3 * depth, width)
    return pl.pallas_call(
        functools.partial(last_rows_kernel, n_filt, n_sp, j, len(riders)),
        out_shape=jax.ShapeDtypeStruct(out, jnp.float32),
        in_specs=[VMEM] * (2 + len(riders) + len(blocks)),
        out_specs=VMEM,
        scratch_shapes=[
            pltpu.VMEM(total, jnp.float32),
            pltpu.VMEM(turned, blocks[0].dtype),
        ],
        compiler_params=params(
            (turned, 2 + n_sp), (total, 12), (begun.shape, 4), (taps.shape, 4)
        ),
        cost_estimate=pl.CostEstimate(
            flops=18 * rows_dev * own * width * depth,
            bytes_accessed=18 * own * depth,
            transcendentals=0,
        ),
    )(taps, begun, *riders, *blocks)


def silu_parts(shifted, cotangent):
    sigmoid_v = 0.5 * jnp.tanh(0.5 * shifted) + 0.5
    slope = sigmoid_v * (1.0 + shifted * (1.0 - sigmoid_v))
    grad_out = (cotangent.astype(jnp.float32) * slope).astype(jnp.bfloat16)
    return sigmoid_v, grad_out


def silu_kernel(n_filt, mine, theirs, bias, cotangent, grad_out, *activated):
    rows, _, half = activated[0].shape

    for k in range(n_filt):
        first = behind("filt", n_filt, n_filt - k if k else 0) * rows

        @pl.loop(0, rows)
        def _(i):
            r = first + i
            shifted = (mine[r] + theirs[r]) + bias[...]
            sigmoid_v, grad_out[r] = silu_parts(shifted, cotangent[r])
            value = (shifted * sigmoid_v).astype(activated[k].dtype)
            activated[k][i] = jnp.where(
                lax.axis_index("in") == 0, value[:, :half], value[:, half:]
            )


def silu(mine, theirs, bias, cotangent, n_filt):
    rows, own, width = cotangent.shape
    return pl.pallas_call(
        functools.partial(silu_kernel, n_filt),
        out_shape=[jax.ShapeDtypeStruct((rows, own, width), jnp.bfloat16)]
        + [jax.ShapeDtypeStruct((rows // n_filt, own, width // 2), jnp.bfloat16)] * n_filt,
        in_specs=[VMEM] * 4,
        out_specs=[VMEM] * (1 + n_filt),
        compiler_params=params((cotangent.shape, 16)),
        cost_estimate=pl.CostEstimate(
            flops=10 * rows * own * width,
            bytes_accessed=13 * rows * own * width,
            transcendentals=rows * own * width,
        ),
    )(mine, theirs, bias, cotangent)


def shift_grads(grads, grad_out, row):
    own, width = grad_out.shape
    at = pl.ds(pl.multiple_of(row * width, width), width)
    grads[pl.ds(0, own), at] = move_columns(grad_out, -1)
    grads[pl.ds(own, own), at] = grad_out
    grads[pl.ds(2 * own, own), at] = move_columns(grad_out, 1)


def place_blocks(panel, blocks, n_sp, j, side_rows):
    rows_dev, width, depth = blocks[0].shape
    side = behind("sp", n_sp, j)
    zeros = jnp.zeros((width, depth), panel.dtype)

    @pl.when(side == 0)
    def _():
        panel[pl.ds(0, width), :] = zeros

    @pl.when(side == n_sp - 1)
    def _():
        panel[pl.ds((side_rows + 1) * width, width), :] = zeros

    for index, block in enumerate(blocks):
        for i in range(rows_dev):
            place = block_place(index, len(blocks) // n_sp, n_sp)
            slot = place * rows_dev + i - side * side_rows + 1

            @pl.when((slot >= 0) & (slot < side_rows + 2))
            def _():
                panel[pl.ds(pl.multiple_of(slot * width, width), width), :] = block[i]


def row_sums(grads):
    own = grads.shape[0] // 3
    ones = jnp.ones((16, grads.shape[1]), grads.dtype)
    sums = lax.dot_general(
        ones,
        grads[pl.ds(own, own), :],
        (((1,), (1,)), ((), ())),
        preferred_element_type=jnp.float32,
    )
    return sums[:1]


def tap_gradient(grads, panel, a, width):
    window = panel[pl.ds(pl.multiple_of(a * width, width), grads.shape[1]), :]
    product = jnp.dot(grads[...], window, preferred_element_type=jnp.float32)
    return product.reshape(3, grads.shape[0] // 3, panel.shape[1])


def own_gradient_kernel(n_sp, own_grad, *refs):
    blocks, (weight_sum, bias_sum, grads, panel) = refs[:-4], refs[-4:]
    side_rows, _, width = own_grad.shape
    place_blocks(panel, blocks, n_sp, 0, side_rows)

    for r in range(side_rows):
        shift_grads(grads, own_grad[r], r)

    bias_sum[...] = row_sums(grads)

    @pl.loop(0, 3)
    def _(a):
        weight_sum[a] = tap_gradient(grads, panel, a, width)


def add_gradient_kernel(n_sp, j, n_pieces, bias, mine, theirs, near, swapped, *refs):
    (weight_in, bias_in), refs = refs[:2], refs[2:]
    pieces, refs = refs[:n_pieces], refs[n_pieces:]
    if pieces:
        *refs, stage, sems, piece_sems = refs
    *blocks, weight_sum, bias_sum, grads, panel = refs
    if pieces:
        *blocks, output = blocks
    half_rows, own, width = near.shape
    side_rows = 2 * half_rows
    half = lax.axis_index("in")

    piece_copies = [
        pltpu.make_async_copy(
            piece,
            output.at[
                :, pl.ds(pl.multiple_of(behind("filt", n_pieces, k) * own, own), own), :
            ],
            piece_sems.at[k],
        )
        for k, piece in enumerate(pieces)
    ]
    for copy in piece_copies:
        copy.start()

    place_blocks(panel, blocks, n_sp, j, side_rows)
    far = swapped.at[pl.ds(side_rows + (j - 1) * half_rows, half_rows)]
    for h, cotangent in enumerate((near, far)):
        start = (half if h == 0 else 1 - half) * half_rows
        for r in range(half_rows):
            shifted = (mine[start + r] + theirs[start + r]) + bias[...]
            _, grad_out = silu_parts(shifted, cotangent[r])
            shift_grads(grads, grad_out, start + r)

    bias_sum[...] = bias_in[...] + row_sums(grads)

    def copy_out(a, b):
        return pltpu.make_async_copy(stage.at[a, b], weight_sum.at[a, b], sems.at[a, b])

    @pl.loop(0, 3)
    def _(a):
        product = tap_gradient(grads, panel, a, width)
        if pieces:
            for b in range(3):
                stage[a, b] = weight_in[a, b] + product[b]
                copy_out(a, b).start()
        else:
            weight_sum[a] = weight_in[a] + product

    if pieces:

        @pl.loop(0, 9)
        def _(i):
            copy_out(lax.div(i, 3), lax.rem(i, 3)).wait()

    for copy in piece_copies:
        copy.wait()


def gradient_call(kernel, operands, blocks, shape, first_out=(), specs=(VMEM, VMEM), scratch=()):
    side_rows, own, width = shape
    _, _, depth = blocks[0].shape
    grads = (3 * own, side_rows * width)
    panel = ((side_rows + 2) * width, depth)
    total = (3, 3, own, depth)
    held = math.prod((len(blocks),) + blocks[0].shape)
    return pl.pallas_call(
        kernel,
        out_shape=[
            *first_out,
            jax.ShapeDtypeStruct(total, jnp.float32),
            jax.ShapeDtypeStruct((1, own), jnp.float32),
        ],
        in_specs=[VMEM] * (len(operands) + len(blocks)),
        out_specs=list(specs),
        scratch_shapes=[
            pltpu.VMEM(grads, jnp.bfloat16),
            pltpu.VMEM(panel, blocks[0].dtype),
            *scratch,
        ],
        compiler_params=params((grads, 2), (panel, 2), (total, 8), (shape, 16), ((held,), 2)),
        cost_estimate=pl.CostEstimate(
            flops=18 * side_rows * own * width * depth,
            bytes_accessed=36 * own * depth + 2 * side_rows * width * depth,
            transcendentals=side_rows * own * width,
        ),
    )(*operands, *blocks)


def own_gradient(own_grad, blocks, n_sp):
    return gradient_call(
        functools.partial(own_gradient_kernel, n_sp), [own_grad], blocks, own_grad.shape
    )


def add_gradient(j, bias, side, sums, blocks, pieces, n_sp):
    half_rows, own, width = side[2].shape
    shape = (2 * half_rows, own, width)
    rows_dev, _, depth = blocks[0].shape
    kernel = functools.partial(add_gradient_kernel, n_sp, j, len(pieces))
    operands = [bias, *side, *sums, *pieces]
    if not pieces:
        return gradient_call(kernel, operands, blocks, shape)
    rows = jax.ShapeDtypeStruct((rows_dev, len(pieces) * own, width // 2), pieces[0].dtype)
    scratch = [
        pltpu.VMEM((3, 3, own, depth), jnp.float32),
        pltpu.SemaphoreType.DMA((3, 3)),
        pltpu.SemaphoreType.DMA((len(pieces),)),
    ]
    return gradient_call(kernel, operands, blocks, shape, [rows], (ANY, ANY, VMEM), scratch)


def on_device(image, weight, bias, cotangent):
    n_filt, n_sp = lax.axis_size("filt"), lax.axis_size("sp")
    side_rows = cotangent.shape[0]
    swap = shifted_ring("in", 1)

    gathered = gather_blocks(image)
    taps, bias_col = arrange(weight, bias, image.shape[2], [gathered[-1][0]])
    places = [[(j, k) for j in range(n_sp)] for k in range(n_filt)]
    first, second = places[: n_filt // 2], places[n_filt // 2 :]
    second[-1] = [(0, n_filt - 1)]
    begun = add_blocks(taps, gathered, sum(first, []), side_rows)
    near = send_held(gathered, cotangent, [begun])
    begun = add_blocks(taps, gathered, sum(second, []), side_rows, [begun])
    blocks = [block for side in gathered for block in side]

    partial = [last_rows(taps, begun, gathered, 0, side_rows, near[1:])]
    for j in range(1, n_sp):
        partial.append(last_rows(taps, begun, gathered, j, side_rows))
    other = [lax.ppermute(value, "in", swap) for value in partial]

    own_grad, *rows = silu(partial[0], other[0], bias_col, cotangent, n_filt)
    pieces = rows[:1]
    for k in range(1, n_filt):
        pieces.append(lax.ppermute(rows[k], "filt", shifted_ring("filt", k)))
    sums = own_gradient(own_grad, blocks, n_sp)
    for j in range(1, n_sp):
        side = [partial[j], other[j], near[j], other[0]]
        last = pieces if j == n_sp - 1 else []
        sums = add_gradient(j, bias_col, side, sums, blocks, last, n_sp)
    output, grad_weight, grad_bias = sums
    return (output, grad_weight, grad_bias.reshape(-1))


def solution(mesh):
    placed = (
        P(("groups", "sp", "filt"), None, "in"),
        P(None, None, "filt", None),
        P("filt"),
        P(("groups", "sp"), "filt", None),
    )
    return jax.shard_map(
        on_device,
        mesh=mesh,
        in_specs=placed,
        out_specs=(
            P(("groups", "sp", "filt"), None, "in"),
            P("groups", None, "filt", "in"),
            P(("groups", "filt")),
        ),
        check_vma=False,
    )
```

```python
import functools
import math

import jax
import jax.numpy as jnp
from jax import lax
from jax.experimental import pallas as pl
from jax.experimental.pallas import tpu as pltpu
from jax.sharding import PartitionSpec as P

MIB = 1024 * 1024


def params(*arrays):
    held = sum(math.prod(shape) * size for shape, size in arrays)
    return pltpu.CompilerParams(vmem_limit_bytes=max(20 * MIB, held * 5 // 4 + 8 * MIB))


def shifted_ring(axis, shift):
    size = lax.axis_size(axis)
    return [(i, (i + shift) % size) for i in range(size)]


def folded_ring(axis, shift):
    size = lax.axis_size(axis)
    order = [0, *range(1, size, 2), *reversed(range(2, size, 2))]
    return [(order[i], order[(i + shift) % size]) for i in range(size)]


def folded_behind(axis, size, by):
    index = lax.axis_index(axis)
    back = size - lax.div(index, 2)
    place = jnp.where(lax.rem(index, 2) == 1, lax.div(index + 1, 2), lax.rem(back, size))
    place = lax.rem(place + (size - by), size)
    out = 2 * place - 1
    return jnp.where(place == 0, 0, jnp.where(place <= size // 2, out, 2 * (size - place)))


def gather_blocks(image):
    n_filt, n_sp = lax.axis_size("filt"), lax.axis_size("sp")
    onward, outward = shifted_ring("sp", 1), folded_ring("filt", 1)
    blocks = [[None] * n_filt for _ in range(n_sp)]
    blocks[0][0] = image
    last = n_filt - 1
    for k in range(n_filt):
        if k:
            blocks[0][k] = lax.ppermute(blocks[0][k - 1], "filt", outward)
        for j in range(1, n_sp):
            if k < max(last, 1):
                blocks[j][k] = lax.ppermute(blocks[j - 1][k], "sp", onward)
    return blocks


def send_held(blocks, cotangent, after):
    n_filt, n_sp = len(blocks[0]), len(blocks)
    first = [side[0] for side in blocks[1:]]
    half, *first = hold(cotangent, first, after)
    halves = [half]
    for j in range(1, n_sp):
        if n_filt > 1:
            blocks[j][-1] = lax.ppermute(first[j - 1], "filt", folded_ring("filt", -1))
        halves.append(lax.ppermute(halves[-1], "sp", shifted_ring("sp", 1)))
    return halves


def move_columns(values, by):
    size = values.shape[1]
    column = lax.broadcasted_iota(jnp.int32, values.shape, 1)
    edge = 0 if by == 1 else size - 1
    return jnp.where(column == edge, jnp.zeros_like(values), pltpu.roll(values, by % size, 1))


VMEM = pl.BlockSpec(memory_space=pltpu.VMEM)
ANY = pl.BlockSpec(memory_space=pl.ANY)


def behind(axis, size, by):
    return lax.rem(lax.axis_index(axis) + (size - by), size)


def hold_kernel(n_blocks, n_after, cotangent, *refs):
    blocks, (half, *copies, sems) = refs[:n_blocks], refs[n_blocks + n_after :]
    rows = half.shape[0]
    moves = [(cotangent.at[pl.ds(lax.axis_index("in") * rows, rows)], half)]
    moves += zip(blocks, copies)
    moves = [pltpu.make_async_copy(*move, sems.at[i]) for i, move in enumerate(moves)]
    for move in moves:
        move.start()
    for move in moves:
        move.wait()


def hold(cotangent, blocks, after):
    shape = (cotangent.shape[0] // 2,) + cotangent.shape[1:]
    held = [jax.ShapeDtypeStruct(block.shape, block.dtype) for block in blocks]
    return pl.pallas_call(
        functools.partial(hold_kernel, len(blocks), len(after)),
        out_shape=[jax.ShapeDtypeStruct(shape, cotangent.dtype), *held],
        in_specs=[ANY] * (1 + len(blocks) + len(after)),
        out_specs=[VMEM] * (1 + len(blocks)),
        scratch_shapes=[pltpu.SemaphoreType.DMA((1 + len(blocks),))],
        compiler_params=params((shape, 2), *((block.shape, 2) for block in blocks)),
        cost_estimate=pl.CostEstimate(
            flops=0, bytes_accessed=4 * math.prod(shape), transcendentals=0
        ),
    )(cotangent, *blocks, *after)


def arrange_kernel(weight, bias, *refs):
    taps, bias_col, sems = refs[-3:]
    depth = taps.shape[1] // 3
    own = weight.shape[2]
    half = lax.axis_index("in")
    copies = [
        pltpu.make_async_copy(
            weight.at[a, b, :, pl.ds(pl.multiple_of(half * depth, depth), depth)],
            taps.at[pl.ds(a * own, own), pl.ds(b * depth, depth)],
            sems.at[a * 3 + b],
        )
        for a in range(3)
        for b in range(3)
    ]
    for copy in copies:
        copy.start()
    bias_col[...] = jnp.broadcast_to(bias[...], (128, own)).T[:, :1]
    for copy in copies:
        copy.wait()


def arrange(weight, bias, depth, after):
    own = weight.shape[2]
    shape = (3 * own, 3 * depth)
    return pl.pallas_call(
        arrange_kernel,
        out_shape=(
            jax.ShapeDtypeStruct(shape, weight.dtype),
            jax.ShapeDtypeStruct((own, 1), bias.dtype),
        ),
        in_specs=[ANY, VMEM] + [ANY] * len(after),
        out_specs=(VMEM, VMEM),
        scratch_shapes=[pltpu.SemaphoreType.DMA((9,))],
        compiler_params=params((shape, 2)),
        cost_estimate=pl.CostEstimate(
            flops=0, bytes_accessed=36 * own * depth, transcendentals=0
        ),
    )(weight, bias.reshape(1, own), *after)


def block_place(index, n_filt, n_sp):
    j, k = divmod(index, n_filt)
    return behind("sp", n_sp, j) * n_filt + folded_behind("filt", n_filt, k)


def turn_row(turned, row):
    values = row.T
    depth = values.shape[0]
    turned[pl.ds(0, depth), :] = move_columns(values, 1)
    turned[pl.ds(depth, depth), :] = values
    turned[pl.ds(2 * depth, depth), :] = move_columns(values, -1)


def add_row(total, slot, taps, row, turned):
    own = taps.shape[0] // 3
    turn_row(turned, row)
    product = jnp.dot(taps[...], turned[...], preferred_element_type=jnp.float32)
    for a in range(3):
        total[slot + 1 - a] += product[a * own : (a + 1) * own]


def add_blocks_kernel(where, n_filt, n_sp, fresh, taps, *refs):
    *blocks, total, turned = refs if fresh else refs[1:]
    rows_dev = blocks[0].shape[0]
    total[...] = jnp.zeros(total.shape, total.dtype) if fresh else refs[0][...]
    for index, (block, (j, k)) in enumerate(zip(blocks, where)):
        place = block_place(j * n_filt + k, n_filt, n_sp)
        for i in range(rows_dev):
            at = index * rows_dev + i
            add_row(total, place * rows_dev + i + 1, taps, block[i], turned.at[at])


def add_blocks(taps, sides, where, side_rows, begun=()):
    n_sp, n_filt = len(sides), len(sides[0])
    blocks = [sides[j][k] for j, k in where]
    rows_dev, width, depth = blocks[0].shape
    own = taps.shape[0] // 3
    shape = (n_sp * side_rows + 2, own, width)
    turned = (len(blocks) * rows_dev, 3 * depth, width)
    return pl.pallas_call(
        functools.partial(add_blocks_kernel, where, n_filt, n_sp, not begun),
        out_shape=jax.ShapeDtypeStruct(shape, jnp.float32),
        in_specs=[VMEM] * (1 + len(begun) + len(blocks)),
        out_specs=VMEM,
        scratch_shapes=[pltpu.VMEM(turned, blocks[0].dtype)],
        compiler_params=params((turned, 2), (shape, 8), (taps.shape, 4)),
        cost_estimate=pl.CostEstimate(
            flops=30 * len(blocks) * rows_dev * own * width * depth,
            bytes_accessed=18 * own * depth,
            transcendentals=0,
        ),
    )(taps, *begun, *blocks)


def last_rows_kernel(n_filt, n_sp, j, n_riders, taps, begun, *refs):
    riders, refs = refs[:n_riders], refs[n_riders:]
    *blocks, out, total, turned = refs
    rows_dev = blocks[0].shape[0]
    side_rows, own = total.shape[0] - 2, total.shape[1]
    side = behind("sp", n_sp, j)
    total[...] = begun[pl.ds(side * side_rows, side_rows + 2)]

    def slot_of(other):
        place = block_place(other * n_filt + n_filt - 1, n_filt, n_sp)
        return place * rows_dev - side * side_rows + 1

    for other, block in enumerate(blocks, 1):
        for i in range(rows_dev):
            if other == j:
                add_row(total, slot_of(other) + i, taps, block[i], turned.at[i])
        if other != j:
            for i, at, edge, a in ((rows_dev - 1, 0, 1, 0), (0, side_rows + 1, side_rows, 2)):

                @pl.when(slot_of(other) + i == at)
                def _():
                    turn_row(turned.at[0], block[i])
                    rows = taps[pl.ds(a * own, own), :]
                    product = jnp.dot(rows, turned[0], preferred_element_type=jnp.float32)
                    total[edge] += product

    out[pl.ds(0, side_rows)] = total[pl.ds(1, side_rows)]
    for index, rider in enumerate(riders):
        rows = rider.shape[0]
        out[pl.ds(side_rows + index * rows, rows)] = rider[...].astype(out.dtype)


def last_rows(taps, begun, sides, j, side_rows, riders=()):
    n_sp, n_filt = len(sides), len(sides[0])
    blocks = [side[-1] for side in sides[1:]]
    rows_dev, width, depth = blocks[0].shape
    own = taps.shape[0] // 3
    out = (side_rows + sum(rider.shape[0] for rider in riders), own, width)
    total = (side_rows + 2, own, width)
    turned = (rows_dev, 3 * depth, width)
    return pl.pallas_call(
        functools.partial(last_rows_kernel, n_filt, n_sp, j, len(riders)),
        out_shape=jax.ShapeDtypeStruct(out, jnp.float32),
        in_specs=[VMEM] * (2 + len(riders) + len(blocks)),
        out_specs=VMEM,
        scratch_shapes=[
            pltpu.VMEM(total, jnp.float32),
            pltpu.VMEM(turned, blocks[0].dtype),
        ],
        compiler_params=params(
            (turned, 2 + n_sp), (total, 12), (begun.shape, 4), (taps.shape, 4)
        ),
        cost_estimate=pl.CostEstimate(
            flops=18 * rows_dev * own * width * depth,
            bytes_accessed=18 * own * depth,
            transcendentals=0,
        ),
    )(taps, begun, *riders, *blocks)


def silu_parts(shifted, cotangent):
    sigmoid_v = 0.5 * jnp.tanh(0.5 * shifted) + 0.5
    slope = sigmoid_v * (1.0 + shifted * (1.0 - sigmoid_v))
    grad_out = (cotangent.astype(jnp.float32) * slope).astype(jnp.bfloat16)
    return sigmoid_v, grad_out


def silu_kernel(n_filt, mine, theirs, bias, cotangent, grad_out, *activated):
    rows, _, half = activated[0].shape

    for k in range(n_filt):
        first = behind("filt", n_filt, n_filt - k if k else 0) * rows

        @pl.loop(0, rows)
        def _(i):
            r = first + i
            shifted = (mine[r] + theirs[r]) + bias[...]
            sigmoid_v, grad_out[r] = silu_parts(shifted, cotangent[r])
            value = (shifted * sigmoid_v).astype(activated[k].dtype)
            activated[k][i] = jnp.where(
                lax.axis_index("in") == 0, value[:, :half], value[:, half:]
            )


def silu(mine, theirs, bias, cotangent, n_filt):
    rows, own, width = cotangent.shape
    return pl.pallas_call(
        functools.partial(silu_kernel, n_filt),
        out_shape=[jax.ShapeDtypeStruct((rows, own, width), jnp.bfloat16)]
        + [jax.ShapeDtypeStruct((rows // n_filt, own, width // 2), jnp.bfloat16)] * n_filt,
        in_specs=[VMEM] * 4,
        out_specs=[VMEM] * (1 + n_filt),
        compiler_params=params((cotangent.shape, 16)),
        cost_estimate=pl.CostEstimate(
            flops=10 * rows * own * width,
            bytes_accessed=13 * rows * own * width,
            transcendentals=rows * own * width,
        ),
    )(mine, theirs, bias, cotangent)


def shift_grads(grads, grad_out, row):
    own, width = grad_out.shape
    at = pl.ds(pl.multiple_of(row * width, width), width)
    grads[pl.ds(0, own), at] = move_columns(grad_out, -1)
    grads[pl.ds(own, own), at] = grad_out
    grads[pl.ds(2 * own, own), at] = move_columns(grad_out, 1)


def panel_copies(panel, blocks, n_filt, n_sp, sems):
    rows_dev, width, _ = blocks[0].shape
    copies = []
    for index, block in enumerate(blocks):
        place = block_place(index, n_filt, n_sp)
        for i in range(rows_dev):
            at = pl.multiple_of((place * rows_dev + i + 1) * width, width)
            to = panel.at[pl.ds(at, width), :]
            copies.append(pltpu.make_async_copy(block.at[i], to, sems.at[index * rows_dev + i]))
    return copies


def gradient_kernel(n_filt, n_sp, bias, own_grad, swapped, *refs):
    others, refs = refs[: 3 * (n_sp - 1)], refs[3 * (n_sp - 1) :]
    *blocks, weight_sum, bias_sum, formed, grads, panel, stage, sems, row_sems = refs
    side_rows, own, width = own_grad.shape
    copies = panel_copies(panel, blocks, n_filt, n_sp, row_sems)
    for copy in copies:
        copy.start()
    zeros = jnp.zeros((width, panel.shape[1]), panel.dtype)
    panel[pl.ds(0, width), :] = zeros
    panel[pl.ds((n_sp * side_rows + 1) * width, width), :] = zeros
    half_rows = side_rows // 2
    half = lax.axis_index("in")
    first = lax.axis_index("sp") * side_rows
    for r in range(side_rows):
        shift_grads(grads, own_grad[r], first + r)
    for j in range(1, n_sp):
        mine, theirs, near = others[3 * (j - 1) : 3 * j]
        first = behind("sp", n_sp, j) * side_rows
        far = swapped.at[pl.ds(side_rows + (j - 1) * half_rows, half_rows)]
        for h, cotangent in enumerate((near, far)):
            start = (half if h == 0 else 1 - half) * half_rows
            for r in range(half_rows):
                shifted = (mine[start + r] + theirs[start + r]) + bias[...]
                _, grad_out = silu_parts(shifted, cotangent[r])
                shift_grads(grads, grad_out, first + start + r)

    ones = jnp.ones((16, grads.shape[1]), grads.dtype)
    sums = lax.dot_general(
        ones,
        grads[pl.ds(own, own), :],
        (((1,), (1,)), ((), ())),
        preferred_element_type=jnp.float32,
    )
    bias_sum[...] = sums[:1]
    formed[...] = jnp.zeros(formed.shape, formed.dtype)
    for copy in copies:
        copy.wait()

    def copy_out(a, b):
        return pltpu.make_async_copy(stage.at[a, b], weight_sum.at[a, b], sems.at[a, b])

    @pl.loop(0, 3)
    def _(a):
        window = panel[pl.ds(pl.multiple_of(a * width, width), grads.shape[1]), :]
        product = jnp.dot(grads[...], window, preferred_element_type=jnp.float32)
        for b in range(3):
            stage[a, b] = product[b * own : (b + 1) * own]
            copy_out(a, b).start()

    @pl.loop(0, 9)
    def _(i):
        copy_out(lax.div(i, 3), lax.rem(i, 3)).wait()


def gradient(bias, own_grad, swapped, others, sides):
    n_sp, n_filt = len(sides), len(sides[0])
    blocks = [block for side in sides for block in side]
    side_rows, own, width = own_grad.shape
    depth = blocks[0].shape[2]
    all_rows = n_sp * side_rows
    panel = ((all_rows + 2) * width, depth)
    grads = (3 * own, all_rows * width)
    total = (3, 3, own, depth)
    return pl.pallas_call(
        functools.partial(gradient_kernel, n_filt, n_sp),
        out_shape=[
            jax.ShapeDtypeStruct(total, jnp.float32),
            jax.ShapeDtypeStruct((1, own), jnp.float32),
            jax.ShapeDtypeStruct((8, 128), jnp.float32),
        ],
        in_specs=[VMEM] * (3 + len(others)) + [ANY] * len(blocks),
        out_specs=[ANY, VMEM, VMEM],
        scratch_shapes=[
            pltpu.VMEM(grads, jnp.bfloat16),
            pltpu.VMEM(panel, blocks[0].dtype),
            pltpu.VMEM(total, jnp.float32),
            pltpu.SemaphoreType.DMA((3, 3)),
            pltpu.SemaphoreType.DMA((all_rows,)),
        ],
        compiler_params=params(
            (grads, 2), (panel, 2), (total, 5), ((all_rows, own, width), 12)
        ),
        cost_estimate=pl.CostEstimate(
            flops=18 * all_rows * own * width * depth,
            bytes_accessed=36 * own * depth + 2 * all_rows * width * depth,
            transcendentals=all_rows * own * width,
        ),
    )(bias, own_grad, swapped, *others, *blocks)


def place_kernel(*refs):
    *pieces, _, output, sems = refs
    own = pieces[0].shape[1]
    copies = []
    for k, piece in enumerate(pieces):
        at = pl.multiple_of(behind("filt", len(pieces), k) * own, own)
        rows = output.at[:, pl.ds(at, own), :]
        copies.append(pltpu.make_async_copy(piece, rows, sems.at[k]))
    for copy in copies:
        copy.start()
    for copy in copies:
        copy.wait()


def place_pieces(pieces, after):
    rows, own, half = pieces[0].shape
    return pl.pallas_call(
        place_kernel,
        out_shape=jax.ShapeDtypeStruct((rows, len(pieces) * own, half), pieces[0].dtype),
        in_specs=[ANY] * (len(pieces) + 1),
        out_specs=ANY,
        scratch_shapes=[pltpu.SemaphoreType.DMA((len(pieces),))],
        cost_estimate=pl.CostEstimate(
            flops=0, bytes_accessed=4 * len(pieces) * rows * own * half, transcendentals=0
        ),
    )(*pieces, after)


def on_device(image, weight, bias, cotangent):
    n_filt, n_sp = lax.axis_size("filt"), lax.axis_size("sp")
    side_rows = cotangent.shape[0]
    swap = shifted_ring("in", 1)

    gathered = gather_blocks(image)
    taps, bias_col = arrange(weight, bias, image.shape[2], [gathered[-1][0]])
    places = [[(j, k) for j in range(n_sp)] for k in range(n_filt)]
    first, second = places[: n_filt // 2], places[n_filt // 2 :]
    second[-1] = [(0, n_filt - 1)]
    begun = add_blocks(taps, gathered, first[0], side_rows)
    near = send_held(gathered, cotangent, [begun, gathered[0][-2]])
    for group in (sum(first[1:], []), sum(second, [])):
        begun = add_blocks(taps, gathered, group, side_rows, [begun])

    partial = [last_rows(taps, begun, gathered, 0, side_rows, near[1:])]
    for j in range(1, n_sp):
        partial.append(last_rows(taps, begun, gathered, j, side_rows))
    other = [lax.ppermute(value, "in", swap) for value in partial]

    own_grad, *rows = silu(partial[0], other[0], bias_col, cotangent, n_filt)
    pieces = rows[:1]
    for k in range(1, n_filt):
        pieces.append(lax.ppermute(rows[k], "filt", shifted_ring("filt", k)))
    others = []
    for j in range(1, n_sp):
        others += [partial[j], other[j], near[j]]
    grad_weight, grad_bias, formed = gradient(
        bias_col, own_grad, other[0], others, gathered
    )
    output = place_pieces(pieces, formed)
    return (output, grad_weight, grad_bias.reshape(-1))


def solution(mesh):
    placed = (
        P(("groups", "sp", "filt"), None, "in"),
        P(None, None, "filt", None),
        P("filt"),
        P(("groups", "sp"), "filt", None),
    )
    return jax.shard_map(
        on_device,
        mesh=mesh,
        in_specs=placed,
        out_specs=(
            P(("groups", "sp", "filt"), None, "in"),
            P("groups", None, "filt", "in"),
            P(("groups", "filt")),
        ),
        check_vma=False,
    )
```

```python
import functools
import math

import jax
import jax.numpy as jnp
from jax import lax
from jax.experimental import pallas as pl
from jax.experimental.pallas import tpu as pltpu
from jax.sharding import PartitionSpec as P

MIB = 1024 * 1024


def params(*arrays):
    held = sum(math.prod(shape) * size for shape, size in arrays)
    return pltpu.CompilerParams(vmem_limit_bytes=max(20 * MIB, held * 5 // 4 + 8 * MIB))


def shifted_ring(axis, shift):
    size = lax.axis_size(axis)
    return [(i, (i + shift) % size) for i in range(size)]


def folded_ring(axis, shift):
    size = lax.axis_size(axis)
    order = [0, *range(1, size, 2), *reversed(range(2, size, 2))]
    return [(order[i], order[(i + shift) % size]) for i in range(size)]


def folded_behind(axis, size, by):
    index = lax.axis_index(axis)
    back = size - lax.div(index, 2)
    place = jnp.where(lax.rem(index, 2) == 1, lax.div(index + 1, 2), lax.rem(back, size))
    place = lax.rem(place + (size - by), size)
    out = 2 * place - 1
    return jnp.where(place == 0, 0, jnp.where(place <= size // 2, out, 2 * (size - place)))


def gather_blocks(image):
    n_filt, n_sp = lax.axis_size("filt"), lax.axis_size("sp")
    onward, outward = shifted_ring("sp", 1), folded_ring("filt", 1)
    blocks = [[None] * n_filt for _ in range(n_sp)]
    blocks[0][0] = image
    last = n_filt - 1
    for k in range(n_filt):
        if k:
            blocks[0][k] = lax.ppermute(blocks[0][k - 1], "filt", outward)
        for j in range(1, n_sp):
            if k < max(last, 1):
                blocks[j][k] = lax.ppermute(blocks[j - 1][k], "sp", onward)
    return blocks


def send_held(blocks, cotangent, after):
    n_filt, n_sp = len(blocks[0]), len(blocks)
    first = [side[0] for side in blocks[1:]]
    half, *first = hold(cotangent, first, after)
    halves = [half]
    for j in range(1, n_sp):
        if n_filt > 1:
            blocks[j][-1] = lax.ppermute(first[j - 1], "filt", folded_ring("filt", -1))
        halves.append(lax.ppermute(halves[-1], "sp", shifted_ring("sp", 1)))
    return halves


def move_columns(values, by):
    size = values.shape[1]
    column = lax.broadcasted_iota(jnp.int32, values.shape, 1)
    edge = 0 if by == 1 else size - 1
    return jnp.where(column == edge, jnp.zeros_like(values), pltpu.roll(values, by % size, 1))


VMEM = pl.BlockSpec(memory_space=pltpu.VMEM)
ANY = pl.BlockSpec(memory_space=pl.ANY)


def behind(axis, size, by):
    return lax.rem(lax.axis_index(axis) + (size - by), size)


def hold_kernel(n_blocks, n_after, cotangent, *refs):
    blocks, (half, *copies, sems) = refs[:n_blocks], refs[n_blocks + n_after :]
    rows = half.shape[0]
    moves = [(cotangent.at[pl.ds(lax.axis_index("in") * rows, rows)], half)]
    moves += zip(blocks, copies)
    moves = [pltpu.make_async_copy(*move, sems.at[i]) for i, move in enumerate(moves)]
    for move in moves:
        move.start()
    for move in moves:
        move.wait()


def hold(cotangent, blocks, after):
    shape = (cotangent.shape[0] // 2,) + cotangent.shape[1:]
    held = [jax.ShapeDtypeStruct(block.shape, block.dtype) for block in blocks]
    return pl.pallas_call(
        functools.partial(hold_kernel, len(blocks), len(after)),
        out_shape=[jax.ShapeDtypeStruct(shape, cotangent.dtype), *held],
        in_specs=[ANY] * (1 + len(blocks) + len(after)),
        out_specs=[VMEM] * (1 + len(blocks)),
        scratch_shapes=[pltpu.SemaphoreType.DMA((1 + len(blocks),))],
        compiler_params=params((shape, 2), *((block.shape, 2) for block in blocks)),
        cost_estimate=pl.CostEstimate(
            flops=0, bytes_accessed=4 * math.prod(shape), transcendentals=0
        ),
    )(cotangent, *blocks, *after)


def arrange_kernel(weight, bias, *refs):
    taps, bias_col, sems = refs[-3:]
    depth = taps.shape[1] // 3
    own = weight.shape[2]
    half = lax.axis_index("in")
    copies = [
        pltpu.make_async_copy(
            weight.at[a, b, :, pl.ds(pl.multiple_of(half * depth, depth), depth)],
            taps.at[pl.ds(a * own, own), pl.ds(b * depth, depth)],
            sems.at[a * 3 + b],
        )
        for a in range(3)
        for b in range(3)
    ]
    for copy in copies:
        copy.start()
    bias_col[...] = jnp.broadcast_to(bias[...], (128, own)).T[:, :1]
    for copy in copies:
        copy.wait()


def arrange(weight, bias, depth, after):
    own = weight.shape[2]
    shape = (3 * own, 3 * depth)
    return pl.pallas_call(
        arrange_kernel,
        out_shape=(
            jax.ShapeDtypeStruct(shape, weight.dtype),
            jax.ShapeDtypeStruct((own, 1), bias.dtype),
        ),
        in_specs=[ANY, VMEM] + [ANY] * len(after),
        out_specs=(VMEM, VMEM),
        scratch_shapes=[pltpu.SemaphoreType.DMA((9,))],
        compiler_params=params((shape, 2)),
        cost_estimate=pl.CostEstimate(
            flops=0, bytes_accessed=36 * own * depth, transcendentals=0
        ),
    )(weight, bias.reshape(1, own), *after)


def block_place(index, n_filt, n_sp):
    j, k = divmod(index, n_filt)
    return behind("sp", n_sp, j) * n_filt + folded_behind("filt", n_filt, k)


def turn_row(turned, row):
    values = row.T
    depth = values.shape[0]
    turned[pl.ds(0, depth), :] = move_columns(values, 1)
    turned[pl.ds(depth, depth), :] = values
    turned[pl.ds(2 * depth, depth), :] = move_columns(values, -1)


def add_row(total, slot, taps, row, turned):
    own = taps.shape[0] // 3
    turn_row(turned, row)
    product = jnp.dot(taps[...], turned[...], preferred_element_type=jnp.float32)
    for a in range(3):
        total[slot + 1 - a] += product[a * own : (a + 1) * own]


def add_blocks_kernel(where, n_filt, n_sp, fresh, taps, *refs):
    *blocks, total, turned = refs if fresh else refs[1:]
    rows_dev = blocks[0].shape[0]
    total[...] = jnp.zeros(total.shape, total.dtype) if fresh else refs[0][...]
    for index, (block, (j, k)) in enumerate(zip(blocks, where)):
        place = block_place(j * n_filt + k, n_filt, n_sp)
        for i in range(rows_dev):
            at = index * rows_dev + i
            add_row(total, place * rows_dev + i + 1, taps, block[i], turned.at[at])


def add_blocks(taps, sides, where, side_rows, begun=()):
    n_sp, n_filt = len(sides), len(sides[0])
    blocks = [sides[j][k] for j, k in where]
    rows_dev, width, depth = blocks[0].shape
    own = taps.shape[0] // 3
    shape = (n_sp * side_rows + 2, own, width)
    turned = (len(blocks) * rows_dev, 3 * depth, width)
    return pl.pallas_call(
        functools.partial(add_blocks_kernel, where, n_filt, n_sp, not begun),
        out_shape=jax.ShapeDtypeStruct(shape, jnp.float32),
        in_specs=[VMEM] * (1 + len(begun) + len(blocks)),
        out_specs=VMEM,
        scratch_shapes=[pltpu.VMEM(turned, blocks[0].dtype)],
        compiler_params=params((turned, 2), (shape, 8), (taps.shape, 4)),
        cost_estimate=pl.CostEstimate(
            flops=30 * len(blocks) * rows_dev * own * width * depth,
            bytes_accessed=18 * own * depth,
            transcendentals=0,
        ),
    )(taps, *begun, *blocks)


def last_rows_kernel(n_filt, n_sp, j, n_after, taps, begun, *refs):
    *blocks, out, total, turned = refs[n_after:]
    rows_dev = blocks[0].shape[0]
    side_rows, own = total.shape[0] - 2, total.shape[1]
    side = behind("sp", n_sp, j)
    total[...] = begun[pl.ds(side * side_rows, side_rows + 2)]

    def slot_of(other):
        place = block_place(other * n_filt + n_filt - 1, n_filt, n_sp)
        return place * rows_dev - side * side_rows + 1

    for other, block in enumerate(blocks, 1):
        for i in range(rows_dev):
            if other == j:
                add_row(total, slot_of(other) + i, taps, block[i], turned.at[i])
        if other != j:
            for i, at, edge, a in ((rows_dev - 1, 0, 1, 0), (0, side_rows + 1, side_rows, 2)):

                @pl.when(slot_of(other) + i == at)
                def _():
                    turn_row(turned.at[0], block[i])
                    rows = taps[pl.ds(a * own, own), :]
                    product = jnp.dot(rows, turned[0], preferred_element_type=jnp.float32)
                    total[edge] += product

    out[...] = total[pl.ds(1, side_rows)]


def last_rows(taps, begun, sides, j, side_rows, after=()):
    n_sp, n_filt = len(sides), len(sides[0])
    blocks = [side[-1] for side in sides[1:]]
    rows_dev, width, depth = blocks[0].shape
    own = taps.shape[0] // 3
    out = (side_rows, own, width)
    total = (side_rows + 2, own, width)
    turned = (rows_dev, 3 * depth, width)
    return pl.pallas_call(
        functools.partial(last_rows_kernel, n_filt, n_sp, j, len(after)),
        out_shape=jax.ShapeDtypeStruct(out, jnp.float32),
        in_specs=[VMEM] * 2 + [ANY] * len(after) + [VMEM] * len(blocks),
        out_specs=VMEM,
        scratch_shapes=[
            pltpu.VMEM(total, jnp.float32),
            pltpu.VMEM(turned, blocks[0].dtype),
        ],
        compiler_params=params(
            (turned, 2 + n_sp), (total, 12), (begun.shape, 4), (taps.shape, 4)
        ),
        cost_estimate=pl.CostEstimate(
            flops=18 * rows_dev * own * width * depth,
            bytes_accessed=18 * own * depth,
            transcendentals=0,
        ),
    )(taps, begun, *after, *blocks)


def silu_parts(shifted, cotangent):
    sigmoid_v = 0.5 * jnp.tanh(0.5 * shifted) + 0.5
    slope = sigmoid_v * (1.0 + shifted * (1.0 - sigmoid_v))
    grad_out = (cotangent.astype(jnp.float32) * slope).astype(jnp.bfloat16)
    return sigmoid_v, grad_out


def silu_kernel(n_filt, mine, theirs, bias, cotangent, grad_out, *activated):
    rows, _, half = activated[0].shape

    for k in range(n_filt):
        first = behind("filt", n_filt, n_filt - k if k else 0) * rows

        @pl.loop(0, rows)
        def _(i):
            r = first + i
            shifted = (mine[r] + theirs[r]) + bias[...]
            sigmoid_v, grad_out[r] = silu_parts(shifted, cotangent[r])
            value = (shifted * sigmoid_v).astype(activated[k].dtype)
            activated[k][i] = jnp.where(
                lax.axis_index("in") == 0, value[:, :half], value[:, half:]
            )


def silu(mine, theirs, bias, cotangent, n_filt):
    rows, own, width = cotangent.shape
    return pl.pallas_call(
        functools.partial(silu_kernel, n_filt),
        out_shape=[jax.ShapeDtypeStruct((rows, own, width), jnp.bfloat16)]
        + [jax.ShapeDtypeStruct((rows // n_filt, own, width // 2), jnp.bfloat16)] * n_filt,
        in_specs=[VMEM] * 4,
        out_specs=[VMEM] * (1 + n_filt),
        compiler_params=params((cotangent.shape, 16)),
        cost_estimate=pl.CostEstimate(
            flops=10 * rows * own * width,
            bytes_accessed=13 * rows * own * width,
            transcendentals=rows * own * width,
        ),
    )(mine, theirs, bias, cotangent)


def shift_grads(grads, grad_out, row):
    own, width = grad_out.shape
    at = pl.ds(pl.multiple_of(row * width, width), width)
    grads[pl.ds(0, own), at] = move_columns(grad_out, -1)
    grads[pl.ds(own, own), at] = grad_out
    grads[pl.ds(2 * own, own), at] = move_columns(grad_out, 1)


def panel_copies(panel, blocks, n_filt, n_sp, sems):
    rows_dev, width, _ = blocks[0].shape
    copies = []
    for index, block in enumerate(blocks):
        place = block_place(index, n_filt, n_sp)
        for i in range(rows_dev):
            at = pl.multiple_of((place * rows_dev + i + 1) * width, width)
            to = panel.at[pl.ds(at, width), :]
            copies.append(pltpu.make_async_copy(block.at[i], to, sems.at[index * rows_dev + i]))
    return copies


def gradient_kernel(n_filt, n_sp, bias, own_grad, *refs):
    others, refs = refs[: 4 * (n_sp - 1)], refs[4 * (n_sp - 1) :]
    *blocks, weight_sum, bias_sum, formed, grads, panel, stage, sems, row_sems = refs
    side_rows, own, width = own_grad.shape
    copies = panel_copies(panel, blocks, n_filt, n_sp, row_sems)
    for copy in copies:
        copy.start()
    zeros = jnp.zeros((width, panel.shape[1]), panel.dtype)
    panel[pl.ds(0, width), :] = zeros
    panel[pl.ds((n_sp * side_rows + 1) * width, width), :] = zeros
    half_rows = side_rows // 2
    half = lax.axis_index("in")
    first = lax.axis_index("sp") * side_rows
    for r in range(side_rows):
        shift_grads(grads, own_grad[r], first + r)
    for j in range(1, n_sp):
        mine, theirs, near, far = others[4 * (j - 1) : 4 * j]
        first = behind("sp", n_sp, j) * side_rows
        for h, cotangent in enumerate((near, far)):
            start = (half if h == 0 else 1 - half) * half_rows
            for r in range(half_rows):
                shifted = (mine[start + r] + theirs[start + r]) + bias[...]
                _, grad_out = silu_parts(shifted, cotangent[r])
                shift_grads(grads, grad_out, first + start + r)

    formed[...] = jnp.zeros(formed.shape, formed.dtype)
    for copy in copies:
        copy.wait()

    def copy_out(a, b):
        return pltpu.make_async_copy(stage.at[a, b], weight_sum.at[a, b], sems.at[a, b])

    @pl.loop(0, 3)
    def _(a):
        window = panel[pl.ds(pl.multiple_of(a * width, width), grads.shape[1]), :]
        product = jnp.dot(grads[...], window, preferred_element_type=jnp.float32)
        for b in range(3):
            stage[a, b] = product[b * own : (b + 1) * own]
            copy_out(a, b).start()

    ones = jnp.ones((16, grads.shape[1]), grads.dtype)
    sums = lax.dot_general(
        ones,
        grads[pl.ds(own, own), :],
        (((1,), (1,)), ((), ())),
        preferred_element_type=jnp.float32,
    )
    bias_sum[...] = sums[:1]

    @pl.loop(0, 9)
    def _(i):
        copy_out(lax.div(i, 3), lax.rem(i, 3)).wait()


def gradient(bias, own_grad, others, sides):
    n_sp, n_filt = len(sides), len(sides[0])
    blocks = [block for side in sides for block in side]
    side_rows, own, width = own_grad.shape
    depth = blocks[0].shape[2]
    all_rows = n_sp * side_rows
    panel = ((all_rows + 2) * width, depth)
    grads = (3 * own, all_rows * width)
    total = (3, 3, own, depth)
    return pl.pallas_call(
        functools.partial(gradient_kernel, n_filt, n_sp),
        out_shape=[
            jax.ShapeDtypeStruct(total, jnp.float32),
            jax.ShapeDtypeStruct((1, own), jnp.float32),
            jax.ShapeDtypeStruct((8, 128), jnp.float32),
        ],
        in_specs=[VMEM] * (2 + len(others)) + [ANY] * len(blocks),
        out_specs=[ANY, VMEM, VMEM],
        scratch_shapes=[
            pltpu.VMEM(grads, jnp.bfloat16),
            pltpu.VMEM(panel, blocks[0].dtype),
            pltpu.VMEM(total, jnp.float32),
            pltpu.SemaphoreType.DMA((3, 3)),
            pltpu.SemaphoreType.DMA((all_rows,)),
        ],
        compiler_params=params(
            (grads, 2), (panel, 2), (total, 5), ((all_rows, own, width), 12)
        ),
        cost_estimate=pl.CostEstimate(
            flops=18 * all_rows * own * width * depth,
            bytes_accessed=36 * own * depth + 2 * all_rows * width * depth,
            transcendentals=all_rows * own * width,
        ),
    )(bias, own_grad, *others, *blocks)


def place_kernel(*refs):
    *pieces, _, output, sems = refs
    own = pieces[0].shape[1]
    copies = []
    for k, piece in enumerate(pieces):
        at = pl.multiple_of(behind("filt", len(pieces), k) * own, own)
        rows = output.at[:, pl.ds(at, own), :]
        copies.append(pltpu.make_async_copy(piece, rows, sems.at[k]))
    for copy in copies:
        copy.start()
    for copy in copies:
        copy.wait()


def place_pieces(pieces, after):
    rows, own, half = pieces[0].shape
    return pl.pallas_call(
        place_kernel,
        out_shape=jax.ShapeDtypeStruct((rows, len(pieces) * own, half), pieces[0].dtype),
        in_specs=[VMEM] * (len(pieces) + 1),
        out_specs=ANY,
        scratch_shapes=[pltpu.SemaphoreType.DMA((len(pieces),))],
        compiler_params=params((pieces[0].shape, 2 * len(pieces))),
        cost_estimate=pl.CostEstimate(
            flops=0, bytes_accessed=4 * len(pieces) * rows * own * half, transcendentals=0
        ),
    )(*pieces, after)


def on_device(image, weight, bias, cotangent):
    n_filt, n_sp = lax.axis_size("filt"), lax.axis_size("sp")
    side_rows = cotangent.shape[0]
    swap = shifted_ring("in", 1)

    gathered = gather_blocks(image)
    taps, bias_col = arrange(weight, bias, image.shape[2], [gathered[-1][0]])
    places = [[(j, k) for j in range(n_sp)] for k in range(n_filt)]
    first, second = places[: n_filt // 2], places[n_filt // 2 :]
    second[-1] = [(0, n_filt - 1)]
    begun = add_blocks(taps, gathered, first[0], side_rows)
    near = send_held(gathered, cotangent, [begun, gathered[0][-2]])
    for group in (sum(first[1:], []), sum(second, [])):
        begun = add_blocks(taps, gathered, group, side_rows, [begun])

    partial = [last_rows(taps, begun, gathered, 0, side_rows)]
    for j in range(1, n_sp):
        partial.append(last_rows(taps, begun, gathered, j, side_rows, [near[j]]))
    other = [lax.ppermute(value, "in", swap) for value in partial]

    own_grad, *rows = silu(partial[0], other[0], bias_col, cotangent, n_filt)
    pieces = rows[:1]
    for k in range(1, n_filt):
        pieces.append(lax.ppermute(rows[k], "filt", shifted_ring("filt", k)))
    others = []
    for j in range(1, n_sp):
        others += [partial[j], other[j], near[j], lax.ppermute(near[j], "in", swap)]
    grad_weight, grad_bias, formed = gradient(bias_col, own_grad, others, gathered)
    output = place_pieces(pieces, formed)
    return (output, grad_weight, grad_bias.reshape(-1))


def solution(mesh):
    placed = (
        P(("groups", "sp", "filt"), None, "in"),
        P(None, None, "filt", None),
        P("filt"),
        P(("groups", "sp"), "filt", None),
    )
    return jax.shard_map(
        on_device,
        mesh=mesh,
        in_specs=placed,
        out_specs=(
            P(("groups", "sp", "filt"), None, "in"),
            P("groups", None, "filt", "in"),
            P(("groups", "filt")),
        ),
        check_vma=False,
    )
```

```python
import functools
import math

import jax
import jax.numpy as jnp
from jax import lax
from jax.experimental import pallas as pl
from jax.experimental.pallas import tpu as pltpu
from jax.sharding import PartitionSpec as P

MIB = 1024 * 1024


def params(*arrays):
    held = sum(math.prod(shape) * size for shape, size in arrays)
    return pltpu.CompilerParams(vmem_limit_bytes=max(20 * MIB, held * 5 // 4 + 8 * MIB))


def shifted_ring(axis, shift):
    size = lax.axis_size(axis)
    return [(i, (i + shift) % size) for i in range(size)]


def folded_ring(axis, shift):
    size = lax.axis_size(axis)
    order = [0, *range(1, size, 2), *reversed(range(2, size, 2))]
    return [(order[i], order[(i + shift) % size]) for i in range(size)]


def folded_behind(axis, size, by):
    index = lax.axis_index(axis)
    back = size - lax.div(index, 2)
    place = jnp.where(lax.rem(index, 2) == 1, lax.div(index + 1, 2), lax.rem(back, size))
    place = lax.rem(place + (size - by), size)
    out = 2 * place - 1
    return jnp.where(place == 0, 0, jnp.where(place <= size // 2, out, 2 * (size - place)))


def gather_blocks(image):
    n_filt, n_sp = lax.axis_size("filt"), lax.axis_size("sp")
    onward, outward = shifted_ring("sp", 1), folded_ring("filt", 1)
    blocks = [[None] * n_filt for _ in range(n_sp)]
    blocks[0][0] = image
    last = n_filt - 1
    for k in range(n_filt):
        if k:
            blocks[0][k] = lax.ppermute(blocks[0][k - 1], "filt", outward)
        for j in range(1, n_sp):
            if k < max(last, 1):
                blocks[j][k] = lax.ppermute(blocks[j - 1][k], "sp", onward)
    return blocks


def send_held(blocks, cotangent, after):
    n_filt, n_sp = len(blocks[0]), len(blocks)
    first = [side[0] for side in blocks[1:]]
    half, *first = hold(cotangent, first, after)
    halves = [half]
    for j in range(1, n_sp):
        if n_filt > 1:
            blocks[j][-1] = lax.ppermute(first[j - 1], "filt", folded_ring("filt", -1))
        halves.append(lax.ppermute(halves[-1], "sp", shifted_ring("sp", 1)))
    return halves


def move_columns(values, by):
    size = values.shape[1]
    column = lax.broadcasted_iota(jnp.int32, values.shape, 1)
    edge = 0 if by == 1 else size - 1
    return jnp.where(column == edge, jnp.zeros_like(values), pltpu.roll(values, by % size, 1))


VMEM = pl.BlockSpec(memory_space=pltpu.VMEM)
ANY = pl.BlockSpec(memory_space=pl.ANY)


def behind(axis, size, by):
    return lax.rem(lax.axis_index(axis) + (size - by), size)


def hold_kernel(n_blocks, n_after, cotangent, *refs):
    blocks, (half, *copies, sems) = refs[:n_blocks], refs[n_blocks + n_after :]
    rows = half.shape[0]
    moves = [(cotangent.at[pl.ds(lax.axis_index("in") * rows, rows)], half)]
    moves += zip(blocks, copies)
    moves = [pltpu.make_async_copy(*move, sems.at[i]) for i, move in enumerate(moves)]
    for move in moves:
        move.start()
    for move in moves:
        move.wait()


def hold(cotangent, blocks, after):
    shape = (cotangent.shape[0] // 2,) + cotangent.shape[1:]
    held = [jax.ShapeDtypeStruct(block.shape, block.dtype) for block in blocks]
    return pl.pallas_call(
        functools.partial(hold_kernel, len(blocks), len(after)),
        out_shape=[jax.ShapeDtypeStruct(shape, cotangent.dtype), *held],
        in_specs=[ANY] * (1 + len(blocks) + len(after)),
        out_specs=[VMEM] * (1 + len(blocks)),
        scratch_shapes=[pltpu.SemaphoreType.DMA((1 + len(blocks),))],
        compiler_params=params((shape, 2), *((block.shape, 2) for block in blocks)),
        cost_estimate=pl.CostEstimate(
            flops=0, bytes_accessed=4 * math.prod(shape), transcendentals=0
        ),
    )(cotangent, *blocks, *after)


def arrange_kernel(weight, bias, *refs):
    taps, bias_col, sems = refs[-3:]
    depth = taps.shape[1] // 3
    own = weight.shape[2]
    half = lax.axis_index("in")
    copies = [
        pltpu.make_async_copy(
            weight.at[a, b, :, pl.ds(pl.multiple_of(half * depth, depth), depth)],
            taps.at[pl.ds(a * own, own), pl.ds(b * depth, depth)],
            sems.at[a * 3 + b],
        )
        for a in range(3)
        for b in range(3)
    ]
    for copy in copies:
        copy.start()
    bias_col[...] = jnp.broadcast_to(bias[...], (128, own)).T[:, :1]
    for copy in copies:
        copy.wait()


def arrange(weight, bias, depth, after):
    own = weight.shape[2]
    shape = (3 * own, 3 * depth)
    return pl.pallas_call(
        arrange_kernel,
        out_shape=(
            jax.ShapeDtypeStruct(shape, weight.dtype),
            jax.ShapeDtypeStruct((own, 1), bias.dtype),
        ),
        in_specs=[ANY, VMEM] + [ANY] * len(after),
        out_specs=(VMEM, VMEM),
        scratch_shapes=[pltpu.SemaphoreType.DMA((9,))],
        compiler_params=params((shape, 2)),
        cost_estimate=pl.CostEstimate(
            flops=0, bytes_accessed=36 * own * depth, transcendentals=0
        ),
    )(weight, bias.reshape(1, own), *after)


def block_place(index, n_filt, n_sp):
    j, k = divmod(index, n_filt)
    return behind("sp", n_sp, j) * n_filt + folded_behind("filt", n_filt, k)


def turn_row(turned, row):
    values = row.T
    depth = values.shape[0]
    turned[pl.ds(0, depth), :] = move_columns(values, 1)
    turned[pl.ds(depth, depth), :] = values
    turned[pl.ds(2 * depth, depth), :] = move_columns(values, -1)


def add_row(total, slot, taps, row, turned):
    own = taps.shape[0] // 3
    turn_row(turned, row)
    product = jnp.dot(taps[...], turned[...], preferred_element_type=jnp.float32)
    for a in range(3):
        total[slot + 1 - a] += product[a * own : (a + 1) * own]


def add_blocks_kernel(where, n_filt, n_sp, fresh, taps, *refs):
    *blocks, total, turned = refs if fresh else refs[1:]
    rows_dev = blocks[0].shape[0]
    total[...] = jnp.zeros(total.shape, total.dtype) if fresh else refs[0][...]
    for index, (block, (j, k)) in enumerate(zip(blocks, where)):
        place = block_place(j * n_filt + k, n_filt, n_sp)
        for i in range(rows_dev):
            at = index * rows_dev + i
            add_row(total, place * rows_dev + i + 1, taps, block[i], turned.at[at])


def add_blocks(taps, sides, where, side_rows, begun=()):
    n_sp, n_filt = len(sides), len(sides[0])
    blocks = [sides[j][k] for j, k in where]
    rows_dev, width, depth = blocks[0].shape
    own = taps.shape[0] // 3
    shape = (n_sp * side_rows + 2, own, width)
    turned = (len(blocks) * rows_dev, 3 * depth, width)
    return pl.pallas_call(
        functools.partial(add_blocks_kernel, where, n_filt, n_sp, not begun),
        out_shape=jax.ShapeDtypeStruct(shape, jnp.float32),
        in_specs=[VMEM] * (1 + len(begun) + len(blocks)),
        out_specs=VMEM,
        scratch_shapes=[pltpu.VMEM(turned, blocks[0].dtype)],
        compiler_params=params((turned, 2), (shape, 8), (taps.shape, 4)),
        cost_estimate=pl.CostEstimate(
            flops=30 * len(blocks) * rows_dev * own * width * depth,
            bytes_accessed=18 * own * depth,
            transcendentals=0,
        ),
    )(taps, *begun, *blocks)


def last_rows_kernel(n_filt, n_sp, j, n_after, taps, begun, *refs):
    *blocks, out, total, turned = refs[n_after:]
    rows_dev = blocks[0].shape[0]
    side_rows, own = total.shape[0] - 2, total.shape[1]
    side = behind("sp", n_sp, j)
    total[...] = begun[pl.ds(side * side_rows, side_rows + 2)]

    def slot_of(other):
        place = block_place(other * n_filt + n_filt - 1, n_filt, n_sp)
        return place * rows_dev - side * side_rows + 1

    for other, block in enumerate(blocks, 1):
        for i in range(rows_dev):
            if other == j:
                add_row(total, slot_of(other) + i, taps, block[i], turned.at[i])
        if other != j:
            for i, at, edge, a in ((rows_dev - 1, 0, 1, 0), (0, side_rows + 1, side_rows, 2)):

                @pl.when(slot_of(other) + i == at)
                def _():
                    turn_row(turned.at[0], block[i])
                    rows = taps[pl.ds(a * own, own), :]
                    product = jnp.dot(rows, turned[0], preferred_element_type=jnp.float32)
                    total[edge] += product

    out[...] = total[pl.ds(1, side_rows)]


def last_rows(taps, begun, sides, j, side_rows, after=()):
    n_sp, n_filt = len(sides), len(sides[0])
    blocks = [side[-1] for side in sides[1:]]
    rows_dev, width, depth = blocks[0].shape
    own = taps.shape[0] // 3
    out = (side_rows, own, width)
    total = (side_rows + 2, own, width)
    turned = (rows_dev, 3 * depth, width)
    return pl.pallas_call(
        functools.partial(last_rows_kernel, n_filt, n_sp, j, len(after)),
        out_shape=jax.ShapeDtypeStruct(out, jnp.float32),
        in_specs=[VMEM] * 2 + [ANY] * len(after) + [VMEM] * len(blocks),
        out_specs=VMEM,
        scratch_shapes=[
            pltpu.VMEM(total, jnp.float32),
            pltpu.VMEM(turned, blocks[0].dtype),
        ],
        compiler_params=params(
            (turned, 2 + n_sp), (total, 12), (begun.shape, 4), (taps.shape, 4)
        ),
        cost_estimate=pl.CostEstimate(
            flops=18 * rows_dev * own * width * depth,
            bytes_accessed=18 * own * depth,
            transcendentals=0,
        ),
    )(taps, begun, *after, *blocks)


def silu_parts(shifted, cotangent):
    sigmoid_v = 0.5 * jnp.tanh(0.5 * shifted) + 0.5
    slope = sigmoid_v * (1.0 + shifted * (1.0 - sigmoid_v))
    grad_out = (cotangent.astype(jnp.float32) * slope).astype(jnp.bfloat16)
    return sigmoid_v, grad_out


def silu_kernel(n_filt, mine, theirs, bias, cotangent, grad_out, *activated):
    rows, _, half = activated[0].shape

    for k in range(n_filt):
        first = behind("filt", n_filt, n_filt - k if k else 0) * rows

        @pl.loop(0, rows)
        def _(i):
            r = first + i
            shifted = (mine[r] + theirs[r]) + bias[...]
            sigmoid_v, grad_out[r] = silu_parts(shifted, cotangent[r])
            value = (shifted * sigmoid_v).astype(activated[k].dtype)
            activated[k][i] = jnp.where(
                lax.axis_index("in") == 0, value[:, :half], value[:, half:]
            )


def silu(mine, theirs, bias, cotangent, n_filt):
    rows, own, width = cotangent.shape
    return pl.pallas_call(
        functools.partial(silu_kernel, n_filt),
        out_shape=[jax.ShapeDtypeStruct((rows, own, width), jnp.bfloat16)]
        + [jax.ShapeDtypeStruct((rows // n_filt, own, width // 2), jnp.bfloat16)] * n_filt,
        in_specs=[VMEM] * 4,
        out_specs=[VMEM] * (1 + n_filt),
        compiler_params=params((cotangent.shape, 16)),
        cost_estimate=pl.CostEstimate(
            flops=10 * rows * own * width,
            bytes_accessed=13 * rows * own * width,
            transcendentals=rows * own * width,
        ),
    )(mine, theirs, bias, cotangent)


def shift_grads(grads, grad_out, row):
    own, width = grad_out.shape
    at = pl.ds(pl.multiple_of(row * width, width), width)
    grads[pl.ds(0, own), at] = move_columns(grad_out, -1)
    grads[pl.ds(own, own), at] = grad_out
    grads[pl.ds(2 * own, own), at] = move_columns(grad_out, 1)


def panel_copies(panel, blocks, n_filt, n_sp, sems):
    rows_dev, width, _ = blocks[0].shape
    copies = []
    for index, block in enumerate(blocks):
        place = block_place(index, n_filt, n_sp)
        for i in range(rows_dev):
            at = pl.multiple_of((place * rows_dev + i + 1) * width, width)
            to = panel.at[pl.ds(at, width), :]
            copies.append(pltpu.make_async_copy(block.at[i], to, sems.at[index * rows_dev + i]))
    return copies


def gradient_kernel(n_filt, n_sp, bias, own_grad, *refs):
    others, refs = refs[: 4 * (n_sp - 1)], refs[4 * (n_sp - 1) :]
    *blocks, weight_sum, bias_sum, formed = refs[: n_sp * n_filt + 3]
    grads, (panel, stage, sems, row_sems) = refs[-4 - n_sp : -4], refs[-4:]
    side_rows, own, width = own_grad.shape
    half_rows = side_rows // 2
    half = lax.axis_index("in")
    copies = panel_copies(panel, blocks, n_filt, n_sp, row_sems)
    for copy in copies:
        copy.start()
    zeros = jnp.zeros((width, panel.shape[1]), panel.dtype)
    panel[pl.ds(0, width), :] = zeros
    panel[pl.ds((n_sp * side_rows + 1) * width, width), :] = zeros
    for r in range(side_rows):
        shift_grads(grads[0], own_grad[r], r)
    for copy in copies:
        copy.wait()

    def tap_gradient(j, a):
        first = (behind("sp", n_sp, j) * side_rows + a) * width
        window = panel[pl.ds(pl.multiple_of(first, width), side_rows * width), :]
        return jnp.dot(grads[j][...], window, preferred_element_type=jnp.float32)

    def copy_out(a, b):
        return pltpu.make_async_copy(stage.at[a, b], weight_sum.at[a, b], sems.at[a, b])

    for a in range(3):
        stage[a] = tap_gradient(0, a).reshape(stage.shape[1:])
    for j in range(1, n_sp):
        mine, theirs, near, far = others[4 * (j - 1) : 4 * j]
        for h, cotangent in enumerate((near, far)):
            start = (half if h == 0 else 1 - half) * half_rows
            for r in range(half_rows):
                shifted = (mine[start + r] + theirs[start + r]) + bias[...]
                _, grad_out = silu_parts(shifted, cotangent[r])
                shift_grads(grads[j], grad_out, start + r)

    for a in range(3):
        for j in range(1, n_sp):
            product = tap_gradient(j, a)
            for b in range(3):
                stage[a, b] += product[b * own : (b + 1) * own]
                if j == n_sp - 1:
                    copy_out(a, b).start()

    total = jnp.zeros((16, own), jnp.float32)
    for side in grads:
        total += lax.dot_general(
            jnp.ones((16, side.shape[1]), side.dtype),
            side[pl.ds(own, own), :],
            (((1,), (1,)), ((), ())),
            preferred_element_type=jnp.float32,
        )
    bias_sum[...] = total[:1]
    formed[...] = jnp.zeros(formed.shape, formed.dtype)
    for a in range(3):
        for b in range(3):
            copy_out(a, b).wait()


def gradient(bias, own_grad, others, sides):
    n_sp, n_filt = len(sides), len(sides[0])
    blocks = [block for side in sides for block in side]
    side_rows, own, width = own_grad.shape
    depth = blocks[0].shape[2]
    all_rows = n_sp * side_rows
    panel = ((all_rows + 2) * width, depth)
    grads = (3 * own, side_rows * width)
    total = (3, 3, own, depth)
    return pl.pallas_call(
        functools.partial(gradient_kernel, n_filt, n_sp),
        out_shape=[
            jax.ShapeDtypeStruct(total, jnp.float32),
            jax.ShapeDtypeStruct((1, own), jnp.float32),
            jax.ShapeDtypeStruct((8, 128), jnp.float32),
        ],
        in_specs=[VMEM] * (2 + len(others)) + [ANY] * len(blocks),
        out_specs=[ANY, VMEM, VMEM],
        scratch_shapes=[
            *[pltpu.VMEM(grads, jnp.bfloat16)] * n_sp,
            pltpu.VMEM(panel, blocks[0].dtype),
            pltpu.VMEM(total, jnp.float32),
            pltpu.SemaphoreType.DMA((3, 3)),
            pltpu.SemaphoreType.DMA((all_rows,)),
        ],
        compiler_params=params(
            (grads, 2 * n_sp), (panel, 2), (total, 6), ((all_rows, own, width), 12)
        ),
        cost_estimate=pl.CostEstimate(
            flops=18 * all_rows * own * width * depth,
            bytes_accessed=36 * own * depth + 2 * all_rows * width * depth,
            transcendentals=all_rows * own * width,
        ),
    )(bias, own_grad, *others, *blocks)


def place_kernel(*refs):
    *pieces, _, output, sems = refs
    own = pieces[0].shape[1]
    copies = []
    for k, piece in enumerate(pieces):
        at = pl.multiple_of(behind("filt", len(pieces), k) * own, own)
        rows = output.at[:, pl.ds(at, own), :]
        copies.append(pltpu.make_async_copy(piece, rows, sems.at[k]))
    for copy in copies:
        copy.start()
    for copy in copies:
        copy.wait()


def place_pieces(pieces, after):
    rows, own, half = pieces[0].shape
    return pl.pallas_call(
        place_kernel,
        out_shape=jax.ShapeDtypeStruct((rows, len(pieces) * own, half), pieces[0].dtype),
        in_specs=[VMEM] * (len(pieces) + 1),
        out_specs=ANY,
        scratch_shapes=[pltpu.SemaphoreType.DMA((len(pieces),))],
        compiler_params=params((pieces[0].shape, 2 * len(pieces))),
        cost_estimate=pl.CostEstimate(
            flops=0, bytes_accessed=4 * len(pieces) * rows * own * half, transcendentals=0
        ),
    )(*pieces, after)


def on_device(image, weight, bias, cotangent):
    n_filt, n_sp = lax.axis_size("filt"), lax.axis_size("sp")
    side_rows = cotangent.shape[0]
    swap = shifted_ring("in", 1)

    gathered = gather_blocks(image)
    taps, bias_col = arrange(weight, bias, image.shape[2], [gathered[-1][0]])
    places = [[(j, k) for j in range(n_sp)] for k in range(n_filt)]
    first, second = places[: n_filt // 2], places[n_filt // 2 :]
    second[-1] = [(0, n_filt - 1)]
    begun = add_blocks(taps, gathered, first[0], side_rows)
    near = send_held(gathered, cotangent, [begun, gathered[0][-2]])
    for group in (sum(first[1:], []), sum(second, [])):
        begun = add_blocks(taps, gathered, group, side_rows, [begun])

    partial = [last_rows(taps, begun, gathered, 0, side_rows)]
    for j in range(1, n_sp):
        partial.append(last_rows(taps, begun, gathered, j, side_rows, [near[j]]))
    other = [lax.ppermute(value, "in", swap) for value in partial]

    own_grad, *rows = silu(partial[0], other[0], bias_col, cotangent, n_filt)
    pieces = rows[:1]
    for k in range(1, n_filt):
        pieces.append(lax.ppermute(rows[k], "filt", shifted_ring("filt", k)))
    others = []
    for j in range(1, n_sp):
        others += [partial[j], other[j], near[j], lax.ppermute(near[j], "in", swap)]
    grad_weight, grad_bias, formed = gradient(bias_col, own_grad, others, gathered)
    output = place_pieces(pieces, formed)
    return (output, grad_weight, grad_bias.reshape(-1))


def solution(mesh):
    placed = (
        P(("groups", "sp", "filt"), None, "in"),
        P(None, None, "filt", None),
        P("filt"),
        P(("groups", "sp"), "filt", None),
    )
    return jax.shard_map(
        on_device,
        mesh=mesh,
        in_specs=placed,
        out_specs=(
            P(("groups", "sp", "filt"), None, "in"),
            P("groups", None, "filt", "in"),
            P(("groups", "filt")),
        ),
        check_vma=False,
    )
```

```python
import functools
import math

import jax
import jax.numpy as jnp
from jax import lax
from jax.experimental import pallas as pl
from jax.experimental.pallas import tpu as pltpu
from jax.sharding import PartitionSpec as P

MIB = 1024 * 1024


def params(*arrays):
    held = sum(math.prod(shape) * size for shape, size in arrays)
    return pltpu.CompilerParams(vmem_limit_bytes=max(20 * MIB, held * 5 // 4 + 8 * MIB))


def shifted_ring(axis, shift):
    size = lax.axis_size(axis)
    return [(i, (i + shift) % size) for i in range(size)]


def folded_ring(axis, shift):
    size = lax.axis_size(axis)
    order = [0, *range(1, size, 2), *reversed(range(2, size, 2))]
    return [(order[i], order[(i + shift) % size]) for i in range(size)]


def folded_behind(axis, size, by):
    index = lax.axis_index(axis)
    back = size - lax.div(index, 2)
    place = jnp.where(lax.rem(index, 2) == 1, lax.div(index + 1, 2), lax.rem(back, size))
    place = lax.rem(place + (size - by), size)
    out = 2 * place - 1
    return jnp.where(place == 0, 0, jnp.where(place <= size // 2, out, 2 * (size - place)))


def gather_blocks(image):
    n_filt, n_sp = lax.axis_size("filt"), lax.axis_size("sp")
    onward, outward = shifted_ring("sp", 1), folded_ring("filt", 1)
    blocks = [[None] * n_filt for _ in range(n_sp)]
    blocks[0][0] = image
    last = n_filt - 1
    for k in range(n_filt):
        if k:
            blocks[0][k] = lax.ppermute(blocks[0][k - 1], "filt", outward)
        for j in range(1, n_sp):
            if k < max(last, 1):
                blocks[j][k] = lax.ppermute(blocks[j - 1][k], "sp", onward)
    return blocks


def send_held(blocks, cotangent, after):
    n_filt, n_sp = len(blocks[0]), len(blocks)
    first = [side[0] for side in blocks[1:]]
    half, *first = hold(cotangent, first, after)
    halves = [half]
    for j in range(1, n_sp):
        if n_filt > 1:
            blocks[j][-1] = lax.ppermute(first[j - 1], "filt", folded_ring("filt", -1))
        halves.append(lax.ppermute(halves[-1], "sp", shifted_ring("sp", 1)))
    return halves


def move_columns(values, by):
    size = values.shape[1]
    column = lax.broadcasted_iota(jnp.int32, values.shape, 1)
    edge = 0 if by == 1 else size - 1
    return jnp.where(column == edge, jnp.zeros_like(values), pltpu.roll(values, by % size, 1))


VMEM = pl.BlockSpec(memory_space=pltpu.VMEM)
ANY = pl.BlockSpec(memory_space=pl.ANY)


def behind(axis, size, by):
    return lax.rem(lax.axis_index(axis) + (size - by), size)


def hold_kernel(n_blocks, n_after, cotangent, *refs):
    blocks, (half, *copies, sems) = refs[:n_blocks], refs[n_blocks + n_after :]
    rows = half.shape[0]
    moves = [(cotangent.at[pl.ds(lax.axis_index("in") * rows, rows)], half)]
    moves += zip(blocks, copies)
    moves = [pltpu.make_async_copy(*move, sems.at[i]) for i, move in enumerate(moves)]
    for move in moves:
        move.start()
    for move in moves:
        move.wait()


def hold(cotangent, blocks, after):
    shape = (cotangent.shape[0] // 2,) + cotangent.shape[1:]
    held = [jax.ShapeDtypeStruct(block.shape, block.dtype) for block in blocks]
    return pl.pallas_call(
        functools.partial(hold_kernel, len(blocks), len(after)),
        out_shape=[jax.ShapeDtypeStruct(shape, cotangent.dtype), *held],
        in_specs=[ANY] * (1 + len(blocks) + len(after)),
        out_specs=[VMEM] * (1 + len(blocks)),
        scratch_shapes=[pltpu.SemaphoreType.DMA((1 + len(blocks),))],
        compiler_params=params((shape, 2), *((block.shape, 2) for block in blocks)),
        cost_estimate=pl.CostEstimate(
            flops=0, bytes_accessed=4 * math.prod(shape), transcendentals=0
        ),
    )(cotangent, *blocks, *after)


def arrange_kernel(weight, bias, *refs):
    taps, bias_col, sems = refs[-3:]
    depth = taps.shape[1] // 3
    own = weight.shape[2]
    half = lax.axis_index("in")
    copies = [
        pltpu.make_async_copy(
            weight.at[a, b, :, pl.ds(pl.multiple_of(half * depth, depth), depth)],
            taps.at[pl.ds(a * own, own), pl.ds(b * depth, depth)],
            sems.at[a * 3 + b],
        )
        for a in range(3)
        for b in range(3)
    ]
    for copy in copies:
        copy.start()
    bias_col[...] = jnp.broadcast_to(bias[...], (128, own)).T[:, :1]
    for copy in copies:
        copy.wait()


def arrange(weight, bias, depth, after):
    own = weight.shape[2]
    shape = (3 * own, 3 * depth)
    return pl.pallas_call(
        arrange_kernel,
        out_shape=(
            jax.ShapeDtypeStruct(shape, weight.dtype),
            jax.ShapeDtypeStruct((own, 1), bias.dtype),
        ),
        in_specs=[ANY, VMEM] + [ANY] * len(after),
        out_specs=(VMEM, VMEM),
        scratch_shapes=[pltpu.SemaphoreType.DMA((9,))],
        compiler_params=params((shape, 2)),
        cost_estimate=pl.CostEstimate(
            flops=0, bytes_accessed=36 * own * depth, transcendentals=0
        ),
    )(weight, bias.reshape(1, own), *after)


def block_place(index, n_filt, n_sp):
    j, k = divmod(index, n_filt)
    return behind("sp", n_sp, j) * n_filt + folded_behind("filt", n_filt, k)


def turn_row(turned, row):
    values = row.T
    depth = values.shape[0]
    turned[pl.ds(0, depth), :] = move_columns(values, 1)
    turned[pl.ds(depth, depth), :] = values
    turned[pl.ds(2 * depth, depth), :] = move_columns(values, -1)


def add_row(total, slot, taps, row, turned):
    own = taps.shape[0] // 3
    turn_row(turned, row)
    product = jnp.dot(taps[...], turned[...], preferred_element_type=jnp.float32)
    for a in range(3):
        total[slot + 1 - a] += product[a * own : (a + 1) * own]


def add_blocks_kernel(where, n_filt, n_sp, fresh, taps, *refs):
    *blocks, total, turned = refs if fresh else refs[1:]
    rows_dev = blocks[0].shape[0]
    total[...] = jnp.zeros(total.shape, total.dtype) if fresh else refs[0][...]
    for index, (block, (j, k)) in enumerate(zip(blocks, where)):
        place = block_place(j * n_filt + k, n_filt, n_sp)
        for i in range(rows_dev):
            at = index * rows_dev + i
            add_row(total, place * rows_dev + i + 1, taps, block[i], turned.at[at])


def add_blocks(taps, sides, where, side_rows, begun=()):
    n_sp, n_filt = len(sides), len(sides[0])
    blocks = [sides[j][k] for j, k in where]
    rows_dev, width, depth = blocks[0].shape
    own = taps.shape[0] // 3
    shape = (n_sp * side_rows + 2, own, width)
    turned = (len(blocks) * rows_dev, 3 * depth, width)
    return pl.pallas_call(
        functools.partial(add_blocks_kernel, where, n_filt, n_sp, not begun),
        out_shape=jax.ShapeDtypeStruct(shape, jnp.float32),
        in_specs=[VMEM] * (1 + len(begun) + len(blocks)),
        out_specs=VMEM,
        scratch_shapes=[pltpu.VMEM(turned, blocks[0].dtype)],
        compiler_params=params((turned, 2), (shape, 8), (taps.shape, 4)),
        cost_estimate=pl.CostEstimate(
            flops=(1 if begun else 30) * len(blocks) * rows_dev * own * width * depth,
            bytes_accessed=1,
            transcendentals=0,
        ),
    )(taps, *begun, *blocks)


def last_rows_kernel(n_filt, n_sp, j, n_after, taps, begun, *refs):
    *blocks, out, total, turned = refs[n_after:]
    rows_dev = blocks[0].shape[0]
    side_rows, own = total.shape[0] - 2, total.shape[1]
    side = behind("sp", n_sp, j)
    total[...] = begun[pl.ds(side * side_rows, side_rows + 2)]

    def slot_of(other):
        place = block_place(other * n_filt + n_filt - 1, n_filt, n_sp)
        return place * rows_dev - side * side_rows + 1

    for other, block in enumerate(blocks, 1):
        for i in range(rows_dev):
            if other == j:
                add_row(total, slot_of(other) + i, taps, block[i], turned.at[i])
        if other != j:
            for i, at, edge, a in ((rows_dev - 1, 0, 1, 0), (0, side_rows + 1, side_rows, 2)):

                @pl.when(slot_of(other) + i == at)
                def _():
                    turn_row(turned.at[0], block[i])
                    rows = taps[pl.ds(a * own, own), :]
                    product = jnp.dot(rows, turned[0], preferred_element_type=jnp.float32)
                    total[edge] += product

    out[...] = total[pl.ds(1, side_rows)]


def last_rows(taps, begun, sides, j, side_rows, after=()):
    n_sp, n_filt = len(sides), len(sides[0])
    blocks = [side[-1] for side in sides[1:]]
    rows_dev, width, depth = blocks[0].shape
    own = taps.shape[0] // 3
    out = (side_rows, own, width)
    total = (side_rows + 2, own, width)
    turned = (rows_dev, 3 * depth, width)
    return pl.pallas_call(
        functools.partial(last_rows_kernel, n_filt, n_sp, j, len(after)),
        out_shape=jax.ShapeDtypeStruct(out, jnp.float32),
        in_specs=[VMEM] * 2 + [ANY] * len(after) + [VMEM] * len(blocks),
        out_specs=VMEM,
        scratch_shapes=[
            pltpu.VMEM(total, jnp.float32),
            pltpu.VMEM(turned, blocks[0].dtype),
        ],
        compiler_params=params(
            (turned, 2 + n_sp), (total, 12), (begun.shape, 4), (taps.shape, 4)
        ),
        cost_estimate=pl.CostEstimate(
            flops=18 * rows_dev * own * width * depth,
            bytes_accessed=18 * own * depth,
            transcendentals=0,
        ),
    )(taps, begun, *after, *blocks)


def silu_parts(shifted, cotangent):
    sigmoid_v = 0.5 * jnp.tanh(0.5 * shifted) + 0.5
    slope = sigmoid_v * (1.0 + shifted * (1.0 - sigmoid_v))
    grad_out = (cotangent.astype(jnp.float32) * slope).astype(jnp.bfloat16)
    return sigmoid_v, grad_out


def silu_kernel(n_filt, mine, theirs, bias, cotangent, grad_out, *activated):
    rows, _, half = activated[0].shape

    for k in range(n_filt):
        first = behind("filt", n_filt, n_filt - k if k else 0) * rows

        @pl.loop(0, rows)
        def _(i):
            r = first + i
            shifted = (mine[r] + theirs[r]) + bias[...]
            sigmoid_v, grad_out[r] = silu_parts(shifted, cotangent[r])
            value = (shifted * sigmoid_v).astype(activated[k].dtype)
            activated[k][i] = jnp.where(
                lax.axis_index("in") == 0, value[:, :half], value[:, half:]
            )


def silu(mine, theirs, bias, cotangent, n_filt):
    rows, own, width = cotangent.shape
    return pl.pallas_call(
        functools.partial(silu_kernel, n_filt),
        out_shape=[jax.ShapeDtypeStruct((rows, own, width), jnp.bfloat16)]
        + [jax.ShapeDtypeStruct((rows // n_filt, own, width // 2), jnp.bfloat16)] * n_filt,
        in_specs=[VMEM] * 4,
        out_specs=[VMEM] * (1 + n_filt),
        compiler_params=params((cotangent.shape, 16)),
        cost_estimate=pl.CostEstimate(
            flops=10 * rows * own * width,
            bytes_accessed=13 * rows * own * width,
            transcendentals=rows * own * width,
        ),
    )(mine, theirs, bias, cotangent)


def shift_grads(grads, grad_out, row):
    own, width = grad_out.shape
    at = pl.ds(pl.multiple_of(row * width, width), width)
    grads[pl.ds(0, own), at] = move_columns(grad_out, -1)
    grads[pl.ds(own, own), at] = grad_out
    grads[pl.ds(2 * own, own), at] = move_columns(grad_out, 1)


def panel_copies(panel, blocks, n_filt, n_sp, sems):
    rows_dev, width, _ = blocks[0].shape
    copies = []
    for index, block in enumerate(blocks):
        place = block_place(index, n_filt, n_sp)
        for i in range(rows_dev):
            at = pl.multiple_of((place * rows_dev + i + 1) * width, width)
            to = panel.at[pl.ds(at, width), :]
            copies.append(pltpu.make_async_copy(block.at[i], to, sems.at[index * rows_dev + i]))
    return copies


def gradient_kernel(n_filt, n_sp, bias, own_grad, *refs):
    others, refs = refs[: 4 * (n_sp - 1)], refs[4 * (n_sp - 1) :]
    *blocks, weight_sum, bias_sum, formed = refs[: n_sp * n_filt + 3]
    grads, (panel, stage, sems, row_sems) = refs[-4 - n_sp : -4], refs[-4:]
    side_rows, own, width = own_grad.shape
    half_rows = side_rows // 2
    half = lax.axis_index("in")
    copies = panel_copies(panel, blocks, n_filt, n_sp, row_sems)
    for copy in copies:
        copy.start()
    zeros = jnp.zeros((width, panel.shape[1]), panel.dtype)
    panel[pl.ds(0, width), :] = zeros
    panel[pl.ds((n_sp * side_rows + 1) * width, width), :] = zeros
    for r in range(side_rows):
        shift_grads(grads[0], own_grad[r], r)
    for copy in copies:
        copy.wait()

    def tap_gradient(j, a):
        first = (behind("sp", n_sp, j) * side_rows + a) * width
        window = panel[pl.ds(pl.multiple_of(first, width), side_rows * width), :]
        return jnp.dot(grads[j][...], window, preferred_element_type=jnp.float32)

    def copy_out(a, b):
        return pltpu.make_async_copy(stage.at[a, b], weight_sum.at[a, b], sems.at[a, b])

    for a in range(3):
        stage[a] = tap_gradient(0, a).reshape(stage.shape[1:])
    for j in range(1, n_sp):
        mine, theirs, near, far = others[4 * (j - 1) : 4 * j]
        for h, cotangent in enumerate((near, far)):
            start = (half if h == 0 else 1 - half) * half_rows
            for r in range(half_rows):
                shifted = (mine[start + r] + theirs[start + r]) + bias[...]
                _, grad_out = silu_parts(shifted, cotangent[r])
                shift_grads(grads[j], grad_out, start + r)

    for a in range(3):
        for j in range(1, n_sp):
            product = tap_gradient(j, a)
            for b in range(3):
                stage[a, b] += product[b * own : (b + 1) * own]
                if j == n_sp - 1:
                    copy_out(a, b).start()

    total = jnp.zeros((16, own), jnp.float32)
    for side in grads:
        total += lax.dot_general(
            jnp.ones((16, side.shape[1]), side.dtype),
            side[pl.ds(own, own), :],
            (((1,), (1,)), ((), ())),
            preferred_element_type=jnp.float32,
        )
    bias_sum[...] = total[:1]
    formed[...] = jnp.zeros(formed.shape, formed.dtype)
    for a in range(3):
        for b in range(3):
            copy_out(a, b).wait()


def gradient(bias, own_grad, others, sides):
    n_sp, n_filt = len(sides), len(sides[0])
    blocks = [block for side in sides for block in side]
    side_rows, own, width = own_grad.shape
    depth = blocks[0].shape[2]
    all_rows = n_sp * side_rows
    panel = ((all_rows + 2) * width, depth)
    grads = (3 * own, side_rows * width)
    total = (3, 3, own, depth)
    return pl.pallas_call(
        functools.partial(gradient_kernel, n_filt, n_sp),
        out_shape=[
            jax.ShapeDtypeStruct(total, jnp.float32),
            jax.ShapeDtypeStruct((1, own), jnp.float32),
            jax.ShapeDtypeStruct((8, 128), jnp.float32),
        ],
        in_specs=[VMEM] * (2 + len(others)) + [ANY] * len(blocks),
        out_specs=[ANY, VMEM, VMEM],
        scratch_shapes=[
            *[pltpu.VMEM(grads, jnp.bfloat16)] * n_sp,
            pltpu.VMEM(panel, blocks[0].dtype),
            pltpu.VMEM(total, jnp.float32),
            pltpu.SemaphoreType.DMA((3, 3)),
            pltpu.SemaphoreType.DMA((all_rows,)),
        ],
        compiler_params=params(
            (grads, 2 * n_sp), (panel, 2), (total, 6), ((all_rows, own, width), 12)
        ),
        cost_estimate=pl.CostEstimate(
            flops=18 * all_rows * own * width * depth,
            bytes_accessed=36 * own * depth + 2 * all_rows * width * depth,
            transcendentals=all_rows * own * width,
        ),
    )(bias, own_grad, *others, *blocks)


def place_kernel(*refs):
    *pieces, _, output, sems = refs
    own = pieces[0].shape[1]
    copies = []
    for k, piece in enumerate(pieces):
        at = pl.multiple_of(behind("filt", len(pieces), k) * own, own)
        rows = output.at[:, pl.ds(at, own), :]
        copies.append(pltpu.make_async_copy(piece, rows, sems.at[k]))
    for copy in copies:
        copy.start()
    for copy in copies:
        copy.wait()


def place_pieces(pieces, after):
    rows, own, half = pieces[0].shape
    return pl.pallas_call(
        place_kernel,
        out_shape=jax.ShapeDtypeStruct((rows, len(pieces) * own, half), pieces[0].dtype),
        in_specs=[VMEM] * (len(pieces) + 1),
        out_specs=ANY,
        scratch_shapes=[pltpu.SemaphoreType.DMA((len(pieces),))],
        compiler_params=params((pieces[0].shape, 2 * len(pieces))),
        cost_estimate=pl.CostEstimate(
            flops=0, bytes_accessed=4 * len(pieces) * rows * own * half, transcendentals=0
        ),
    )(*pieces, after)


def on_device(image, weight, bias, cotangent):
    n_filt, n_sp = lax.axis_size("filt"), lax.axis_size("sp")
    side_rows = cotangent.shape[0]
    swap = shifted_ring("in", 1)

    gathered = gather_blocks(image)
    taps, bias_col = arrange(weight, bias, image.shape[2], [gathered[-1][0]])
    places = [[(j, k) for j in range(n_sp)] for k in range(n_filt)]
    first, second = places[: n_filt // 2], places[n_filt // 2 :]
    second[-1] = [(0, n_filt - 1)]
    begun = add_blocks(taps, gathered, first[0], side_rows)
    near = send_held(gathered, cotangent, [begun, gathered[0][-2]])
    for group in (sum(first[1:], []), sum(second[:-1], []), second[-1]):
        begun = add_blocks(taps, gathered, group, side_rows, [begun])

    partial = [last_rows(taps, begun, gathered, 0, side_rows)]
    for j in range(1, n_sp):
        partial.append(last_rows(taps, begun, gathered, j, side_rows, [near[j]]))
    other = [lax.ppermute(value, "in", swap) for value in partial]

    own_grad, *rows = silu(partial[0], other[0], bias_col, cotangent, n_filt)
    pieces = rows[:1]
    for k in range(1, n_filt):
        pieces.append(lax.ppermute(rows[k], "filt", shifted_ring("filt", k)))
    others = []
    for j in range(1, n_sp):
        others += [partial[j], other[j], near[j], lax.ppermute(near[j], "in", swap)]
    grad_weight, grad_bias, formed = gradient(bias_col, own_grad, others, gathered)
    output = place_pieces(pieces, formed)
    return (output, grad_weight, grad_bias.reshape(-1))


def solution(mesh):
    placed = (
        P(("groups", "sp", "filt"), None, "in"),
        P(None, None, "filt", None),
        P("filt"),
        P(("groups", "sp"), "filt", None),
    )
    return jax.shard_map(
        on_device,
        mesh=mesh,
        in_specs=placed,
        out_specs=(
            P(("groups", "sp", "filt"), None, "in"),
            P("groups", None, "filt", "in"),
            P(("groups", "filt")),
        ),
        check_vma=False,
    )
```

```python
import functools
import math

import jax
import jax.numpy as jnp
from jax import lax
from jax.experimental import pallas as pl
from jax.experimental.pallas import tpu as pltpu
from jax.sharding import PartitionSpec as P

MIB = 1024 * 1024


def params(*arrays):
    held = sum(math.prod(shape) * size for shape, size in arrays)
    return pltpu.CompilerParams(vmem_limit_bytes=max(20 * MIB, held * 5 // 4 + 8 * MIB))


def shifted_ring(axis, shift):
    size = lax.axis_size(axis)
    return [(i, (i + shift) % size) for i in range(size)]


def folded_ring(axis, shift):
    size = lax.axis_size(axis)
    order = [0, *range(1, size, 2), *reversed(range(2, size, 2))]
    return [(order[i], order[(i + shift) % size]) for i in range(size)]


def folded_behind(axis, size, by):
    index = lax.axis_index(axis)
    back = size - lax.div(index, 2)
    place = jnp.where(lax.rem(index, 2) == 1, lax.div(index + 1, 2), lax.rem(back, size))
    place = lax.rem(place + (size - by), size)
    out = 2 * place - 1
    return jnp.where(place == 0, 0, jnp.where(place <= size // 2, out, 2 * (size - place)))


def gather_blocks(image):
    n_filt, n_sp = lax.axis_size("filt"), lax.axis_size("sp")
    onward, outward = shifted_ring("sp", 1), folded_ring("filt", 1)
    blocks = [[None] * n_filt for _ in range(n_sp)]
    blocks[0][0] = image
    last = n_filt - 1
    for k in range(n_filt):
        if k:
            blocks[0][k] = lax.ppermute(blocks[0][k - 1], "filt", outward)
        for j in range(1, n_sp):
            if k < max(last, 1):
                blocks[j][k] = lax.ppermute(blocks[j - 1][k], "sp", onward)
    return blocks


def send_held(blocks, cotangent, after):
    n_filt, n_sp = len(blocks[0]), len(blocks)
    first = [side[0] for side in blocks[1:]]
    half, *first = hold(cotangent, first, after)
    halves = [half]
    for j in range(1, n_sp):
        if n_filt > 1:
            blocks[j][-1] = lax.ppermute(first[j - 1], "filt", folded_ring("filt", -1))
        halves.append(lax.ppermute(halves[-1], "sp", shifted_ring("sp", 1)))
    return halves


def move_columns(values, by):
    size = values.shape[1]
    column = lax.broadcasted_iota(jnp.int32, values.shape, 1)
    edge = 0 if by == 1 else size - 1
    return jnp.where(column == edge, jnp.zeros_like(values), pltpu.roll(values, by % size, 1))


VMEM = pl.BlockSpec(memory_space=pltpu.VMEM)
ANY = pl.BlockSpec(memory_space=pl.ANY)


def behind(axis, size, by):
    return lax.rem(lax.axis_index(axis) + (size - by), size)


def hold_kernel(n_blocks, n_after, cotangent, *refs):
    blocks, (half, *copies, sems) = refs[:n_blocks], refs[n_blocks + n_after :]
    rows = half.shape[0]
    moves = [(cotangent.at[pl.ds(lax.axis_index("in") * rows, rows)], half)]
    moves += zip(blocks, copies)
    moves = [pltpu.make_async_copy(*move, sems.at[i]) for i, move in enumerate(moves)]
    for move in moves:
        move.start()
    for move in moves:
        move.wait()


def hold(cotangent, blocks, after):
    shape = (cotangent.shape[0] // 2,) + cotangent.shape[1:]
    held = [jax.ShapeDtypeStruct(block.shape, block.dtype) for block in blocks]
    return pl.pallas_call(
        functools.partial(hold_kernel, len(blocks), len(after)),
        out_shape=[jax.ShapeDtypeStruct(shape, cotangent.dtype), *held],
        in_specs=[ANY] * (1 + len(blocks) + len(after)),
        out_specs=[VMEM] * (1 + len(blocks)),
        scratch_shapes=[pltpu.SemaphoreType.DMA((1 + len(blocks),))],
        compiler_params=params((shape, 2), *((block.shape, 2) for block in blocks)),
        cost_estimate=pl.CostEstimate(
            flops=0, bytes_accessed=4 * math.prod(shape), transcendentals=0
        ),
    )(cotangent, *blocks, *after)


def arrange_kernel(weight, bias, *refs):
    taps, bias_col, sems = refs[-3:]
    depth = taps.shape[1] // 3
    own = weight.shape[2]
    half = lax.axis_index("in")
    copies = [
        pltpu.make_async_copy(
            weight.at[a, b, :, pl.ds(pl.multiple_of(half * depth, depth), depth)],
            taps.at[pl.ds(a * own, own), pl.ds(b * depth, depth)],
            sems.at[a * 3 + b],
        )
        for a in range(3)
        for b in range(3)
    ]
    for copy in copies:
        copy.start()
    bias_col[...] = jnp.broadcast_to(bias[...], (128, own)).T[:, :1]
    for copy in copies:
        copy.wait()


def arrange(weight, bias, depth, after):
    own = weight.shape[2]
    shape = (3 * own, 3 * depth)
    return pl.pallas_call(
        arrange_kernel,
        out_shape=(
            jax.ShapeDtypeStruct(shape, weight.dtype),
            jax.ShapeDtypeStruct((own, 1), bias.dtype),
        ),
        in_specs=[ANY, VMEM] + [ANY] * len(after),
        out_specs=(VMEM, VMEM),
        scratch_shapes=[pltpu.SemaphoreType.DMA((9,))],
        compiler_params=params((shape, 2)),
        cost_estimate=pl.CostEstimate(
            flops=0, bytes_accessed=36 * own * depth, transcendentals=0
        ),
    )(weight, bias.reshape(1, own), *after)


def block_place(index, n_filt, n_sp):
    j, k = divmod(index, n_filt)
    return behind("sp", n_sp, j) * n_filt + folded_behind("filt", n_filt, k)


def turn_row(turned, row):
    values = row.T
    depth = values.shape[0]
    turned[pl.ds(0, depth), :] = move_columns(values, 1)
    turned[pl.ds(depth, depth), :] = values
    turned[pl.ds(2 * depth, depth), :] = move_columns(values, -1)


def add_row(total, slot, taps, row, turned):
    own = taps.shape[0] // 3
    turn_row(turned, row)
    product = jnp.dot(taps[...], turned[...], preferred_element_type=jnp.float32)
    for a in range(3):
        total[slot + 1 - a] += product[a * own : (a + 1) * own]


def add_blocks_kernel(where, n_filt, n_sp, fresh, taps, *refs):
    *blocks, total, turned = refs if fresh else refs[1:]
    rows_dev = blocks[0].shape[0]
    total[...] = jnp.zeros(total.shape, total.dtype) if fresh else refs[0][...]
    for index, (block, (j, k)) in enumerate(zip(blocks, where)):
        place = block_place(j * n_filt + k, n_filt, n_sp)
        for i in range(rows_dev):
            at = index * rows_dev + i
            add_row(total, place * rows_dev + i + 1, taps, block[i], turned.at[at])


def add_blocks(taps, sides, where, side_rows, begun=()):
    n_sp, n_filt = len(sides), len(sides[0])
    blocks = [sides[j][k] for j, k in where]
    rows_dev, width, depth = blocks[0].shape
    own = taps.shape[0] // 3
    shape = (n_sp * side_rows + 2, own, width)
    turned = (len(blocks) * rows_dev, 3 * depth, width)
    return pl.pallas_call(
        functools.partial(add_blocks_kernel, where, n_filt, n_sp, not begun),
        out_shape=jax.ShapeDtypeStruct(shape, jnp.float32),
        in_specs=[VMEM] * (1 + len(begun) + len(blocks)),
        out_specs=VMEM,
        scratch_shapes=[pltpu.VMEM(turned, blocks[0].dtype)],
        compiler_params=params((turned, 2), (shape, 8), (taps.shape, 4)),
        cost_estimate=pl.CostEstimate(
            flops=(1 if begun else 30) * len(blocks) * rows_dev * own * width * depth,
            bytes_accessed=1,
            transcendentals=0,
        ),
    )(taps, *begun, *blocks)


def row_terms_kernel(taps, block, _, terms, turned):
    own = taps.shape[0] // 3
    for i in range(block.shape[0]):
        turn_row(turned.at[i], block[i])
        product = jnp.dot(taps[...], turned[i], preferred_element_type=jnp.float32)
        for a in range(3):
            terms[i, a] = product[a * own : (a + 1) * own]


def row_terms(taps, block, after):
    rows_dev, width, depth = block.shape
    own = taps.shape[0] // 3
    shape = (rows_dev, 3, own, width)
    turned = (rows_dev, 3 * depth, width)
    return pl.pallas_call(
        row_terms_kernel,
        out_shape=jax.ShapeDtypeStruct(shape, jnp.float32),
        in_specs=[VMEM, VMEM, ANY],
        out_specs=VMEM,
        scratch_shapes=[pltpu.VMEM(turned, block.dtype)],
        compiler_params=params((turned, 3), (shape, 8), (taps.shape, 4)),
        cost_estimate=pl.CostEstimate(
            flops=18 * rows_dev * own * width * depth, bytes_accessed=1, transcendentals=0
        ),
    )(taps, block, after)


def last_rows_kernel(n_filt, n_sp, j, n_after, taps, begun, terms, *refs):
    *blocks, out, total, turned = refs[n_after:]
    rows_dev = blocks[0].shape[0]
    side_rows, own = total.shape[0] - 2, total.shape[1]
    side = behind("sp", n_sp, j)
    total[...] = begun[pl.ds(side * side_rows, side_rows + 2)]
    first = block_place(n_filt - 1, n_filt, n_sp) * rows_dev - side * side_rows + 1
    for i in range(rows_dev):
        for a in range(3):
            slot = first + i + 1 - a

            @pl.when((slot >= 0) & (slot < side_rows + 2))
            def _():
                total[slot] += terms[i, a]

    def slot_of(other):
        place = block_place(other * n_filt + n_filt - 1, n_filt, n_sp)
        return place * rows_dev - side * side_rows + 1

    for other, block in enumerate(blocks, 1):
        for i in range(rows_dev):
            if other == j:
                add_row(total, slot_of(other) + i, taps, block[i], turned.at[i])
        if other != j:
            for i, at, edge, a in ((rows_dev - 1, 0, 1, 0), (0, side_rows + 1, side_rows, 2)):

                @pl.when(slot_of(other) + i == at)
                def _():
                    turn_row(turned.at[0], block[i])
                    rows = taps[pl.ds(a * own, own), :]
                    product = jnp.dot(rows, turned[0], preferred_element_type=jnp.float32)
                    total[edge] += product

    out[...] = total[pl.ds(1, side_rows)]


def last_rows(taps, begun, terms, sides, j, side_rows, after=()):
    n_sp, n_filt = len(sides), len(sides[0])
    blocks = [side[-1] for side in sides[1:]]
    rows_dev, width, depth = blocks[0].shape
    own = taps.shape[0] // 3
    out = (side_rows, own, width)
    total = (side_rows + 2, own, width)
    turned = (rows_dev, 3 * depth, width)
    return pl.pallas_call(
        functools.partial(last_rows_kernel, n_filt, n_sp, j, len(after)),
        out_shape=jax.ShapeDtypeStruct(out, jnp.float32),
        in_specs=[VMEM] * 3 + [ANY] * len(after) + [VMEM] * len(blocks),
        out_specs=VMEM,
        scratch_shapes=[
            pltpu.VMEM(total, jnp.float32),
            pltpu.VMEM(turned, blocks[0].dtype),
        ],
        compiler_params=params(
            (turned, 2 + n_sp), (total, 12), (begun.shape, 4), (taps.shape, 4), (terms.shape, 4)
        ),
        cost_estimate=pl.CostEstimate(
            flops=18 * rows_dev * own * width * depth,
            bytes_accessed=18 * own * depth,
            transcendentals=0,
        ),
    )(taps, begun, terms, *after, *blocks)


def silu_parts(shifted, cotangent):
    sigmoid_v = 0.5 * jnp.tanh(0.5 * shifted) + 0.5
    slope = sigmoid_v * (1.0 + shifted * (1.0 - sigmoid_v))
    grad_out = (cotangent.astype(jnp.float32) * slope).astype(jnp.bfloat16)
    return sigmoid_v, grad_out


def silu_kernel(n_filt, mine, theirs, bias, cotangent, grad_out, *activated):
    rows, _, half = activated[0].shape

    for k in range(n_filt):
        first = behind("filt", n_filt, n_filt - k if k else 0) * rows

        @pl.loop(0, rows)
        def _(i):
            r = first + i
            shifted = (mine[r] + theirs[r]) + bias[...]
            sigmoid_v, grad_out[r] = silu_parts(shifted, cotangent[r])
            value = (shifted * sigmoid_v).astype(activated[k].dtype)
            activated[k][i] = jnp.where(
                lax.axis_index("in") == 0, value[:, :half], value[:, half:]
            )


def silu(mine, theirs, bias, cotangent, n_filt):
    rows, own, width = cotangent.shape
    return pl.pallas_call(
        functools.partial(silu_kernel, n_filt),
        out_shape=[jax.ShapeDtypeStruct((rows, own, width), jnp.bfloat16)]
        + [jax.ShapeDtypeStruct((rows // n_filt, own, width // 2), jnp.bfloat16)] * n_filt,
        in_specs=[VMEM] * 4,
        out_specs=[VMEM] * (1 + n_filt),
        compiler_params=params((cotangent.shape, 16)),
        cost_estimate=pl.CostEstimate(
            flops=10 * rows * own * width,
            bytes_accessed=13 * rows * own * width,
            transcendentals=rows * own * width,
        ),
    )(mine, theirs, bias, cotangent)


def shift_grads(grads, grad_out, row):
    own, width = grad_out.shape
    at = pl.ds(pl.multiple_of(row * width, width), width)
    grads[pl.ds(0, own), at] = move_columns(grad_out, -1)
    grads[pl.ds(own, own), at] = grad_out
    grads[pl.ds(2 * own, own), at] = move_columns(grad_out, 1)


def panel_copies(panel, blocks, n_filt, n_sp, sems):
    rows_dev, width, _ = blocks[0].shape
    copies = []
    for index, block in enumerate(blocks):
        place = block_place(index, n_filt, n_sp)
        for i in range(rows_dev):
            at = pl.multiple_of((place * rows_dev + i + 1) * width, width)
            to = panel.at[pl.ds(at, width), :]
            copies.append(pltpu.make_async_copy(block.at[i], to, sems.at[index * rows_dev + i]))
    return copies


def gradient_kernel(n_filt, n_sp, bias, own_grad, *refs):
    others, refs = refs[: 4 * (n_sp - 1)], refs[4 * (n_sp - 1) :]
    *blocks, weight_sum, bias_sum, formed = refs[: n_sp * n_filt + 3]
    grads, (panel, stage, sems, row_sems) = refs[-4 - n_sp : -4], refs[-4:]
    side_rows, own, width = own_grad.shape
    half_rows = side_rows // 2
    half = lax.axis_index("in")
    copies = panel_copies(panel, blocks, n_filt, n_sp, row_sems)
    for copy in copies:
        copy.start()
    zeros = jnp.zeros((width, panel.shape[1]), panel.dtype)
    panel[pl.ds(0, width), :] = zeros
    panel[pl.ds((n_sp * side_rows + 1) * width, width), :] = zeros
    for r in range(side_rows):
        shift_grads(grads[0], own_grad[r], r)
    for copy in copies:
        copy.wait()

    def tap_gradient(j, a):
        first = (behind("sp", n_sp, j) * side_rows + a) * width
        window = panel[pl.ds(pl.multiple_of(first, width), side_rows * width), :]
        return jnp.dot(grads[j][...], window, preferred_element_type=jnp.float32)

    def copy_out(a, b):
        return pltpu.make_async_copy(stage.at[a, b], weight_sum.at[a, b], sems.at[a, b])

    stage[0] = tap_gradient(0, 0).reshape(stage.shape[1:])
    for j in range(1, n_sp):
        mine, theirs, near, far = others[4 * (j - 1) : 4 * j]
        for h, cotangent in enumerate((near, far)):
            start = (half if h == 0 else 1 - half) * half_rows
            for r in range(half_rows):
                shifted = (mine[start + r] + theirs[start + r]) + bias[...]
                _, grad_out = silu_parts(shifted, cotangent[r])
                shift_grads(grads[j], grad_out, start + r)

    for a in range(3):
        product = tap_gradient(1, a)
        for j in [*([0] if a else []), *range(2, n_sp)]:
            product += tap_gradient(j, a)
        for b in range(3):
            term = product[b * own : (b + 1) * own]
            stage[a, b] = term if a else stage[a, b] + term
            copy_out(a, b).start()

    total = jnp.zeros((16, own), jnp.float32)
    for side in grads:
        total += lax.dot_general(
            jnp.ones((16, side.shape[1]), side.dtype),
            side[pl.ds(own, own), :],
            (((1,), (1,)), ((), ())),
            preferred_element_type=jnp.float32,
        )
    bias_sum[...] = total[:1]
    formed[...] = jnp.zeros(formed.shape, formed.dtype)
    for a in range(3):
        for b in range(3):
            copy_out(a, b).wait()


def gradient(bias, own_grad, others, sides):
    n_sp, n_filt = len(sides), len(sides[0])
    blocks = [block for side in sides for block in side]
    side_rows, own, width = own_grad.shape
    depth = blocks[0].shape[2]
    all_rows = n_sp * side_rows
    panel = ((all_rows + 2) * width, depth)
    grads = (3 * own, side_rows * width)
    total = (3, 3, own, depth)
    return pl.pallas_call(
        functools.partial(gradient_kernel, n_filt, n_sp),
        out_shape=[
            jax.ShapeDtypeStruct(total, jnp.float32),
            jax.ShapeDtypeStruct((1, own), jnp.float32),
            jax.ShapeDtypeStruct((8, 128), jnp.float32),
        ],
        in_specs=[VMEM] * (2 + len(others)) + [ANY] * len(blocks),
        out_specs=[ANY, VMEM, VMEM],
        scratch_shapes=[
            *[pltpu.VMEM(grads, jnp.bfloat16)] * n_sp,
            pltpu.VMEM(panel, blocks[0].dtype),
            pltpu.VMEM(total, jnp.float32),
            pltpu.SemaphoreType.DMA((3, 3)),
            pltpu.SemaphoreType.DMA((all_rows,)),
        ],
        compiler_params=params(
            (grads, 2 * n_sp), (panel, 2), (total, 6), ((all_rows, own, width), 12)
        ),
        cost_estimate=pl.CostEstimate(
            flops=18 * all_rows * own * width * depth,
            bytes_accessed=36 * own * depth + 2 * all_rows * width * depth,
            transcendentals=all_rows * own * width,
        ),
    )(bias, own_grad, *others, *blocks)


def place_kernel(*refs):
    *pieces, _, output, sems = refs
    own = pieces[0].shape[1]
    copies = []
    for k, piece in enumerate(pieces):
        at = pl.multiple_of(behind("filt", len(pieces), k) * own, own)
        rows = output.at[:, pl.ds(at, own), :]
        copies.append(pltpu.make_async_copy(piece, rows, sems.at[k]))
    for copy in copies:
        copy.start()
    for copy in copies:
        copy.wait()


def place_pieces(pieces, after):
    rows, own, half = pieces[0].shape
    return pl.pallas_call(
        place_kernel,
        out_shape=jax.ShapeDtypeStruct((rows, len(pieces) * own, half), pieces[0].dtype),
        in_specs=[VMEM] * (len(pieces) + 1),
        out_specs=ANY,
        scratch_shapes=[pltpu.SemaphoreType.DMA((len(pieces),))],
        compiler_params=params((pieces[0].shape, 2 * len(pieces))),
        cost_estimate=pl.CostEstimate(
            flops=0, bytes_accessed=4 * len(pieces) * rows * own * half, transcendentals=0
        ),
    )(*pieces, after)


def on_device(image, weight, bias, cotangent):
    n_filt, n_sp = lax.axis_size("filt"), lax.axis_size("sp")
    side_rows = cotangent.shape[0]
    swap = shifted_ring("in", 1)

    gathered = gather_blocks(image)
    taps, bias_col = arrange(weight, bias, image.shape[2], [gathered[-1][0]])
    places = [[(j, k) for j in range(n_sp)] for k in range(n_filt)]
    first, second = places[: n_filt // 2], places[n_filt // 2 :]
    begun = add_blocks(taps, gathered, first[0], side_rows)
    near = send_held(gathered, cotangent, [begun, gathered[0][-2]])
    for group in (sum(first[1:], []), sum(second[:-1], [])):
        begun = add_blocks(taps, gathered, group, side_rows, [begun])

    terms = row_terms(taps, gathered[0][-1], begun)
    partial = [last_rows(taps, begun, terms, gathered, 0, side_rows)]
    for j in range(1, n_sp):
        partial.append(last_rows(taps, begun, terms, gathered, j, side_rows, [near[j]]))
    other = [lax.ppermute(value, "in", swap) for value in partial]

    own_grad, *rows = silu(partial[0], other[0], bias_col, cotangent, n_filt)
    pieces = rows[:1]
    for k in range(1, n_filt):
        pieces.append(lax.ppermute(rows[k], "filt", shifted_ring("filt", k)))
    others = []
    for j in range(1, n_sp):
        others += [partial[j], other[j], near[j], lax.ppermute(near[j], "in", swap)]
    grad_weight, grad_bias, formed = gradient(bias_col, own_grad, others, gathered)
    output = place_pieces(pieces, formed)
    return (output, grad_weight, grad_bias.reshape(-1))


def solution(mesh):
    placed = (
        P(("groups", "sp", "filt"), None, "in"),
        P(None, None, "filt", None),
        P("filt"),
        P(("groups", "sp"), "filt", None),
    )
    return jax.shard_map(
        on_device,
        mesh=mesh,
        in_specs=placed,
        out_specs=(
            P(("groups", "sp", "filt"), None, "in"),
            P("groups", None, "filt", "in"),
            P(("groups", "filt")),
        ),
        check_vma=False,
    )
```

```python
import functools
import math

import jax
import jax.numpy as jnp
from jax import lax
from jax.experimental import pallas as pl
from jax.experimental.pallas import tpu as pltpu
from jax.sharding import PartitionSpec as P

MIB = 1024 * 1024


def params(*arrays):
    held = sum(math.prod(shape) * size for shape, size in arrays)
    return pltpu.CompilerParams(vmem_limit_bytes=max(20 * MIB, held * 5 // 4 + 8 * MIB))


def shifted_ring(axis, shift):
    size = lax.axis_size(axis)
    return [(i, (i + shift) % size) for i in range(size)]


def exchange_masks(size):
    return [k ^ (k >> 1) for k in range(size)]


def folded_ring(axis, shift):
    size = lax.axis_size(axis)
    order = [0, *range(1, size, 2), *reversed(range(2, size, 2))]
    return [(order[i], order[(i + shift) % size]) for i in range(size)]


def folded_behind(axis, size, by):
    index = lax.axis_index(axis)
    back = size - lax.div(index, 2)
    place = jnp.where(lax.rem(index, 2) == 1, lax.div(index + 1, 2), lax.rem(back, size))
    place = lax.rem(place + (size - by), size)
    out = 2 * place - 1
    return jnp.where(place == 0, 0, jnp.where(place <= size // 2, out, 2 * (size - place)))


def gather_blocks(image):
    n_filt, n_sp = lax.axis_size("filt"), lax.axis_size("sp")
    onward, outward = shifted_ring("sp", 1), folded_ring("filt", 1)
    blocks = [[None] * n_filt for _ in range(n_sp)]
    blocks[0][0] = image
    last = n_filt - 1
    for k in range(n_filt):
        if k:
            blocks[0][k] = lax.ppermute(blocks[0][k - 1], "filt", outward)
        for j in range(1, n_sp):
            if k < max(last, 1):
                blocks[j][k] = lax.ppermute(blocks[j - 1][k], "sp", onward)
    return blocks


def send_held(blocks, cotangent, after):
    n_filt, n_sp = len(blocks[0]), len(blocks)
    first = [side[0] for side in blocks[1:]]
    half, *first = hold(cotangent, first, after)
    halves = [half]
    for j in range(1, n_sp):
        if n_filt > 1:
            blocks[j][-1] = lax.ppermute(first[j - 1], "filt", folded_ring("filt", -1))
        halves.append(lax.ppermute(halves[-1], "sp", shifted_ring("sp", 1)))
    return halves


def move_columns(values, by):
    size = values.shape[1]
    column = lax.broadcasted_iota(jnp.int32, values.shape, 1)
    edge = 0 if by == 1 else size - 1
    return jnp.where(column == edge, jnp.zeros_like(values), pltpu.roll(values, by % size, 1))


VMEM = pl.BlockSpec(memory_space=pltpu.VMEM)
ANY = pl.BlockSpec(memory_space=pl.ANY)


def behind(axis, size, by):
    return lax.rem(lax.axis_index(axis) + (size - by), size)


def hold_kernel(n_blocks, n_after, cotangent, *refs):
    blocks, (half, *copies, sems) = refs[:n_blocks], refs[n_blocks + n_after :]
    rows = half.shape[0]
    moves = [(cotangent.at[pl.ds(lax.axis_index("in") * rows, rows)], half)]
    moves += zip(blocks, copies)
    moves = [pltpu.make_async_copy(*move, sems.at[i]) for i, move in enumerate(moves)]
    for move in moves:
        move.start()
    for move in moves:
        move.wait()


def hold(cotangent, blocks, after):
    shape = (cotangent.shape[0] // 2,) + cotangent.shape[1:]
    held = [jax.ShapeDtypeStruct(block.shape, block.dtype) for block in blocks]
    return pl.pallas_call(
        functools.partial(hold_kernel, len(blocks), len(after)),
        out_shape=[jax.ShapeDtypeStruct(shape, cotangent.dtype), *held],
        in_specs=[ANY] * (1 + len(blocks) + len(after)),
        out_specs=[VMEM] * (1 + len(blocks)),
        scratch_shapes=[pltpu.SemaphoreType.DMA((1 + len(blocks),))],
        compiler_params=params((shape, 2), *((block.shape, 2) for block in blocks)),
        cost_estimate=pl.CostEstimate(
            flops=0, bytes_accessed=4 * math.prod(shape), transcendentals=0
        ),
    )(cotangent, *blocks, *after)


def arrange_kernel(weight, bias, *refs):
    taps, bias_col, sems = refs[-3:]
    depth = taps.shape[1] // 3
    own = weight.shape[2]
    half = lax.axis_index("in")
    copies = [
        pltpu.make_async_copy(
            weight.at[a, b, :, pl.ds(pl.multiple_of(half * depth, depth), depth)],
            taps.at[pl.ds(a * own, own), pl.ds(b * depth, depth)],
            sems.at[a * 3 + b],
        )
        for a in range(3)
        for b in range(3)
    ]
    for copy in copies:
        copy.start()
    bias_col[...] = jnp.broadcast_to(bias[...], (128, own)).T[:, :1]
    for copy in copies:
        copy.wait()


def arrange(weight, bias, depth, after):
    own = weight.shape[2]
    shape = (3 * own, 3 * depth)
    return pl.pallas_call(
        arrange_kernel,
        out_shape=(
            jax.ShapeDtypeStruct(shape, weight.dtype),
            jax.ShapeDtypeStruct((own, 1), bias.dtype),
        ),
        in_specs=[ANY, VMEM] + [ANY] * len(after),
        out_specs=(VMEM, VMEM),
        scratch_shapes=[pltpu.SemaphoreType.DMA((9,))],
        compiler_params=params((shape, 2)),
        cost_estimate=pl.CostEstimate(
            flops=0, bytes_accessed=36 * own * depth, transcendentals=0
        ),
    )(weight, bias.reshape(1, own), *after)


def block_place(index, n_filt, n_sp):
    j, k = divmod(index, n_filt)
    return behind("sp", n_sp, j) * n_filt + folded_behind("filt", n_filt, k)


def turn_row(turned, row):
    values = row.T
    depth = values.shape[0]
    turned[pl.ds(0, depth), :] = move_columns(values, 1)
    turned[pl.ds(depth, depth), :] = values
    turned[pl.ds(2 * depth, depth), :] = move_columns(values, -1)


def add_row(total, slot, taps, row, turned):
    own = taps.shape[0] // 3
    turn_row(turned, row)
    product = jnp.dot(taps[...], turned[...], preferred_element_type=jnp.float32)
    for a in range(3):
        total[slot + 1 - a] += product[a * own : (a + 1) * own]


def add_blocks_kernel(where, n_filt, n_sp, fresh, taps, *refs):
    *blocks, total, turned = refs if fresh else refs[1:]
    rows_dev = blocks[0].shape[0]
    total[...] = jnp.zeros(total.shape, total.dtype) if fresh else refs[0][...]
    for index, (block, (j, k)) in enumerate(zip(blocks, where)):
        place = block_place(j * n_filt + k, n_filt, n_sp)
        for i in range(rows_dev):
            at = index * rows_dev + i
            add_row(total, place * rows_dev + i + 1, taps, block[i], turned.at[at])


def add_blocks(taps, sides, where, side_rows, begun=()):
    n_sp, n_filt = len(sides), len(sides[0])
    blocks = [sides[j][k] for j, k in where]
    rows_dev, width, depth = blocks[0].shape
    own = taps.shape[0] // 3
    shape = (n_sp * side_rows + 2, own, width)
    turned = (len(blocks) * rows_dev, 3 * depth, width)
    return pl.pallas_call(
        functools.partial(add_blocks_kernel, where, n_filt, n_sp, not begun),
        out_shape=jax.ShapeDtypeStruct(shape, jnp.float32),
        in_specs=[VMEM] * (1 + len(begun) + len(blocks)),
        out_specs=VMEM,
        scratch_shapes=[pltpu.VMEM(turned, blocks[0].dtype)],
        compiler_params=params((turned, 2), (shape, 8), (taps.shape, 4)),
        cost_estimate=pl.CostEstimate(
            flops=(1 if begun else 30) * len(blocks) * rows_dev * own * width * depth,
            bytes_accessed=1,
            transcendentals=0,
        ),
    )(taps, *begun, *blocks)


def last_rows_kernel(n_filt, n_sp, j, n_after, taps, begun, *refs):
    *blocks, out, total, turned = refs[n_after:]
    rows_dev = blocks[0].shape[0]
    side_rows, own = total.shape[0] - 2, total.shape[1]
    side = behind("sp", n_sp, j)
    total[...] = begun[pl.ds(side * side_rows, side_rows + 2)]

    def slot_of(other):
        place = block_place(other * n_filt + n_filt - 1, n_filt, n_sp)
        return place * rows_dev - side * side_rows + 1

    for other, block in enumerate(blocks, 1):
        for i in range(rows_dev):
            if other == j:
                add_row(total, slot_of(other) + i, taps, block[i], turned.at[i])
        if other != j:
            for i, at, edge, a in ((rows_dev - 1, 0, 1, 0), (0, side_rows + 1, side_rows, 2)):

                @pl.when(slot_of(other) + i == at)
                def _():
                    turn_row(turned.at[0], block[i])
                    rows = taps[pl.ds(a * own, own), :]
                    product = jnp.dot(rows, turned[0], preferred_element_type=jnp.float32)
                    total[edge] += product

    out[...] = total[pl.ds(1, side_rows)]


def last_rows(taps, begun, sides, j, side_rows, after=()):
    n_sp, n_filt = len(sides), len(sides[0])
    blocks = [side[-1] for side in sides[1:]]
    rows_dev, width, depth = blocks[0].shape
    own = taps.shape[0] // 3
    out = (side_rows, own, width)
    total = (side_rows + 2, own, width)
    turned = (rows_dev, 3 * depth, width)
    return pl.pallas_call(
        functools.partial(last_rows_kernel, n_filt, n_sp, j, len(after)),
        out_shape=jax.ShapeDtypeStruct(out, jnp.float32),
        in_specs=[VMEM] * 2 + [ANY] * len(after) + [VMEM] * len(blocks),
        out_specs=VMEM,
        scratch_shapes=[
            pltpu.VMEM(total, jnp.float32),
            pltpu.VMEM(turned, blocks[0].dtype),
        ],
        compiler_params=params(
            (turned, 2 + n_sp), (total, 12), (begun.shape, 4), (taps.shape, 4)
        ),
        cost_estimate=pl.CostEstimate(
            flops=18 * rows_dev * own * width * depth,
            bytes_accessed=18 * own * depth,
            transcendentals=0,
        ),
    )(taps, begun, *after, *blocks)


def silu_parts(shifted, cotangent):
    sigmoid_v = 0.5 * jnp.tanh(0.5 * shifted) + 0.5
    slope = sigmoid_v * (1.0 + shifted * (1.0 - sigmoid_v))
    grad_out = (cotangent.astype(jnp.float32) * slope).astype(jnp.bfloat16)
    return sigmoid_v, grad_out


def silu_kernel(n_filt, mine, theirs, bias, cotangent, grad_out, *activated):
    rows, _, half = activated[0].shape

    for k, mask in enumerate(exchange_masks(n_filt)):
        first = lax.bitwise_xor(lax.axis_index("filt"), jnp.int32(mask)) * rows

        @pl.loop(0, rows)
        def _(i):
            r = first + i
            shifted = (mine[r] + theirs[r]) + bias[...]
            sigmoid_v, grad_out[r] = silu_parts(shifted, cotangent[r])
            value = (shifted * sigmoid_v).astype(activated[k].dtype)
            activated[k][i] = jnp.where(
                lax.axis_index("in") == 0, value[:, :half], value[:, half:]
            )


def silu(mine, theirs, bias, cotangent, n_filt):
    rows, own, width = cotangent.shape
    return pl.pallas_call(
        functools.partial(silu_kernel, n_filt),
        out_shape=[jax.ShapeDtypeStruct((rows, own, width), jnp.bfloat16)]
        + [jax.ShapeDtypeStruct((rows // n_filt, own, width // 2), jnp.bfloat16)] * n_filt,
        in_specs=[VMEM] * 4,
        out_specs=[VMEM] * (1 + n_filt),
        compiler_params=params((cotangent.shape, 16)),
        cost_estimate=pl.CostEstimate(
            flops=10 * rows * own * width,
            bytes_accessed=13 * rows * own * width,
            transcendentals=rows * own * width,
        ),
    )(mine, theirs, bias, cotangent)


def shift_grads(grads, grad_out, row):
    own, width = grad_out.shape
    at = pl.ds(pl.multiple_of(row * width, width), width)
    grads[pl.ds(0, own), at] = move_columns(grad_out, -1)
    grads[pl.ds(own, own), at] = grad_out
    grads[pl.ds(2 * own, own), at] = move_columns(grad_out, 1)


def panel_copies(panel, blocks, n_filt, n_sp, sems):
    rows_dev, width, _ = blocks[0].shape
    copies = []
    for index, block in enumerate(blocks):
        place = block_place(index, n_filt, n_sp)
        for i in range(rows_dev):
            at = pl.multiple_of((place * rows_dev + i + 1) * width, width)
            to = panel.at[pl.ds(at, width), :]
            copies.append(pltpu.make_async_copy(block.at[i], to, sems.at[index * rows_dev + i]))
    return copies


def gradient_kernel(n_filt, n_sp, bias, own_grad, *refs):
    others, refs = refs[: 4 * (n_sp - 1)], refs[4 * (n_sp - 1) :]
    *blocks, weight_sum, bias_sum, formed = refs[: n_sp * n_filt + 3]
    grads, (panel, stage, sems, row_sems) = refs[-4 - n_sp : -4], refs[-4:]
    side_rows, own, width = own_grad.shape
    half_rows = side_rows // 2
    half = lax.axis_index("in")
    copies = panel_copies(panel, blocks, n_filt, n_sp, row_sems)
    for copy in copies:
        copy.start()
    zeros = jnp.zeros((width, panel.shape[1]), panel.dtype)
    panel[pl.ds(0, width), :] = zeros
    panel[pl.ds((n_sp * side_rows + 1) * width, width), :] = zeros
    for r in range(side_rows):
        shift_grads(grads[0], own_grad[r], r)
    for copy in copies:
        copy.wait()

    def tap_gradient(j, a):
        first = (behind("sp", n_sp, j) * side_rows + a) * width
        window = panel[pl.ds(pl.multiple_of(first, width), side_rows * width), :]
        return jnp.dot(grads[j][...], window, preferred_element_type=jnp.float32)

    def copy_out(a, b):
        return pltpu.make_async_copy(stage.at[a, b], weight_sum.at[a, b], sems.at[a, b])

    for a in range(3):
        stage[a] = tap_gradient(0, a).reshape(stage.shape[1:])
    for j in range(1, n_sp):
        mine, theirs, near, far = others[4 * (j - 1) : 4 * j]
        for h, cotangent in enumerate((near, far)):
            start = (half if h == 0 else 1 - half) * half_rows
            for r in range(half_rows):
                shifted = (mine[start + r] + theirs[start + r]) + bias[...]
                _, grad_out = silu_parts(shifted, cotangent[r])
                shift_grads(grads[j], grad_out, start + r)

    for a in range(3):
        for j in range(1, n_sp):
            product = tap_gradient(j, a)
            for b in range(3):
                stage[a, b] += product[b * own : (b + 1) * own]
                if j == n_sp - 1:
                    copy_out(a, b).start()

    total = jnp.zeros((16, own), jnp.float32)
    for side in grads:
        total += lax.dot_general(
            jnp.ones((16, side.shape[1]), side.dtype),
            side[pl.ds(own, own), :],
            (((1,), (1,)), ((), ())),
            preferred_element_type=jnp.float32,
        )
    bias_sum[...] = total[:1]
    formed[...] = jnp.zeros(formed.shape, formed.dtype)
    for a in range(3):
        for b in range(3):
            copy_out(a, b).wait()


def gradient(bias, own_grad, others, sides):
    n_sp, n_filt = len(sides), len(sides[0])
    blocks = [block for side in sides for block in side]
    side_rows, own, width = own_grad.shape
    depth = blocks[0].shape[2]
    all_rows = n_sp * side_rows
    panel = ((all_rows + 2) * width, depth)
    grads = (3 * own, side_rows * width)
    total = (3, 3, own, depth)
    return pl.pallas_call(
        functools.partial(gradient_kernel, n_filt, n_sp),
        out_shape=[
            jax.ShapeDtypeStruct(total, jnp.float32),
            jax.ShapeDtypeStruct((1, own), jnp.float32),
            jax.ShapeDtypeStruct((8, 128), jnp.float32),
        ],
        in_specs=[VMEM] * (2 + len(others)) + [ANY] * len(blocks),
        out_specs=[ANY, VMEM, VMEM],
        scratch_shapes=[
            *[pltpu.VMEM(grads, jnp.bfloat16)] * n_sp,
            pltpu.VMEM(panel, blocks[0].dtype),
            pltpu.VMEM(total, jnp.float32),
            pltpu.SemaphoreType.DMA((3, 3)),
            pltpu.SemaphoreType.DMA((all_rows,)),
        ],
        compiler_params=params(
            (grads, 2 * n_sp), (panel, 2), (total, 6), ((all_rows, own, width), 12)
        ),
        cost_estimate=pl.CostEstimate(
            flops=18 * all_rows * own * width * depth,
            bytes_accessed=36 * own * depth + 2 * all_rows * width * depth,
            transcendentals=all_rows * own * width,
        ),
    )(bias, own_grad, *others, *blocks)


def place_kernel(*refs):
    *pieces, _, output, sems = refs
    own = pieces[0].shape[1]
    copies = []
    for k, mask in enumerate(exchange_masks(len(pieces))):
        piece = pieces[k]
        partner = lax.bitwise_xor(lax.axis_index("filt"), jnp.int32(mask))
        at = pl.multiple_of(partner * own, own)
        rows = output.at[:, pl.ds(at, own), :]
        copies.append(pltpu.make_async_copy(piece, rows, sems.at[k]))
    for copy in copies:
        copy.start()
    for copy in copies:
        copy.wait()


def place_pieces(pieces, after):
    rows, own, half = pieces[0].shape
    return pl.pallas_call(
        place_kernel,
        out_shape=jax.ShapeDtypeStruct((rows, len(pieces) * own, half), pieces[0].dtype),
        in_specs=[VMEM] * (len(pieces) + 1),
        out_specs=ANY,
        scratch_shapes=[pltpu.SemaphoreType.DMA((len(pieces),))],
        compiler_params=params((pieces[0].shape, 2 * len(pieces))),
        cost_estimate=pl.CostEstimate(
            flops=0, bytes_accessed=4 * len(pieces) * rows * own * half, transcendentals=0
        ),
    )(*pieces, after)


def on_device(image, weight, bias, cotangent):
    n_filt, n_sp = lax.axis_size("filt"), lax.axis_size("sp")
    side_rows = cotangent.shape[0]
    swap = shifted_ring("in", 1)

    gathered = gather_blocks(image)
    taps, bias_col = arrange(weight, bias, image.shape[2], [gathered[-1][0]])
    places = [[(j, k) for j in range(n_sp)] for k in range(n_filt)]
    first, second = places[: n_filt // 2], places[n_filt // 2 :]
    second[-1] = [(0, n_filt - 1)]
    begun = add_blocks(taps, gathered, first[0], side_rows)
    near = send_held(gathered, cotangent, [begun, gathered[0][-2]])
    for group in (sum(first[1:], []), sum(second[:-1], []), second[-1]):
        begun = add_blocks(taps, gathered, group, side_rows, [begun])

    partial = [last_rows(taps, begun, gathered, 0, side_rows)]
    for j in range(1, n_sp):
        partial.append(last_rows(taps, begun, gathered, j, side_rows, [near[j]]))
    other = [lax.ppermute(value, "in", swap) for value in partial]

    own_grad, *rows = silu(partial[0], other[0], bias_col, cotangent, n_filt)
    pieces = rows[:1]
    for row, mask in list(zip(rows, exchange_masks(n_filt)))[1:]:
        pairs = [(i, i ^ mask) for i in range(n_filt)]
        pieces.append(lax.ppermute(row, "filt", pairs))
    others = []
    for j in range(1, n_sp):
        others += [partial[j], other[j], near[j], lax.ppermute(near[j], "in", swap)]
    grad_weight, grad_bias, formed = gradient(bias_col, own_grad, others, gathered)
    output = place_pieces(pieces, formed)
    return (output, grad_weight, grad_bias.reshape(-1))


def solution(mesh):
    placed = (
        P(("groups", "sp", "filt"), None, "in"),
        P(None, None, "filt", None),
        P("filt"),
        P(("groups", "sp"), "filt", None),
    )
    return jax.shard_map(
        on_device,
        mesh=mesh,
        in_specs=placed,
        out_specs=(
            P(("groups", "sp", "filt"), None, "in"),
            P("groups", None, "filt", "in"),
            P(("groups", "filt")),
        ),
        check_vma=False,
    )
```

```python
import functools
import math

import jax
import jax.numpy as jnp
from jax import lax
from jax.experimental import pallas as pl
from jax.experimental.pallas import tpu as pltpu
from jax.sharding import PartitionSpec as P

MIB = 1024 * 1024


def params(*arrays):
    held = sum(math.prod(shape) * size for shape, size in arrays)
    return pltpu.CompilerParams(vmem_limit_bytes=max(20 * MIB, held * 5 // 4 + 8 * MIB))


def shifted_ring(axis, shift):
    size = lax.axis_size(axis)
    return [(i, (i + shift) % size) for i in range(size)]


def folded_ring(axis, shift):
    size = lax.axis_size(axis)
    order = [0, *range(1, size, 2), *reversed(range(2, size, 2))]
    return [(order[i], order[(i + shift) % size]) for i in range(size)]


def folded_behind(axis, size, by):
    index = lax.axis_index(axis)
    back = size - lax.div(index, 2)
    place = jnp.where(lax.rem(index, 2) == 1, lax.div(index + 1, 2), lax.rem(back, size))
    place = lax.rem(place + (size - by), size)
    out = 2 * place - 1
    return jnp.where(place == 0, 0, jnp.where(place <= size // 2, out, 2 * (size - place)))


def gather_blocks(image):
    n_filt, n_sp = lax.axis_size("filt"), lax.axis_size("sp")
    onward, outward = shifted_ring("sp", 1), folded_ring("filt", 1)
    blocks = [[None] * n_filt for _ in range(n_sp)]
    blocks[0][0] = image
    last = n_filt - 1
    for k in range(n_filt):
        if k:
            blocks[0][k] = lax.ppermute(blocks[0][k - 1], "filt", outward)
        for j in range(1, n_sp):
            if k < max(last, 1):
                blocks[j][k] = lax.ppermute(blocks[j - 1][k], "sp", onward)
    return blocks


def send_held(blocks, cotangent, after):
    n_filt, n_sp = len(blocks[0]), len(blocks)
    first = [side[0] for side in blocks[1:]]
    half, *first = hold(cotangent, first, after)
    halves = [half]
    for j in range(1, n_sp):
        if n_filt > 1:
            blocks[j][-1] = lax.ppermute(first[j - 1], "filt", folded_ring("filt", -1))
        halves.append(lax.ppermute(halves[-1], "sp", shifted_ring("sp", 1)))
    return halves


def move_columns(values, by):
    size = values.shape[1]
    column = lax.broadcasted_iota(jnp.int32, values.shape, 1)
    edge = 0 if by == 1 else size - 1
    return jnp.where(column == edge, jnp.zeros_like(values), pltpu.roll(values, by % size, 1))


VMEM = pl.BlockSpec(memory_space=pltpu.VMEM)
ANY = pl.BlockSpec(memory_space=pl.ANY)


def behind(axis, size, by):
    return lax.rem(lax.axis_index(axis) + (size - by), size)


def hold_kernel(n_blocks, n_after, cotangent, *refs):
    blocks, (half, *copies, sems) = refs[:n_blocks], refs[n_blocks + n_after :]
    rows = half.shape[0]
    moves = [(cotangent.at[pl.ds(lax.axis_index("in") * rows, rows)], half)]
    moves += zip(blocks, copies)
    moves = [pltpu.make_async_copy(*move, sems.at[i]) for i, move in enumerate(moves)]
    for move in moves:
        move.start()
    for move in moves:
        move.wait()


def hold(cotangent, blocks, after):
    shape = (cotangent.shape[0] // 2,) + cotangent.shape[1:]
    held = [jax.ShapeDtypeStruct(block.shape, block.dtype) for block in blocks]
    return pl.pallas_call(
        functools.partial(hold_kernel, len(blocks), len(after)),
        out_shape=[jax.ShapeDtypeStruct(shape, cotangent.dtype), *held],
        in_specs=[ANY] * (1 + len(blocks) + len(after)),
        out_specs=[VMEM] * (1 + len(blocks)),
        scratch_shapes=[pltpu.SemaphoreType.DMA((1 + len(blocks),))],
        compiler_params=params((shape, 2), *((block.shape, 2) for block in blocks)),
        cost_estimate=pl.CostEstimate(
            flops=0, bytes_accessed=4 * math.prod(shape), transcendentals=0
        ),
    )(cotangent, *blocks, *after)


def arrange_kernel(weight, bias, *refs):
    taps, bias_col, sems = refs[-3:]
    depth = taps.shape[1] // 3
    own = weight.shape[2]
    half = lax.axis_index("in")
    copies = [
        pltpu.make_async_copy(
            weight.at[a, b, :, pl.ds(pl.multiple_of(half * depth, depth), depth)],
            taps.at[pl.ds(a * own, own), pl.ds(b * depth, depth)],
            sems.at[a * 3 + b],
        )
        for a in range(3)
        for b in range(3)
    ]
    for copy in copies:
        copy.start()
    bias_col[...] = jnp.broadcast_to(bias[...], (128, own)).T[:, :1]
    for copy in copies:
        copy.wait()


def arrange(weight, bias, depth, after):
    own = weight.shape[2]
    shape = (3 * own, 3 * depth)
    return pl.pallas_call(
        arrange_kernel,
        out_shape=(
            jax.ShapeDtypeStruct(shape, weight.dtype),
            jax.ShapeDtypeStruct((own, 1), bias.dtype),
        ),
        in_specs=[ANY, VMEM] + [ANY] * len(after),
        out_specs=(VMEM, VMEM),
        scratch_shapes=[pltpu.SemaphoreType.DMA((9,))],
        compiler_params=params((shape, 2)),
        cost_estimate=pl.CostEstimate(
            flops=0, bytes_accessed=36 * own * depth, transcendentals=0
        ),
    )(weight, bias.reshape(1, own), *after)


def block_place(index, n_filt, n_sp):
    j, k = divmod(index, n_filt)
    return behind("sp", n_sp, j) * n_filt + folded_behind("filt", n_filt, k)


def turn_row(turned, row):
    values = row.T
    depth = values.shape[0]
    turned[pl.ds(0, depth), :] = move_columns(values, 1)
    turned[pl.ds(depth, depth), :] = values
    turned[pl.ds(2 * depth, depth), :] = move_columns(values, -1)


def add_row(total, slot, taps, row, turned):
    own = taps.shape[0] // 3
    turn_row(turned, row)
    product = jnp.dot(taps[...], turned[...], preferred_element_type=jnp.float32)
    for a in range(3):
        total[slot + 1 - a] += product[a * own : (a + 1) * own]


def add_blocks_kernel(where, n_filt, n_sp, fresh, taps, *refs):
    *blocks, total, turned = refs if fresh else refs[1:]
    rows_dev = blocks[0].shape[0]
    total[...] = jnp.zeros(total.shape, total.dtype) if fresh else refs[0][...]
    for index, (block, (j, k)) in enumerate(zip(blocks, where)):
        place = block_place(j * n_filt + k, n_filt, n_sp)
        for i in range(rows_dev):
            at = index * rows_dev + i
            add_row(total, place * rows_dev + i + 1, taps, block[i], turned.at[at])


def add_blocks(taps, sides, where, side_rows, begun=()):
    n_sp, n_filt = len(sides), len(sides[0])
    blocks = [sides[j][k] for j, k in where]
    rows_dev, width, depth = blocks[0].shape
    own = taps.shape[0] // 3
    shape = (n_sp * side_rows + 2, own, width)
    turned = (len(blocks) * rows_dev, 3 * depth, width)
    return pl.pallas_call(
        functools.partial(add_blocks_kernel, where, n_filt, n_sp, not begun),
        out_shape=jax.ShapeDtypeStruct(shape, jnp.float32),
        in_specs=[VMEM] * (1 + len(begun) + len(blocks)),
        out_specs=VMEM,
        scratch_shapes=[pltpu.VMEM(turned, blocks[0].dtype)],
        compiler_params=params((turned, 2), (shape, 8), (taps.shape, 4)),
        cost_estimate=pl.CostEstimate(
            flops=(1 if begun else 30) * len(blocks) * rows_dev * own * width * depth,
            bytes_accessed=1,
            transcendentals=0,
        ),
    )(taps, *begun, *blocks)


def last_rows_kernel(n_filt, n_sp, j, n_after, taps, begun, *refs):
    *blocks, out, total, turned = refs[n_after:]
    rows_dev = blocks[0].shape[0]
    side_rows, own = total.shape[0] - 2, total.shape[1]
    side = behind("sp", n_sp, j)
    total[...] = begun[pl.ds(side * side_rows, side_rows + 2)]

    def slot_of(other):
        place = block_place(other * n_filt + n_filt - 1, n_filt, n_sp)
        return place * rows_dev - side * side_rows + 1

    for other, block in enumerate(blocks, 1):
        for i in range(rows_dev):
            if other == j:
                add_row(total, slot_of(other) + i, taps, block[i], turned.at[i])
        if other != j:
            for i, at, edge, a in ((rows_dev - 1, 0, 1, 0), (0, side_rows + 1, side_rows, 2)):

                @pl.when(slot_of(other) + i == at)
                def _():
                    turn_row(turned.at[0], block[i])
                    rows = taps[pl.ds(a * own, own), :]
                    product = jnp.dot(rows, turned[0], preferred_element_type=jnp.float32)
                    total[edge] += product

    out[...] = total[pl.ds(1, side_rows)]


def last_rows(taps, begun, sides, j, side_rows, after=()):
    n_sp, n_filt = len(sides), len(sides[0])
    blocks = [side[-1] for side in sides[1:]]
    rows_dev, width, depth = blocks[0].shape
    own = taps.shape[0] // 3
    out = (side_rows, own, width)
    total = (side_rows + 2, own, width)
    turned = (rows_dev, 3 * depth, width)
    return pl.pallas_call(
        functools.partial(last_rows_kernel, n_filt, n_sp, j, len(after)),
        out_shape=jax.ShapeDtypeStruct(out, jnp.float32),
        in_specs=[VMEM] * 2 + [ANY] * len(after) + [VMEM] * len(blocks),
        out_specs=VMEM,
        scratch_shapes=[
            pltpu.VMEM(total, jnp.float32),
            pltpu.VMEM(turned, blocks[0].dtype),
        ],
        compiler_params=params(
            (turned, 2 + n_sp), (total, 12), (begun.shape, 4), (taps.shape, 4)
        ),
        cost_estimate=pl.CostEstimate(
            flops=18 * rows_dev * own * width * depth,
            bytes_accessed=18 * own * depth,
            transcendentals=0,
        ),
    )(taps, begun, *after, *blocks)


def silu_parts(shifted, cotangent):
    sigmoid_v = 0.5 * jnp.tanh(0.5 * shifted) + 0.5
    slope = sigmoid_v * (1.0 + shifted * (1.0 - sigmoid_v))
    grad_out = (cotangent.astype(jnp.float32) * slope).astype(jnp.bfloat16)
    return sigmoid_v, grad_out


def silu_kernel(n_filt, mine, theirs, bias, cotangent, grad_out, *activated):
    rows, _, half = activated[0].shape

    for k in range(n_filt):
        first = behind("filt", n_filt, n_filt - k if k else 0) * rows

        @pl.loop(0, rows)
        def _(i):
            r = first + i
            shifted = (mine[r] + theirs[r]) + bias[...]
            sigmoid_v, grad_out[r] = silu_parts(shifted, cotangent[r])
            value = (shifted * sigmoid_v).astype(activated[k].dtype)
            activated[k][i] = jnp.where(
                lax.axis_index("in") == 0, value[:, :half], value[:, half:]
            )


def silu(mine, theirs, bias, cotangent, n_filt):
    rows, own, width = cotangent.shape
    return pl.pallas_call(
        functools.partial(silu_kernel, n_filt),
        out_shape=[jax.ShapeDtypeStruct((rows, own, width), jnp.bfloat16)]
        + [jax.ShapeDtypeStruct((rows // n_filt, own, width // 2), jnp.bfloat16)] * n_filt,
        in_specs=[VMEM] * 4,
        out_specs=[VMEM] * (1 + n_filt),
        compiler_params=params((cotangent.shape, 16)),
        cost_estimate=pl.CostEstimate(
            flops=10 * rows * own * width,
            bytes_accessed=13 * rows * own * width,
            transcendentals=rows * own * width,
        ),
    )(mine, theirs, bias, cotangent)


def shift_grads(grads, grad_out, row):
    own, width = grad_out.shape
    at = pl.ds(pl.multiple_of(row * width, width), width)
    grads[pl.ds(0, own), at] = move_columns(grad_out, -1)
    grads[pl.ds(own, own), at] = grad_out
    grads[pl.ds(2 * own, own), at] = move_columns(grad_out, 1)


def panel_copies(panel, blocks, n_filt, n_sp, sems):
    rows_dev, width, _ = blocks[0].shape
    copies = []
    for index, block in enumerate(blocks):
        place = block_place(index, n_filt, n_sp)
        for i in range(rows_dev):
            at = pl.multiple_of((place * rows_dev + i + 1) * width, width)
            to = panel.at[pl.ds(at, width), :]
            copies.append(pltpu.make_async_copy(block.at[i], to, sems.at[index * rows_dev + i]))
    return copies


def gradient_kernel(n_filt, n_sp, bias, own_grad, *refs):
    others, refs = refs[: 4 * (n_sp - 1)], refs[4 * (n_sp - 1) :]
    *blocks, weight_sum, bias_sum, formed = refs[: n_sp * n_filt + 3]
    grads, (panel, stage, sems, row_sems) = refs[-4 - n_sp : -4], refs[-4:]
    side_rows, own, width = own_grad.shape
    half_rows = side_rows // 2
    half = lax.axis_index("in")
    copies = panel_copies(panel, blocks, n_filt, n_sp, row_sems)
    for copy in copies:
        copy.start()
    zeros = jnp.zeros((width, panel.shape[1]), panel.dtype)
    panel[pl.ds(0, width), :] = zeros
    panel[pl.ds((n_sp * side_rows + 1) * width, width), :] = zeros
    for r in range(side_rows):
        shift_grads(grads[0], own_grad[r], r)
    for copy in copies:
        copy.wait()

    def tap_gradient(j, a, rows=slice(None)):
        first = (behind("sp", n_sp, j) * side_rows + a) * width
        window = panel[pl.ds(pl.multiple_of(first, width), side_rows * width), :]
        return jnp.dot(grads[j][rows, :], window, preferred_element_type=jnp.float32)

    def copy_out(a, b):
        return pltpu.make_async_copy(stage.at[a, b], weight_sum.at[a, b], sems.at[a, b])

    for a in range(3):
        stage[a] = tap_gradient(0, a).reshape(stage.shape[1:])
    for j in range(1, n_sp):
        mine, theirs, near, far = others[4 * (j - 1) : 4 * j]
        for h, cotangent in enumerate((near, far)):
            start = (half if h == 0 else 1 - half) * half_rows
            for r in range(half_rows):
                shifted = (mine[start + r] + theirs[start + r]) + bias[...]
                _, grad_out = silu_parts(shifted, cotangent[r])
                shift_grads(grads[j], grad_out, start + r)

    for a in range(2):
        for j in range(1, n_sp):
            product = tap_gradient(j, a)
            for b in range(3):
                stage[a, b] += product[b * own : (b + 1) * own]
                if j == n_sp - 1:
                    copy_out(a, b).start()
    for b in range(3):
        for j in range(1, n_sp):
            stage[2, b] += tap_gradient(j, 2, slice(b * own, (b + 1) * own))
        copy_out(2, b).start()

    total = jnp.zeros((16, own), jnp.float32)
    for side in grads:
        total += lax.dot_general(
            jnp.ones((16, side.shape[1]), side.dtype),
            side[pl.ds(own, own), :],
            (((1,), (1,)), ((), ())),
            preferred_element_type=jnp.float32,
        )
    bias_sum[...] = total[:1]
    formed[...] = jnp.zeros(formed.shape, formed.dtype)
    for a in range(3):
        for b in range(3):
            copy_out(a, b).wait()


def gradient(bias, own_grad, others, sides):
    n_sp, n_filt = len(sides), len(sides[0])
    blocks = [block for side in sides for block in side]
    side_rows, own, width = own_grad.shape
    depth = blocks[0].shape[2]
    all_rows = n_sp * side_rows
    panel = ((all_rows + 2) * width, depth)
    grads = (3 * own, side_rows * width)
    total = (3, 3, own, depth)
    return pl.pallas_call(
        functools.partial(gradient_kernel, n_filt, n_sp),
        out_shape=[
            jax.ShapeDtypeStruct(total, jnp.float32),
            jax.ShapeDtypeStruct((1, own), jnp.float32),
            jax.ShapeDtypeStruct((8, 128), jnp.float32),
        ],
        in_specs=[VMEM] * (2 + len(others)) + [ANY] * len(blocks),
        out_specs=[ANY, VMEM, VMEM],
        scratch_shapes=[
            *[pltpu.VMEM(grads, jnp.bfloat16)] * n_sp,
            pltpu.VMEM(panel, blocks[0].dtype),
            pltpu.VMEM(total, jnp.float32),
            pltpu.SemaphoreType.DMA((3, 3)),
            pltpu.SemaphoreType.DMA((all_rows,)),
        ],
        compiler_params=params(
            (grads, 2 * n_sp), (panel, 2), (total, 6), ((all_rows, own, width), 12)
        ),
        cost_estimate=pl.CostEstimate(
            flops=18 * all_rows * own * width * depth,
            bytes_accessed=36 * own * depth + 2 * all_rows * width * depth,
            transcendentals=all_rows * own * width,
        ),
    )(bias, own_grad, *others, *blocks)


def place_kernel(*refs):
    *pieces, _, output, sems = refs
    own = pieces[0].shape[1]
    copies = []
    for k, piece in enumerate(pieces):
        at = pl.multiple_of(behind("filt", len(pieces), k) * own, own)
        rows = output.at[:, pl.ds(at, own), :]
        copies.append(pltpu.make_async_copy(piece, rows, sems.at[k]))
    for copy in copies:
        copy.start()
    for copy in copies:
        copy.wait()


def place_pieces(pieces, after):
    rows, own, half = pieces[0].shape
    return pl.pallas_call(
        place_kernel,
        out_shape=jax.ShapeDtypeStruct((rows, len(pieces) * own, half), pieces[0].dtype),
        in_specs=[VMEM] * (len(pieces) + 1),
        out_specs=ANY,
        scratch_shapes=[pltpu.SemaphoreType.DMA((len(pieces),))],
        compiler_params=params((pieces[0].shape, 2 * len(pieces))),
        cost_estimate=pl.CostEstimate(
            flops=0, bytes_accessed=4 * len(pieces) * rows * own * half, transcendentals=0
        ),
    )(*pieces, after)


def on_device(image, weight, bias, cotangent):
    n_filt, n_sp = lax.axis_size("filt"), lax.axis_size("sp")
    side_rows = cotangent.shape[0]
    swap = shifted_ring("in", 1)

    gathered = gather_blocks(image)
    taps, bias_col = arrange(weight, bias, image.shape[2], [gathered[-1][0]])
    places = [[(j, k) for j in range(n_sp)] for k in range(n_filt)]
    first, second = places[: n_filt // 2], places[n_filt // 2 :]
    second[-1] = [(0, n_filt - 1)]
    begun = add_blocks(taps, gathered, first[0], side_rows)
    near = send_held(gathered, cotangent, [begun, gathered[0][-2]])
    for group in (sum(first[1:], []), sum(second[:-1], []), second[-1]):
        begun = add_blocks(taps, gathered, group, side_rows, [begun])

    partial = [last_rows(taps, begun, gathered, 0, side_rows)]
    for j in range(1, n_sp):
        partial.append(last_rows(taps, begun, gathered, j, side_rows, [near[j]]))
    other = [lax.ppermute(value, "in", swap) for value in partial]

    own_grad, *rows = silu(partial[0], other[0], bias_col, cotangent, n_filt)
    pieces = rows[:1]
    for k in range(1, n_filt):
        pieces.append(lax.ppermute(rows[k], "filt", shifted_ring("filt", k)))
    others = []
    for j in range(1, n_sp):
        others += [partial[j], other[j], near[j], lax.ppermute(near[j], "in", swap)]
    grad_weight, grad_bias, formed = gradient(bias_col, own_grad, others, gathered)
    output = place_pieces(pieces, formed)
    return (output, grad_weight, grad_bias.reshape(-1))


def solution(mesh):
    placed = (
        P(("groups", "sp", "filt"), None, "in"),
        P(None, None, "filt", None),
        P("filt"),
        P(("groups", "sp"), "filt", None),
    )
    return jax.shard_map(
        on_device,
        mesh=mesh,
        in_specs=placed,
        out_specs=(
            P(("groups", "sp", "filt"), None, "in"),
            P("groups", None, "filt", "in"),
            P(("groups", "filt")),
        ),
        check_vma=False,
    )
```
